128 devices in a mesh: row: 16 (over x_lo, y, core), col: 8 (over x_hi, z).
Axes of the slice: x: 4 (x_hi: 2, x_lo: 2; x = x_hi * 2 + x_lo), y: 4, z: 4, core: 2. Of those that a mesh axis runs over, the one named last changes fastest.
Arguments:
- atom_state: bfloat16 [49152, 128], P(('row', 'col')), may hold values from -6 to 6
- token_input: bfloat16 [6144, 768], P(('row', 'col')), may hold values from -6 to 6
- atom_owner: int32 [128, 384], P(('row', 'col')), may hold values from 0 to 47, never falling along the last dimension, each value on 1 to 24 neighbouring positions
- atom_bias: bfloat16 [4, 49152, 128], P(None, ('row', 'col')), may hold values from -6 to 350
- pair_bias: bfloat16 [16, 6144, 6144], P(None, 'row', 'col'), may hold values from -6 to 350
- atom_proj: bfloat16 [4, 128, 128], replicated, may hold values from -0.5 to 0.5
- atom_output: bfloat16 [128, 128], replicated, may hold values from -0.5 to 0.5
- pool_weight: bfloat16 [128, 768], replicated, may hold values from -0.5 to 0.5
- token_proj: bfloat16 [4, 768, 768], replicated, may hold values from -0.21875 to 0.21875
- token_output: bfloat16 [768, 768], replicated, may hold values from -0.21875 to 0.21875
- back_weight: bfloat16 [768, 128], replicated, may hold values from -0.21875 to 0.21875
Outputs:
- atom_result: bfloat16 [49152, 128], P(('row', 'col'))
- token_state: bfloat16 [6144, 768], P(('row', 'col'))
The draws below stay inside these ranges and needn't reach their ends.
Inputs may be any that keep to these rules, and one draw needn't show every extreme that they name: `atom_owner`: in each row the token number never falls; every number 0 to 47 owns 1 to 24 consecutive slots, and some token owns exactly 24.
All inputs are finite; a program needn't handle non-finite values.
Results may differ from the reference program's by a relative error of at most 0.008.
Values may be sent and summed in bfloat16 or wider, within the bound.
No kernel may reach another device: no remote copies, remote signals or barrier semaphores. Data moves between devices by JAX's collectives and lax.ppermute only.
A program may use at most 192 MiB of HBM per device.

```python
import math
import jax
import jax.numpy as jnp
import numpy as np
from jax import lax

D = 768
HEADS = 16
HEAD_DIM = 48
ATOM_WIDTH = 128
ATOM_HEADS = 4
ATOM_HEAD_DIM = 32
WIN_Q = 32
WIN_K = 128
REACH = 48
MOST_ATOMS = 24
TOK_DEV = 48
ATOM_DEV = 384
BLOCKS = 128
TOKENS = 6144
ATOMS = 49152


def draw_atom_bias(key, part):
    key = jax.random.fold_in(key, 5)
    shape = (ATOM_HEADS, ATOMS, WIN_K)
    return jnp.clip(jax.random.normal(key, shape, jnp.float32), -6.0, 6.0).astype(jnp.bfloat16)


def draw_pair_bias(key, part):
    key = jax.random.fold_in(key, 11)
    shape = (HEADS, TOKENS, TOKENS)
    return jnp.clip(jax.random.normal(key, shape, jnp.float32), -6.0, 6.0).astype(jnp.bfloat16)


def steps_of(own_key, shape, split, least, largest):
    factor_of, own = 1.0, jax.random.fold_in(own_key, 6)
    for dim, parts in split:
        heights = jnp.exp(jax.random.uniform(jax.random.fold_in(own, dim), (parts,), jnp.float32, least / len(split), largest / len(split)))
        factor_of = factor_of * jnp.repeat(heights, shape[dim] // parts).reshape([-1 if axis == dim else 1 for axis in range(len(shape))])
    return factor_of


def length_profile(amount, total, bound, lean):
    weights = [(1 << 20) // math.isqrt(rank ** lean) + 1 for rank in range(2, amount + 1)]
    rest, given = total - bound - (amount - 1), [1] * (amount - 1)
    while rest > 0:
        movable = [i for i in range(amount - 1) if given[i] < bound]
        pool, remaining = sum([weights[i] for i in movable]), rest
        for i in movable:
            extra = min(bound - given[i], max(1, remaining * weights[i] // pool), rest)
            given[i] = given[i] + extra
            rest = rest - extra
    return np.array([bound] + given)


def uneven_parts(key, number_of, total, limit, skew):
    if number_of == 2:
        one = jax.random.randint(key, (), max(1, total - limit), min(limit, total - 1) + 1)
        return jnp.stack([one, total - one])
    tallies = jnp.asarray(length_profile(number_of, total, limit, skew), jnp.int32)
    pairs = (number_of - 1) // 2
    donor, sink = tallies[1:1 + 2 * pairs:2], tallies[2:2 + 2 * pairs:2]
    margin = jnp.minimum(donor - 1, limit - sink)
    moved = jax.random.randint(jax.random.fold_in(key, 1), (pairs,), 0, 1 << 20) % (margin + 1)
    tallies = tallies.at[1:1 + 2 * pairs:2].set(donor - moved).at[2:2 + 2 * pairs:2].set(sink + moved)
    return tallies[jax.random.permutation(jax.random.fold_in(key, 2), number_of)]


def normal_values(key, shape, scale, limit, cuts=(), kind=jnp.bfloat16):
    factor_of = steps_of(key, shape, cuts, -0.22, 0.18) if cuts else 1.0
    entries = jax.random.normal(key, shape, jnp.float32) * scale * factor_of
    return jnp.minimum(jnp.maximum(entries, -limit), limit).astype(kind)


def setup_inputs(seed: int = 0) -> dict:
    splits = jax.random.split(jax.random.key(seed), 12)
    atom_state = normal_values(splits[0], (ATOMS, ATOM_WIDTH), 1.0, 6.0, ((0, 128),))
    token_input = normal_values(splits[1], (TOKENS, D), 1.0, 6.0, ((0, 128),))
    atom_owner = jax.vmap(lambda own: jnp.searchsorted(jnp.cumsum(uneven_parts(own, TOK_DEV, ATOM_DEV, MOST_ATOMS, 2)), jnp.arange(ATOM_DEV), side="right"))(jax.random.split(splits[2], BLOCKS)).reshape((BLOCKS, ATOM_DEV)).astype(jnp.int32)
    atom_bias = draw_atom_bias(jax.random.fold_in(splits[11], 71), 0)
    pair_bias = draw_pair_bias(jax.random.fold_in(splits[11], 71), 0)
    atom_proj = normal_values(splits[5], (4, ATOM_WIDTH, ATOM_WIDTH), ATOM_WIDTH ** -0.5, 0.5)
    atom_output = normal_values(splits[6], (ATOM_WIDTH, ATOM_WIDTH), ATOM_WIDTH ** -0.5, 0.5)
    pool_weight = normal_values(splits[7], (ATOM_WIDTH, D), ATOM_WIDTH ** -0.5, 0.5)
    token_proj = normal_values(splits[8], (4, D, D), D ** -0.5, 0.21875)
    token_output = normal_values(splits[9], (D, D), D ** -0.5, 0.21875)
    back_weight = normal_values(splits[10], (D, ATOM_WIDTH), D ** -0.5, 0.21875)
    return {"atom_state": atom_state, "token_input": token_input, "atom_owner": atom_owner, "atom_bias": atom_bias, "pair_bias": pair_bias, "atom_proj": atom_proj, "atom_output": atom_output, "pool_weight": pool_weight, "token_proj": token_proj, "token_output": token_output, "back_weight": back_weight}


EPSILON = 1e-05

def layer_norm(values):
    centred = values - lax.optimization_barrier(jnp.mean(values, axis=-1, keepdims=True))
    spread = lax.optimization_barrier(jnp.mean(centred * centred, axis=-1, keepdims=True))
    return centred * lax.rsqrt(spread + EPSILON)

def reference(atom_state, token_input, atom_owner, atom_bias, pair_bias, atom_proj, atom_output, pool_weight, token_proj, token_output, back_weight):
    atom_norm = layer_norm(atom_state.astype(jnp.float32)).astype(jnp.bfloat16)
    atom_query = jnp.dot(atom_norm, atom_proj[0], preferred_element_type=jnp.float32).astype(jnp.bfloat16)
    pair_weight = jnp.concatenate([atom_proj[1], atom_proj[2]], axis=1)
    atom_pairs = jnp.dot(atom_norm, pair_weight, preferred_element_type=jnp.float32).astype(jnp.bfloat16)
    atom_gate = jax.nn.sigmoid(jnp.dot(atom_norm, atom_proj[3], preferred_element_type=jnp.float32))
    windows = ATOMS // WIN_Q
    window_span = WIN_K // WIN_Q
    padded = jnp.pad(atom_pairs, ((REACH, REACH), (0, 0)))
    blocks = padded.reshape(windows + window_span - 1, WIN_Q, 2 * ATOM_WIDTH)
    window_pairs = jnp.concatenate([blocks[offset_block:offset_block + windows] for offset_block in range(window_span)], axis=1)
    window_keys = window_pairs[:, :, :ATOM_WIDTH].reshape(windows, WIN_K, ATOM_HEADS, ATOM_HEAD_DIM).astype(jnp.float32)
    window_values = window_pairs[:, :, ATOM_WIDTH:].reshape(windows, WIN_K, ATOM_HEADS, ATOM_HEAD_DIM).astype(jnp.float32)
    query_blocks = atom_query.reshape(windows, WIN_Q, ATOM_HEADS, ATOM_HEAD_DIM).astype(jnp.float32)
    scores = jnp.einsum('wqhd,wkhd->whqk', query_blocks, window_keys) / math.sqrt(ATOM_HEAD_DIM)
    scores = scores + atom_bias.reshape(ATOM_HEADS, windows, WIN_Q, WIN_K).transpose(1, 0, 2, 3).astype(jnp.float32)
    position = WIN_Q * jnp.arange(windows, dtype=jnp.int32)[:, None] - REACH + jnp.arange(WIN_K, dtype=jnp.int32)[None, :]
    usable = (position >= 0) & (position < ATOMS)
    scores = jnp.where(usable[:, None, None, :], scores, -1e+30)
    weights = jax.nn.softmax(scores, axis=-1).astype(jnp.bfloat16)
    blended = jnp.einsum('whqk,wkhd->wqhd', weights.astype(jnp.float32), window_values).reshape(ATOMS, ATOM_WIDTH)
    gated_atoms = (blended * atom_gate).astype(jnp.bfloat16)
    atom_mid = atom_state.astype(jnp.float32) + jnp.dot(gated_atoms, atom_output, preferred_element_type=jnp.float32)
    lifted = jax.nn.relu(jnp.dot(atom_mid.astype(jnp.bfloat16), pool_weight, preferred_element_type=jnp.float32)).astype(jnp.bfloat16)
    onehot = (atom_owner[:, None, :] == jnp.arange(TOK_DEV, dtype=jnp.int32)[None, :, None]).astype(jnp.float32)
    pooled_sums = jnp.einsum('bta,bac->btc', onehot, lifted.reshape(BLOCKS, ATOM_DEV, D).astype(jnp.float32))
    counts = lax.optimization_barrier(jnp.sum(onehot, axis=-1))
    single = token_input.astype(jnp.float32) + (pooled_sums / counts[..., None]).reshape(TOKENS, D)
    token_norm = layer_norm(single).astype(jnp.bfloat16)
    token_query = jnp.dot(token_norm, token_proj[0], preferred_element_type=jnp.float32).astype(jnp.bfloat16)
    token_key = jnp.dot(token_norm, token_proj[1], preferred_element_type=jnp.float32).astype(jnp.bfloat16)
    token_value = jnp.dot(token_norm, token_proj[2], preferred_element_type=jnp.float32).astype(jnp.bfloat16)
    token_gate = jax.nn.sigmoid(jnp.dot(token_norm, token_proj[3], preferred_element_type=jnp.float32))

    def one_head(head):
        start_col = head * HEAD_DIM
        query_head = lax.dynamic_slice_in_dim(token_query, start_col, HEAD_DIM, 1)
        key_head = lax.dynamic_slice_in_dim(token_key, start_col, HEAD_DIM, 1)
        value_head = lax.dynamic_slice_in_dim(token_value, start_col, HEAD_DIM, 1)
        head_scores = jnp.dot(query_head, key_head.T, preferred_element_type=jnp.float32) / math.sqrt(HEAD_DIM)
        head_scores = head_scores + pair_bias[head].astype(jnp.float32)
        head_weights = jax.nn.softmax(head_scores, axis=-1).astype(jnp.bfloat16)
        return jnp.dot(head_weights, value_head, preferred_element_type=jnp.float32)
    head_outputs = lax.map(one_head, jnp.arange(HEADS, dtype=jnp.int32))
    token_mix = head_outputs.transpose(1, 0, 2).reshape(TOKENS, D)
    token_gated = (token_mix * token_gate).astype(jnp.bfloat16)
    token_state = (single + jnp.dot(token_gated, token_output, preferred_element_type=jnp.float32)).astype(jnp.bfloat16)
    returned = jnp.dot(token_state, back_weight, preferred_element_type=jnp.float32)
    owners = (atom_owner + TOK_DEV * jnp.arange(BLOCKS, dtype=jnp.int32)[:, None]).reshape(ATOMS)
    atom_result = (atom_mid + jnp.take(returned, owners, axis=0)).astype(jnp.bfloat16)
    return (atom_result, token_state)
```

```python
import math

import jax
import jax.numpy as jnp
from jax import lax
from jax.experimental import pallas as pl
from jax.experimental.pallas import tpu as pltpu
from jax.sharding import PartitionSpec as P

HEADS = 16
HEAD_DIM = 48
SLOT = 64
PAIRS = HEADS // 2
ATOM_HEADS = 4
WIN_Q = 32
WIN_K = 128
REACH = 48
EPSILON = 1e-05

BOTH = ("row", "col")
F32 = jnp.float32
BF16 = jnp.bfloat16
VMEM_LIMIT = 56 * 1024 * 1024


def dot(a, b, contract=((1,), (0,))):
    return lax.dot_general(a, b, (contract, ((), ())), preferred_element_type=F32)


def layer_norm(values):
    centred = values - jnp.mean(values, axis=-1, keepdims=True)
    spread = jnp.mean(centred * centred, axis=-1, keepdims=True)
    return centred * lax.rsqrt(spread + EPSILON)


def lanes(shape, axis):
    return lax.broadcasted_iota(jnp.int32, shape, axis)


def spread_weights(proj_ref, out_ref, proj_wide, out_wide):
    width = HEADS * HEAD_DIM
    wide = HEADS * SLOT
    source = lanes((width, wide), 0)
    target = lanes((width, wide), 1)
    place = (
        (source // HEAD_DIM == target // SLOT) & (source % HEAD_DIM == target % SLOT)
    ).astype(BF16)
    for i in range(4):
        proj_wide[i] = dot(proj_ref[i], place).astype(BF16)
    out_wide[...] = dot(place, out_ref[...], ((0,), (0,))).astype(BF16)


def atom_step(
    left_ref, state_ref, right_ref, input_ref, owner_ref, bias_ref, proj_ref, output_ref,
    pool_ref, mid_ref, single_ref, norm_ref,
):
    count = state_ref.shape[0]
    windows = count // WIN_Q
    rows, cols = lax.axis_size("row"), lax.axis_size("col")
    first = (lax.axis_index("row") * cols + lax.axis_index("col")) * count
    total = count * rows * cols
    state = state_ref[...].astype(F32)
    extended = jnp.concatenate(
        [left_ref[...].astype(F32), state, right_ref[...].astype(F32)], axis=0
    )
    normed = layer_norm(extended).astype(BF16)
    keys = dot(normed, proj_ref[1]).astype(BF16)
    values = dot(normed, proj_ref[2]).astype(BF16)
    own = normed[REACH : REACH + count]
    queries = dot(own, proj_ref[0]).astype(BF16)
    gates = jax.nn.sigmoid(dot(own, proj_ref[3]))
    width = state_ref.shape[1]
    head_width = width // ATOM_HEADS
    head_of = lanes((WIN_Q, width), 1) // head_width
    factor = 1.0 / math.sqrt(head_width)
    gated = []
    for w in range(windows):
        start = w * WIN_Q
        query = queries[start : start + WIN_Q]
        stacked = jnp.concatenate(
            [jnp.where(head_of == h, query, jnp.zeros_like(query)) for h in range(ATOM_HEADS)],
            axis=0,
        )
        scores = dot(stacked, keys[start : start + WIN_K], ((1,), (1,))) * factor
        scores = scores + jnp.concatenate(
            [bias_ref[h, start : start + WIN_Q, :] for h in range(ATOM_HEADS)], axis=0
        ).astype(F32)
        if start < REACH or start + WIN_K > count + REACH:
            position = first + (start - REACH) + lanes(scores.shape, 1)
            scores = jnp.where((position >= 0) & (position < total), scores, -1e30)
        top = jnp.max(scores, axis=-1, keepdims=True)
        weights = jnp.exp(scores - top)
        weights = (weights / jnp.sum(weights, axis=-1, keepdims=True)).astype(BF16)
        mixed = dot(weights, values[start : start + WIN_K])
        mix = jnp.zeros((WIN_Q, width), F32)
        for h in range(ATOM_HEADS):
            mix = jnp.where(head_of == h, mixed[h * WIN_Q : (h + 1) * WIN_Q], mix)
        gated.append((mix * gates[start : start + WIN_Q]).astype(BF16))
    gated = jnp.concatenate(gated, axis=0)
    mid = state + dot(gated, output_ref[...])
    mid_ref[...] = mid
    lifted = jnp.maximum(dot(mid.astype(BF16), pool_ref[...]), 0.0).astype(BF16)
    tokens = input_ref.shape[0]
    owned = (lanes((tokens, count), 0) == owner_ref[...]).astype(F32)
    counts = jnp.sum(owned, axis=1, keepdims=True)
    pooled = dot(owned.astype(BF16), lifted)
    single = input_ref[...].astype(F32) + pooled / counts
    single_ref[...] = single
    norm_ref[...] = layer_norm(single).astype(BF16)


def token_step(query_ref, key_ref, bias_ref, proj_ref, part_ref, q_ref, k_ref, v_ref):
    pair = pl.program_id(0)
    lane = 2 * SLOT

    @pl.when(pair == 0)
    def _():
        wide = HEADS * SLOT
        q = dot(query_ref[...], proj_ref[0]).astype(BF16)
        k = dot(key_ref[...], proj_ref[1]).astype(BF16)
        v = dot(key_ref[...], proj_ref[2])
        v = jnp.where(lanes((1, wide), 1) % SLOT == HEAD_DIM, 1.0, v).astype(BF16)
        for p in range(PAIRS):
            q_ref[p] = q[:, p * lane : (p + 1) * lane]
            k_ref[p] = k[:, p * lane : (p + 1) * lane]
            v_ref[p] = v[:, p * lane : (p + 1) * lane]

    query = q_ref[pair]
    key = k_ref[pair]
    value = v_ref[pair]
    count = query.shape[0]
    at = lanes((count, lane), 1)
    factor = 1.0 / math.sqrt(HEAD_DIM)
    result = jnp.zeros((count, lane), F32)
    for a in range(2):
        mine = jnp.where(at // SLOT == a, query, jnp.zeros_like(query))
        scores = dot(mine, key, ((1,), (1,))) * factor + bias_ref[a].astype(F32)
        top = jnp.max(scores, axis=-1, keepdims=True)
        weights = jnp.exp(scores - top).astype(BF16)
        mixed = dot(weights, value)
        base = a * SLOT + HEAD_DIM
        mass = mixed[:, base : base + 1]
        level = top + jnp.log(mass)
        high = level.astype(BF16).astype(F32)
        middle = (level - high).astype(BF16).astype(F32)
        low = level - high - middle
        part = mixed / mass
        part = jnp.where(at == base, high, part)
        part = jnp.where(at == base + 1, middle, part)
        part = jnp.where(at == base + 2, low, part)
        result = jnp.where(at // SLOT == a, part, result)
    part_ref[...] = result.astype(BF16)


def last_step(
    part_ref, norm_ref, single_ref, mid_ref, owner_ref, proj_ref, output_ref, back_ref,
    atom_ref, token_ref,
):
    lane = 2 * SLOT
    shares, tokens, _ = part_ref.shape
    here, there = lanes((lane, lane), 0), lanes((lane, lane), 1)
    level_of = (
        (here // SLOT == there // SLOT)
        & (here % SLOT >= HEAD_DIM)
        & (here % SLOT < HEAD_DIM + 3)
    ).astype(BF16)
    gates = jax.nn.sigmoid(dot(norm_ref[...], proj_ref[0]))
    gated = []
    for p in range(PAIRS):
        span = slice(p * lane, (p + 1) * lane)
        parts = [part_ref[c, :, span] for c in range(shares)]
        levels = [dot(part, level_of) for part in parts]
        top = levels[0]
        for level in levels[1:]:
            top = jnp.maximum(top, level)
        mass = jnp.zeros((tokens, lane), F32)
        mix = jnp.zeros((tokens, lane), F32)
        for part, level in zip(parts, levels):
            weight = jnp.exp(level - top)
            mass = mass + weight
            mix = mix + weight * part.astype(F32)
        gated.append((mix / mass * gates[:, span]).astype(BF16))
    update = dot(jnp.concatenate(gated, axis=1), output_ref[...])
    token_state = (single_ref[...] + update).astype(BF16)
    token_ref[...] = token_state
    returned = dot(token_state, back_ref[...])
    high = returned.astype(BF16)
    low = (returned - high.astype(F32)).astype(BF16)
    count = mid_ref.shape[0]
    owned = (lanes((tokens, count), 0) == owner_ref[...]).astype(F32).T.astype(BF16)
    atom_ref[...] = (mid_ref[...] + dot(owned, high) + dot(owned, low)).astype(BF16)


def call(kernel, out, cost, **more):
    flops, size = cost
    return pl.pallas_call(
        kernel,
        out_shape=out,
        compiler_params=pltpu.CompilerParams(vmem_limit_bytes=VMEM_LIMIT),
        cost_estimate=pl.CostEstimate(flops=flops, bytes_accessed=size, transcendentals=0),
        **more,
    )


def shape(dims, kind):
    return jax.ShapeDtypeStruct(dims, kind)


def per_device(
    atom_state, token_input, atom_owner, atom_bias, pair_bias, atom_proj, atom_output,
    pool_weight, token_proj, token_output, back_weight,
):
    rows, cols = lax.axis_size("row"), lax.axis_size("col")
    devices = rows * cols
    count, width = atom_state.shape
    tokens, depth = token_input.shape
    wide = HEADS * SLOT
    ends = devices - 1
    left = lax.ppermute(
        atom_state[count - REACH :], BOTH, [(i, i + 1) for i in range(ends)]
    )
    right = lax.ppermute(atom_state[:REACH], BOTH, [(i + 1, i) for i in range(ends)])
    proj_wide, output_wide = call(
        spread_weights,
        (shape((4, depth, wide), BF16), shape((wide, depth), BF16)),
        (10 * depth * depth * wide, 14_000_000),
    )(token_proj, token_output)
    mid, single, norm = call(
        atom_step,
        (
            shape((count, width), F32),
            shape((tokens, depth), F32),
            shape((tokens, depth), BF16),
        ),
        (400_000_000, 2_000_000),
    )(
        left, atom_state, right, token_input, atom_owner, atom_bias, atom_proj, atom_output,
        pool_weight,
    )
    half = rows // cols
    turn = []
    for r in range(rows):
        for c in range(cols):
            turn.append((r * cols + c, ((r % half) * cols + c) * cols + r // half))
    turned = lax.ppermute(norm, BOTH, turn)
    queries = lax.all_to_all(
        jnp.broadcast_to(norm[None], (cols, tokens, depth)), "col", 0, 0
    ).reshape(cols * tokens, depth)
    keys = lax.all_to_all(
        jnp.broadcast_to(turned[None], (rows, tokens, depth)), "row", 0, 0
    ).reshape(rows * tokens, depth)
    q_count, k_count = cols * tokens, rows * tokens
    lane = 2 * SLOT
    whole = lambda *dims: pl.BlockSpec(dims, lambda p: (0,) * len(dims))
    parts = call(
        token_step,
        shape((q_count, wide), BF16),
        (8_000_000_000, 14_000_000),
        grid=(PAIRS,),
        in_specs=[
            whole(q_count, depth),
            whole(k_count, depth),
            pl.BlockSpec((2, q_count, k_count), lambda p: (p, 0, 0)),
            whole(3, depth, wide),
        ],
        out_specs=pl.BlockSpec((q_count, lane), lambda p: (0, p)),
        scratch_shapes=[
            pltpu.VMEM((PAIRS, q_count, lane), BF16),
            pltpu.VMEM((PAIRS, k_count, lane), BF16),
            pltpu.VMEM((PAIRS, k_count, lane), BF16),
        ],
    )(queries, keys, pair_bias, proj_wide)
    parts = lax.all_to_all(parts.reshape(cols, tokens, wide), "col", 0, 0)
    full = lambda *dims: pl.BlockSpec(dims, lambda i: (0,) * len(dims))
    return call(
        last_step,
        (shape((count, width), BF16), shape((tokens, depth), BF16)),
        (400_000_000, 5_000_000),
        grid=(1,),
        in_specs=[
            full(cols, tokens, wide),
            full(tokens, depth),
            full(tokens, depth),
            full(count, width),
            full(1, count),
            pl.BlockSpec((1, depth, wide), lambda i: (3, 0, 0)),
            full(wide, depth),
            full(depth, width),
        ],
        out_specs=(full(count, width), full(tokens, depth)),
    )(parts, norm, single, mid, atom_owner, proj_wide, output_wide, back_weight)


def solution(mesh):
    split = P(BOTH, None)
    placed = (
        split, split, split, P(None, BOTH, None), P(None, "row", "col"),
        P(), P(), P(), P(), P(), P(),
    )
    return jax.shard_map(
        per_device, mesh=mesh, in_specs=placed, out_specs=(split, split), check_vma=False
    )
```

```python
import math

import jax
import jax.numpy as jnp
from jax import lax
from jax.experimental import pallas as pl
from jax.experimental.pallas import tpu as pltpu
from jax.sharding import PartitionSpec as P

HEADS = 16
HEAD_DIM = 48
SLOT = 64
PAIRS = HEADS // 2
ATOM_HEADS = 4
WIN_Q = 32
WIN_K = 128
REACH = 48
EPSILON = 1e-05

BOTH = ("row", "col")
F32 = jnp.float32
BF16 = jnp.bfloat16
ORDER = (2, 3, 0, 1, 6, 7, 4, 5)


def dot(a, b, contract=((1,), (0,))):
    return lax.dot_general(a, b, (contract, ((), ())), preferred_element_type=F32)


def layer_norm(values):
    centred = values - jnp.mean(values, axis=-1, keepdims=True)
    spread = jnp.mean(centred * centred, axis=-1, keepdims=True)
    return centred * lax.rsqrt(spread + EPSILON)


def lanes(shape, axis):
    return lax.broadcasted_iota(jnp.int32, shape, axis)


BAND = 2 * 2 * SLOT
STARTS = (0, 128, 384, 512)


def band_place(group, back=False):
    near = lanes((BAND, BAND), 1 if back else 0) + STARTS[group]
    far = lanes((BAND, BAND), 0 if back else 1) + group * BAND
    return ((near // HEAD_DIM == far // SLOT) & (near % HEAD_DIM == far % SLOT)).astype(BF16)


def spread(values):
    return [
        dot(values[:, STARTS[g] : STARTS[g] + BAND], band_place(g)) for g in range(HEADS // 4)
    ]


def gather_lanes(values):
    parts = [dot(values[g], band_place(g, True)) for g in range(HEADS // 4)]
    lane = 2 * SLOT
    return jnp.concatenate(
        [
            parts[0][:, :lane],
            parts[0][:, lane:] + parts[1][:, :lane],
            parts[1][:, lane:],
            parts[2][:, :lane],
            parts[2][:, lane:] + parts[3][:, :lane],
            parts[3][:, lane:],
        ],
        axis=1,
    )


def store_pairs(ref, bands):
    lane = 2 * SLOT
    for g, band in enumerate(bands):
        ref[2 * g] = band[:, :lane].astype(BF16)
        ref[2 * g + 1] = band[:, lane:].astype(BF16)


def atom_step(
    left_ref, state_ref, right_ref, input_ref, owner_ref, bias_ref, proj_ref, output_ref,
    pool_ref, mid_ref, single_ref, norm_ref,
):
    count = state_ref.shape[0]
    windows = count // WIN_Q
    rows, cols = lax.axis_size("row"), lax.axis_size("col")
    first = (lax.axis_index("row") * cols + lax.axis_index("col")) * count
    total = count * rows * cols
    state = state_ref[...].astype(F32)
    extended = jnp.concatenate(
        [left_ref[...].astype(F32), state, right_ref[...].astype(F32)], axis=0
    )
    normed = layer_norm(extended).astype(BF16)
    keys = dot(normed, proj_ref[1]).astype(BF16)
    values = dot(normed, proj_ref[2]).astype(BF16)
    own = normed[REACH : REACH + count]
    queries = dot(own, proj_ref[0]).astype(BF16)
    gates = jax.nn.sigmoid(dot(own, proj_ref[3]))
    width = state_ref.shape[1]
    head_width = width // ATOM_HEADS
    head_of = lanes((WIN_Q, width), 1) // head_width
    factor = 1.0 / math.sqrt(head_width)
    gated = []
    for w in range(windows):
        start = w * WIN_Q
        query = queries[start : start + WIN_Q]
        stacked = jnp.concatenate(
            [jnp.where(head_of == h, query, jnp.zeros_like(query)) for h in range(ATOM_HEADS)],
            axis=0,
        )
        scores = dot(stacked, keys[start : start + WIN_K], ((1,), (1,))) * factor
        scores = scores + jnp.concatenate(
            [bias_ref[h, start : start + WIN_Q, :] for h in range(ATOM_HEADS)], axis=0
        ).astype(F32)
        if start < REACH or start + WIN_K > count + REACH:
            position = first + (start - REACH) + lanes(scores.shape, 1)
            scores = jnp.where((position >= 0) & (position < total), scores, -1e30)
        top = jnp.max(scores, axis=-1, keepdims=True)
        weights = jnp.exp(scores - top)
        weights = (weights / jnp.sum(weights, axis=-1, keepdims=True)).astype(BF16)
        mixed = dot(weights, values[start : start + WIN_K])
        mix = jnp.zeros((WIN_Q, width), F32)
        for h in range(ATOM_HEADS):
            mix = jnp.where(head_of == h, mixed[h * WIN_Q : (h + 1) * WIN_Q], mix)
        gated.append((mix * gates[start : start + WIN_Q]).astype(BF16))
    gated = jnp.concatenate(gated, axis=0)
    mid = state + dot(gated, output_ref[...])
    mid_ref[...] = mid
    lifted = jnp.maximum(dot(mid.astype(BF16), pool_ref[...]), 0.0).astype(BF16)
    tokens = input_ref.shape[0]
    owned = (lanes((tokens, count), 0) == owner_ref[...]).astype(F32)
    counts = jnp.sum(owned, axis=1, keepdims=True)
    pooled = dot(owned.astype(BF16), lifted)
    single = input_ref[...].astype(F32) + pooled / counts
    single_ref[...] = single
    norm_ref[...] = layer_norm(single).astype(BF16)


def query_step(own_ref, after_ref, before_ref, far_ref, norm_ref, proj_ref, q_ref, gate_ref):
    tokens = norm_ref.shape[0]
    lane = 2 * SLOT
    rows = jnp.concatenate(
        [own_ref[...], after_ref[...], before_ref[...], far_ref[...]], axis=0
    )
    bands = spread(dot(rows, proj_ref[0]).astype(BF16))
    ring = lax.axis_size("col") // 2
    me = lax.axis_index("col")
    high, low = me // ring, me % ring
    for i, step in enumerate((0, ring - 1, 1, 2)):
        for j in range(2):
            source = lax.rem(high + j, 2) * ring + lax.rem(low + step, ring)
            at = pl.ds(pl.multiple_of(source * tokens, 16), tokens)
            first = (2 * i + j) * tokens
            for g, band in enumerate(bands):
                block = band[first : first + tokens].astype(BF16)
                q_ref[2 * g, at, :] = block[:, :lane]
                q_ref[2 * g + 1, at, :] = block[:, lane:]
    gates = jax.nn.sigmoid(dot(norm_ref[...], proj_ref[3]))
    top = gates.astype(BF16)
    rest = (gates - top.astype(F32)).astype(BF16)
    for g, (a, b) in enumerate(zip(spread(top), spread(rest))):
        gate_ref[:, g * BAND : (g + 1) * BAND] = a + b


def project(blocks_ref, proj_ref, k_ref, v_ref):
    rows = jnp.concatenate([blocks_ref[i] for i in ORDER], axis=0)
    store_pairs(k_ref, spread(dot(rows, proj_ref[1]).astype(BF16)))
    mass = lanes((1, BAND), 1) % SLOT == HEAD_DIM
    bands = spread(dot(rows, proj_ref[2]).astype(BF16))
    store_pairs(v_ref, [jnp.where(mass, 1.0, band) for band in bands])


def token_step(
    q_ref, k_ref, v_ref, blocks_ref, proj_ref, bias_hbm, part_ref, bias_ref, other_k, other_v,
    sems,
):
    lane = 2 * SLOT
    copies = [
        pltpu.make_async_copy(bias_hbm.at[h], bias_ref.at[h], sems.at[h]) for h in range(HEADS)
    ]
    for copy in copies:
        copy.start()
    project(blocks_ref, proj_ref, other_k, other_v)
    core = lax.rem(lax.axis_index("row"), 2)
    count, half = q_ref.shape[1], k_ref.shape[1]
    mine_at = pl.ds(pl.multiple_of(core * half, lane), half)
    other_at = pl.ds(pl.multiple_of((1 - core) * half, lane), half)
    at = lanes((count, lane), 1)
    factor = 1.0 / math.sqrt(HEAD_DIM)
    for pair in range(PAIRS):
        query = q_ref[pair]
        result = jnp.zeros((count, lane), F32)
        for a in range(2):
            head = 2 * pair + a
            copies[head].wait()
            mine = jnp.where(at // SLOT == a, query, jnp.zeros_like(query))
            near = dot(mine, k_ref[pair], ((1,), (1,))) * factor
            near = near + bias_ref[head, :, mine_at].astype(F32)
            far = dot(mine, other_k[pair], ((1,), (1,))) * factor
            far = far + bias_ref[head, :, other_at].astype(F32)
            top = jnp.maximum(
                jnp.max(near, axis=-1, keepdims=True), jnp.max(far, axis=-1, keepdims=True)
            )
            mixed = dot(jnp.exp(near - top).astype(BF16), v_ref[pair])
            mixed = mixed + dot(jnp.exp(far - top).astype(BF16), other_v[pair])
            base = a * SLOT + HEAD_DIM
            mass = mixed[:, base : base + 1]
            level = top + jnp.log(mass)
            high = level.astype(BF16).astype(F32)
            middle = (level - high).astype(BF16).astype(F32)
            low = level - high - middle
            part = mixed / mass
            part = jnp.where(at == base, high, part)
            part = jnp.where(at == base + 1, middle, part)
            part = jnp.where(at == base + 2, low, part)
            result = jnp.where(at // SLOT == a, part, result)
        part_ref[:, pair * lane : (pair + 1) * lane] = result.astype(BF16)


def last_step(
    part_ref, gate_ref, single_ref, mid_ref, owner_ref, output_ref, back_ref, atom_ref,
    token_ref,
):
    lane = 2 * SLOT
    shares, tokens, _ = part_ref.shape
    here, there = lanes((lane, lane), 0), lanes((lane, lane), 1)
    level_of = (
        (here // SLOT == there // SLOT)
        & (here % SLOT >= HEAD_DIM)
        & (here % SLOT < HEAD_DIM + 3)
    ).astype(BF16)
    gated = []
    for p in range(PAIRS):
        span = slice(p * lane, (p + 1) * lane)
        parts = [part_ref[c, :, span] for c in range(shares)]
        levels = [dot(part, level_of) for part in parts]
        top = levels[0]
        for level in levels[1:]:
            top = jnp.maximum(top, level)
        mass = jnp.zeros((tokens, lane), F32)
        mix = jnp.zeros((tokens, lane), F32)
        for part, level in zip(parts, levels):
            weight = jnp.exp(level - top)
            mass = mass + weight
            mix = mix + weight * part.astype(F32)
        gated.append((mix / mass * gate_ref[:, span]).astype(BF16))
    gated = [jnp.concatenate(gated[g : g + 2], axis=1) for g in range(0, PAIRS, 2)]
    update = dot(gather_lanes(gated).astype(BF16), output_ref[...])
    token_state = (single_ref[...] + update).astype(BF16)
    token_ref[...] = token_state
    returned = dot(token_state, back_ref[...])
    high = returned.astype(BF16)
    low = (returned - high.astype(F32)).astype(BF16)
    count = mid_ref.shape[0]
    owned = (lanes((tokens, count), 0) == owner_ref[...]).astype(F32).T.astype(BF16)
    atom_ref[...] = (mid_ref[...] + dot(owned, high) + dot(owned, low)).astype(BF16)


def call(kernel, out, megabytes, cost, **more):
    flops, size = cost
    return pl.pallas_call(
        kernel,
        out_shape=out,
        compiler_params=pltpu.CompilerParams(vmem_limit_bytes=megabytes * 1024 * 1024),
        cost_estimate=pl.CostEstimate(flops=flops, bytes_accessed=size, transcendentals=0),
        **more,
    )


def shape(dims, kind):
    return jax.ShapeDtypeStruct(dims, kind)


def per_device(
    atom_state, token_input, atom_owner, atom_bias, pair_bias, atom_proj, atom_output,
    pool_weight, token_proj, token_output, back_weight,
):
    rows, cols = lax.axis_size("row"), lax.axis_size("col")
    devices = rows * cols
    count, width = atom_state.shape
    tokens, depth = token_input.shape
    wide = HEADS * SLOT
    ends = devices - 1
    left = lax.ppermute(
        atom_state[count - REACH :], BOTH, [(i, i + 1) for i in range(ends)]
    )
    right = lax.ppermute(atom_state[:REACH], BOTH, [(i + 1, i) for i in range(ends)])
    mid, single, norm = call(
        atom_step,
        (
            shape((count, width), F32),
            shape((tokens, depth), F32),
            shape((tokens, depth), BF16),
        ),
        12,
        (400_000_000, 2_000_000),
    )(
        left, atom_state, right, token_input, atom_owner, atom_bias, atom_proj, atom_output,
        pool_weight,
    )
    ring = cols // 2
    turn = []
    for r in range(rows):
        for c in range(cols):
            to_row = (c // ring) * cols + 2 * ((c % ring + 2) % ring) + r % 2
            turn.append((r * cols + c, to_row * cols + r // 2))
    turned = lax.ppermute(norm, BOTH, turn)
    across = lax.ppermute(norm, "col", [(i, (i + ring) % cols) for i in range(cols)])
    own = jnp.concatenate([norm, across], axis=0)
    turned, own = lax.optimization_barrier((turned, own))
    same_core = [[i for i in range(rows) if i % 2 == e] for e in range(2)]
    near = lax.all_to_all(
        jnp.broadcast_to(turned[None], (rows // 2, tokens, depth)), "row", 0, 0,
        axis_index_groups=same_core,
    )
    along = [
        lax.ppermute(
            own, "col", [(i, i // ring * ring + (i + step) % ring) for i in range(cols)]
        )
        for step in (1, ring - 1, 2)
    ]
    far = lax.ppermute(near, "row", [(i, i ^ 1) for i in range(rows)])
    q_count, half = cols * tokens, rows * tokens // 2
    lane = 2 * SLOT
    queries, gates = call(
        query_step,
        (shape((PAIRS, q_count, lane), BF16), shape((tokens, wide), F32)),
        14,
        (900_000_000, 5_000_000),
    )(own, *along, norm, token_proj)
    near_k, near_v = call(
        project,
        (shape((PAIRS, half, lane), BF16), shape((PAIRS, half, lane), BF16)),
        14,
        (1_400_000_000, 5_000_000),
    )(near, token_proj)
    parts = call(
        token_step,
        shape((q_count, wide), BF16),
        32,
        (6_000_000_000, 14_000_000),
        in_specs=[pl.BlockSpec(memory_space=pltpu.VMEM)] * 5
        + [pl.BlockSpec(memory_space=pl.ANY)],
        scratch_shapes=[
            pltpu.VMEM((HEADS, q_count, 2 * half), BF16),
            pltpu.VMEM((PAIRS, half, lane), BF16),
            pltpu.VMEM((PAIRS, half, lane), BF16),
            pltpu.SemaphoreType.DMA((HEADS,)),
        ],
    )(queries, near_k, near_v, far, token_proj, pair_bias)
    parts = lax.all_to_all(parts.reshape(cols, tokens, wide), "col", 0, 0)
    return call(
        last_step,
        (shape((count, width), BF16), shape((tokens, depth), BF16)),
        12,
        (400_000_000, 5_000_000),
    )(parts, gates, single, mid, atom_owner, token_output, back_weight)


def solution(mesh):
    split = P(BOTH, None)
    placed = (
        split, split, split, P(None, BOTH, None), P(None, "row", "col"),
        P(), P(), P(), P(), P(), P(),
    )
    return jax.shard_map(
        per_device, mesh=mesh, in_specs=placed, out_specs=(split, split), check_vma=False
    )
```

```python
import math

import jax
import jax.numpy as jnp
from jax import lax
from jax.experimental import pallas as pl
from jax.experimental.pallas import tpu as pltpu
from jax.sharding import PartitionSpec as P

HEADS = 16
HEAD_DIM = 48
SLOT = 64
PAIRS = HEADS // 2
ATOM_HEADS = 4
WIN_Q = 32
WIN_K = 128
REACH = 48
EPSILON = 1e-05

BOTH = ("row", "col")
F32 = jnp.float32
BF16 = jnp.bfloat16
ATOM_MB = 20
SMALL = (1_000_000, 100_000)
ORDER = (2, 3, 0, 1, 6, 7, 4, 5)


def dot(a, b, contract=((1,), (0,))):
    return lax.dot_general(a, b, (contract, ((), ())), preferred_element_type=F32)


def layer_norm(values):
    centred = values - jnp.mean(values, axis=-1, keepdims=True)
    spread = jnp.mean(centred * centred, axis=-1, keepdims=True)
    return centred * lax.rsqrt(spread + EPSILON)


def lanes(shape, axis):
    return lax.broadcasted_iota(jnp.int32, shape, axis)


BAND = 2 * 2 * SLOT
STARTS = (0, 128, 384, 512)


def band_place(group, back=False):
    near = lanes((BAND, BAND), 1 if back else 0) + STARTS[group]
    far = lanes((BAND, BAND), 0 if back else 1) + group * BAND
    return ((near // HEAD_DIM == far // SLOT) & (near % HEAD_DIM == far % SLOT)).astype(BF16)


def spread(values):
    return [
        dot(values[:, STARTS[g] : STARTS[g] + BAND], band_place(g)) for g in range(HEADS // 4)
    ]


def gather_lanes(values):
    parts = [dot(values[g], band_place(g, True)) for g in range(HEADS // 4)]
    lane = 2 * SLOT
    return jnp.concatenate(
        [
            parts[0][:, :lane],
            parts[0][:, lane:] + parts[1][:, :lane],
            parts[1][:, lane:],
            parts[2][:, :lane],
            parts[2][:, lane:] + parts[3][:, :lane],
            parts[3][:, lane:],
        ],
        axis=1,
    )


def store_pairs(ref, bands):
    lane = 2 * SLOT
    for g, band in enumerate(bands):
        ref[2 * g] = band[:, :lane].astype(BF16)
        ref[2 * g + 1] = band[:, lane:].astype(BF16)


def atom_step(
    left_ref, right_ref, narrow_ref, broad_ref, owner_ref, mid_ref, single_ref, norm_ref,
):
    width = narrow_ref.shape[1]
    count = owner_ref.shape[1]
    state_ref = narrow_ref.at[:count]
    after = (1 + ATOM_HEADS) * count
    bias_ref = [narrow_ref.at[(1 + h) * count : (2 + h) * count] for h in range(ATOM_HEADS)]
    proj_ref = [narrow_ref.at[after + i * width : after + (i + 1) * width] for i in range(5)]
    output_ref = proj_ref[4]
    pool_ref, input_ref = broad_ref.at[:width], broad_ref.at[width:]
    windows = count // WIN_Q
    rows, cols = lax.axis_size("row"), lax.axis_size("col")
    first = (lax.axis_index("row") * cols + lax.axis_index("col")) * count
    total = count * rows * cols
    state = state_ref[...].astype(F32)
    extended = jnp.concatenate(
        [left_ref[...].astype(F32), state, right_ref[...].astype(F32)], axis=0
    )
    normed = layer_norm(extended).astype(BF16)
    keys = dot(normed, proj_ref[1][...]).astype(BF16)
    values = dot(normed, proj_ref[2][...]).astype(BF16)
    own = normed[REACH : REACH + count]
    queries = dot(own, proj_ref[0][...]).astype(BF16)
    gates = jax.nn.sigmoid(dot(own, proj_ref[3][...]))
    head_width = width // ATOM_HEADS
    head_of = lanes((WIN_Q, width), 1) // head_width
    factor = 1.0 / math.sqrt(head_width)
    gated = []
    for w in range(windows):
        start = w * WIN_Q
        query = queries[start : start + WIN_Q]
        stacked = jnp.concatenate(
            [jnp.where(head_of == h, query, jnp.zeros_like(query)) for h in range(ATOM_HEADS)],
            axis=0,
        )
        scores = dot(stacked, keys[start : start + WIN_K], ((1,), (1,))) * factor
        scores = scores + jnp.concatenate(
            [bias_ref[h][start : start + WIN_Q, :] for h in range(ATOM_HEADS)], axis=0
        ).astype(F32)
        if start < REACH or start + WIN_K > count + REACH:
            position = first + (start - REACH) + lanes(scores.shape, 1)
            scores = jnp.where((position >= 0) & (position < total), scores, -1e30)
        top = jnp.max(scores, axis=-1, keepdims=True)
        weights = jnp.exp(scores - top)
        weights = (weights / jnp.sum(weights, axis=-1, keepdims=True)).astype(BF16)
        mixed = dot(weights, values[start : start + WIN_K])
        mix = jnp.zeros((WIN_Q, width), F32)
        for h in range(ATOM_HEADS):
            mix = jnp.where(head_of == h, mixed[h * WIN_Q : (h + 1) * WIN_Q], mix)
        gated.append((mix * gates[start : start + WIN_Q]).astype(BF16))
    gated = jnp.concatenate(gated, axis=0)
    mid = state + dot(gated, output_ref[...])
    mid_ref[...] = mid
    lifted = jnp.maximum(dot(mid.astype(BF16), pool_ref[...]), 0.0).astype(BF16)
    tokens = input_ref.shape[0]
    owned = (lanes((tokens, count), 0) == owner_ref[...]).astype(F32)
    counts = jnp.sum(owned, axis=1, keepdims=True)
    pooled = dot(owned.astype(BF16), lifted)
    single = input_ref[...].astype(F32) + pooled / counts
    single_ref[...] = single
    norm_ref[...] = layer_norm(single).astype(BF16)


def query_step(own_ref, after_ref, before_ref, far_ref, norm_ref, proj_ref, q_ref, gate_ref):
    tokens = norm_ref.shape[0]
    lane = 2 * SLOT
    rows = jnp.concatenate(
        [own_ref[...], after_ref[...], before_ref[...], far_ref[...]], axis=0
    )
    bands = spread(dot(rows, proj_ref[0]).astype(BF16))
    ring = lax.axis_size("col") // 2
    me = lax.axis_index("col")
    high, low = me // ring, me % ring
    for i, step in enumerate((0, ring - 1, 1, 2)):
        for j in range(2):
            source = lax.rem(high + j, 2) * ring + lax.rem(low + step, ring)
            at = pl.ds(pl.multiple_of(source * tokens, 16), tokens)
            first = (2 * i + j) * tokens
            for g, band in enumerate(bands):
                block = band[first : first + tokens].astype(BF16)
                q_ref[2 * g, at, :] = block[:, :lane]
                q_ref[2 * g + 1, at, :] = block[:, lane:]
    gates = jax.nn.sigmoid(dot(norm_ref[...], proj_ref[3]))
    top = gates.astype(BF16)
    rest = (gates - top.astype(F32)).astype(BF16)
    for g, (a, b) in enumerate(zip(spread(top), spread(rest))):
        gate_ref[:, g * BAND : (g + 1) * BAND] = a + b


def project(blocks_ref, proj_ref, k_ref, v_ref):
    rows = jnp.concatenate([blocks_ref[i] for i in ORDER], axis=0)
    store_pairs(k_ref, spread(dot(rows, proj_ref[1]).astype(BF16)))
    mass = lanes((1, BAND), 1) % SLOT == HEAD_DIM
    bands = spread(dot(rows, proj_ref[2]).astype(BF16))
    store_pairs(v_ref, [jnp.where(mass, 1.0, band) for band in bands])


def token_step(q_ref, k_ref, v_ref, blocks_ref, proj_ref, bias_ref, part_ref, other_k, other_v):
    lane = 2 * SLOT
    project(blocks_ref, proj_ref, other_k, other_v)
    core = lax.rem(lax.axis_index("row"), 2)
    count, half = q_ref.shape[1], k_ref.shape[1]
    mine_at = pl.ds(pl.multiple_of(core * half, lane), half)
    other_at = pl.ds(pl.multiple_of((1 - core) * half, lane), half)
    at = lanes((count, lane), 1)
    factor = 1.0 / math.sqrt(HEAD_DIM)
    for pair in range(PAIRS):
        query = q_ref[pair]
        key = jnp.concatenate([k_ref[pair], other_k[pair]], axis=0)
        value = jnp.concatenate([v_ref[pair], other_v[pair]], axis=0)
        result = jnp.zeros((count, lane), F32)
        for a in range(2):
            head = 2 * pair + a
            mine = jnp.where(at // SLOT == a, query, jnp.zeros_like(query))
            bias = jnp.concatenate(
                [bias_ref[head, :, mine_at], bias_ref[head, :, other_at]], axis=1
            )
            scores = dot(mine, key, ((1,), (1,))) * factor + bias.astype(F32)
            top = jnp.max(scores, axis=-1, keepdims=True)
            mixed = dot(jnp.exp(scores - top).astype(BF16), value)
            base = a * SLOT + HEAD_DIM
            mass = mixed[:, base : base + 1]
            level = top + jnp.log(mass)
            high = level.astype(BF16).astype(F32)
            middle = (level - high).astype(BF16).astype(F32)
            low = level - high - middle
            part = mixed / mass
            part = jnp.where(at == base, high, part)
            part = jnp.where(at == base + 1, middle, part)
            part = jnp.where(at == base + 2, low, part)
            result = jnp.where(at // SLOT == a, part, result)
        part_ref[:, pair * lane : (pair + 1) * lane] = result.astype(BF16)


def last_step(
    part_ref, gate_ref, single_ref, mid_ref, owner_ref, output_ref, back_ref, atom_ref,
    token_ref,
):
    lane = 2 * SLOT
    shares, tokens, _ = part_ref.shape
    here, there = lanes((lane, lane), 0), lanes((lane, lane), 1)
    level_of = (
        (here // SLOT == there // SLOT)
        & (here % SLOT >= HEAD_DIM)
        & (here % SLOT < HEAD_DIM + 3)
    ).astype(BF16)
    gated = []
    for p in range(PAIRS):
        span = slice(p * lane, (p + 1) * lane)
        parts = [part_ref[c, :, span] for c in range(shares)]
        levels = [dot(part, level_of) for part in parts]
        top = levels[0]
        for level in levels[1:]:
            top = jnp.maximum(top, level)
        mass = jnp.zeros((tokens, lane), F32)
        mix = jnp.zeros((tokens, lane), F32)
        for part, level in zip(parts, levels):
            weight = jnp.exp(level - top)
            mass = mass + weight
            mix = mix + weight * part.astype(F32)
        gated.append((mix / mass * gate_ref[:, span]).astype(BF16))
    gated = [jnp.concatenate(gated[g : g + 2], axis=1) for g in range(0, PAIRS, 2)]
    update = dot(gather_lanes(gated).astype(BF16), output_ref[...])
    token_state = (single_ref[...] + update).astype(BF16)
    token_ref[...] = token_state
    returned = dot(token_state, back_ref[...])
    high = returned.astype(BF16)
    low = (returned - high.astype(F32)).astype(BF16)
    count = mid_ref.shape[0]
    owned = (lanes((tokens, count), 0) == owner_ref[...]).astype(F32).T.astype(BF16)
    atom_ref[...] = (mid_ref[...] + dot(owned, high) + dot(owned, low)).astype(BF16)


def call(kernel, out, megabytes, cost, **more):
    flops, size = cost
    return pl.pallas_call(
        kernel,
        out_shape=out,
        compiler_params=pltpu.CompilerParams(vmem_limit_bytes=megabytes * 1024 * 1024),
        cost_estimate=pl.CostEstimate(flops=flops, bytes_accessed=size, transcendentals=0),
        **more,
    )


def shape(dims, kind):
    return jax.ShapeDtypeStruct(dims, kind)


def per_device(
    atom_state, token_input, atom_owner, atom_bias, pair_bias, atom_proj, atom_output,
    pool_weight, token_proj, token_output, back_weight,
):
    rows, cols = lax.axis_size("row"), lax.axis_size("col")
    devices = rows * cols
    count, width = atom_state.shape
    tokens, depth = token_input.shape
    wide = HEADS * SLOT
    ends = devices - 1
    left = lax.ppermute(
        atom_state[count - REACH :], BOTH, [(i, i + 1) for i in range(ends)]
    )
    right = lax.ppermute(atom_state[:REACH], BOTH, [(i + 1, i) for i in range(ends)])
    narrow = jnp.concatenate(
        [atom_state]
        + [array.reshape(-1, width) for array in (atom_bias, atom_proj, atom_output)],
        axis=0,
    )
    broad = jnp.concatenate([pool_weight, token_input], axis=0)
    mid, single, norm = call(
        atom_step,
        (
            shape((count, width), F32),
            shape((tokens, depth), F32),
            shape((tokens, depth), BF16),
        ),
        ATOM_MB,
        (400_000_000, 2_000_000),
    )(left, right, narrow, broad, atom_owner)
    ring = cols // 2
    turn = []
    for r in range(rows):
        for c in range(cols):
            to_row = (c // ring) * cols + 2 * ((c % ring + 2) % ring) + r % 2
            turn.append((r * cols + c, to_row * cols + r // 2))
    turned = lax.ppermute(norm, BOTH, turn)
    across = lax.ppermute(norm, "col", [(i, (i + ring) % cols) for i in range(cols)])
    own = jnp.concatenate([norm, across], axis=0)
    turned, own = lax.optimization_barrier((turned, own))
    same_core = [[i for i in range(rows) if i % 2 == e] for e in range(2)]
    near = lax.all_to_all(
        jnp.broadcast_to(turned[None], (rows // 2, tokens, depth)), "row", 0, 0,
        axis_index_groups=same_core,
    )
    along = [
        lax.ppermute(
            own, "col", [(i, i // ring * ring + (i + step) % ring) for i in range(cols)]
        )
        for step in (1, ring - 1, 2)
    ]
    near, *along = lax.optimization_barrier((near, *along))
    far = lax.ppermute(near, "row", [(i, i ^ 1) for i in range(rows)])
    q_count, half = cols * tokens, rows * tokens // 2
    lane = 2 * SLOT
    queries, gates = call(
        query_step,
        (shape((PAIRS, q_count, lane), BF16), shape((tokens, wide), F32)),
        14,
        SMALL,
    )(own, *along, norm, token_proj)
    near_k, near_v = call(
        project,
        (shape((PAIRS, half, lane), BF16), shape((PAIRS, half, lane), BF16)),
        14,
        SMALL,
    )(near, token_proj)
    parts = call(
        token_step,
        shape((q_count, wide), BF16),
        32,
        (6_000_000_000, 14_000_000),
        scratch_shapes=[
            pltpu.VMEM((PAIRS, half, lane), BF16),
            pltpu.VMEM((PAIRS, half, lane), BF16),
        ],
    )(queries, near_k, near_v, far, token_proj, pair_bias)
    parts = lax.all_to_all(parts.reshape(cols, tokens, wide), "col", 0, 0)
    return call(
        last_step,
        (shape((count, width), BF16), shape((tokens, depth), BF16)),
        12,
        (400_000_000, 5_000_000),
    )(parts, gates, single, mid, atom_owner, token_output, back_weight)


def solution(mesh):
    split = P(BOTH, None)
    placed = (
        split, split, split, P(None, BOTH, None), P(None, "row", "col"),
        P(), P(), P(), P(), P(), P(),
    )
    return jax.shard_map(
        per_device, mesh=mesh, in_specs=placed, out_specs=(split, split), check_vma=False
    )
```

```python
import math

import jax
import jax.numpy as jnp
from jax import lax
from jax.experimental import pallas as pl
from jax.experimental.pallas import tpu as pltpu
from jax.sharding import PartitionSpec as P

HEADS = 16
HEAD_DIM = 48
SLOT = 64
PAIRS = HEADS // 2
ATOM_HEADS = 4
WIN_Q = 32
WIN_K = 128
REACH = 48
EPSILON = 1e-05

BOTH = ("row", "col")
F32 = jnp.float32
BF16 = jnp.bfloat16
ATOM_MB = 20
MOST = 47
SMALL = (1_000_000, 100_000)
ORDER = (2, 3, 0, 1, 6, 7, 4, 5)


def dot(a, b, contract=((1,), (0,))):
    return lax.dot_general(a, b, (contract, ((), ())), preferred_element_type=F32)


def layer_norm(values):
    centred = values - jnp.mean(values, axis=-1, keepdims=True)
    spread = jnp.mean(centred * centred, axis=-1, keepdims=True)
    return centred * lax.rsqrt(spread + EPSILON)


def lanes(shape, axis):
    return lax.broadcasted_iota(jnp.int32, shape, axis)


BAND = 2 * 2 * SLOT
STARTS = (0, 128, 384, 512)


def band_place(group, back=False):
    near = lanes((BAND, BAND), 1 if back else 0) + STARTS[group]
    far = lanes((BAND, BAND), 0 if back else 1) + group * BAND
    return ((near // HEAD_DIM == far // SLOT) & (near % HEAD_DIM == far % SLOT)).astype(BF16)


def spread(values):
    return [
        dot(values[:, STARTS[g] : STARTS[g] + BAND], band_place(g)) for g in range(HEADS // 4)
    ]


def gather_lanes(values):
    parts = [dot(values[g], band_place(g, True)) for g in range(HEADS // 4)]
    lane = 2 * SLOT
    return jnp.concatenate(
        [
            parts[0][:, :lane],
            parts[0][:, lane:] + parts[1][:, :lane],
            parts[1][:, lane:],
            parts[2][:, :lane],
            parts[2][:, lane:] + parts[3][:, :lane],
            parts[3][:, lane:],
        ],
        axis=1,
    )


def store_pairs(ref, bands):
    lane = 2 * SLOT
    for g, band in enumerate(bands):
        ref[2 * g] = band[:, :lane].astype(BF16)
        ref[2 * g + 1] = band[:, lane:].astype(BF16)


def atom_step(
    left_ref, right_ref, narrow_ref, broad_ref, owner_ref, mid_ref, single_ref, norm_ref,
):
    width = narrow_ref.shape[1]
    count = owner_ref.shape[1]
    state_ref = narrow_ref.at[:count]
    after = (1 + ATOM_HEADS) * count
    bias_ref = [narrow_ref.at[(1 + h) * count : (2 + h) * count] for h in range(ATOM_HEADS)]
    proj_ref = [narrow_ref.at[after + i * width : after + (i + 1) * width] for i in range(5)]
    output_ref = proj_ref[4]
    pool_ref, input_ref = broad_ref.at[:width], broad_ref.at[width:]
    windows = count // WIN_Q
    rows, cols = lax.axis_size("row"), lax.axis_size("col")
    first = (lax.axis_index("row") * cols + lax.axis_index("col")) * count
    total = count * rows * cols
    state = state_ref[...].astype(F32)
    extended = jnp.concatenate(
        [left_ref[...].astype(F32), state, right_ref[...].astype(F32)], axis=0
    )
    normed = layer_norm(extended).astype(BF16)
    keys = dot(normed, proj_ref[1][...]).astype(BF16)
    values = dot(normed, proj_ref[2][...]).astype(BF16)
    own = normed[REACH : REACH + count]
    queries = dot(own, proj_ref[0][...]).astype(BF16)
    gates = jax.nn.sigmoid(dot(own, proj_ref[3][...]))
    head_width = width // ATOM_HEADS
    head_of = lanes((WIN_Q, width), 1) // head_width
    factor = 1.0 / math.sqrt(head_width)
    gated = []
    for w in range(windows):
        start = w * WIN_Q
        query = queries[start : start + WIN_Q]
        stacked = jnp.concatenate(
            [jnp.where(head_of == h, query, jnp.zeros_like(query)) for h in range(ATOM_HEADS)],
            axis=0,
        )
        scores = dot(stacked, keys[start : start + WIN_K], ((1,), (1,))) * factor
        scores = scores + jnp.concatenate(
            [bias_ref[h][start : start + WIN_Q, :] for h in range(ATOM_HEADS)], axis=0
        ).astype(F32)
        if start < REACH or start + WIN_K > count + REACH:
            position = first + (start - REACH) + lanes(scores.shape, 1)
            scores = jnp.where((position >= 0) & (position < total), scores, -1e30)
        top = jnp.max(scores, axis=-1, keepdims=True)
        weights = jnp.exp(scores - top)
        weights = (weights / jnp.sum(weights, axis=-1, keepdims=True)).astype(BF16)
        mixed = dot(weights, values[start : start + WIN_K])
        mix = jnp.zeros((WIN_Q, width), F32)
        for h in range(ATOM_HEADS):
            mix = jnp.where(head_of == h, mixed[h * WIN_Q : (h + 1) * WIN_Q], mix)
        gated.append((mix * gates[start : start + WIN_Q]).astype(BF16))
    gated = jnp.concatenate(gated, axis=0)
    mid = state + dot(gated, output_ref[...])
    mid_ref[...] = mid
    lifted = jnp.maximum(dot(mid.astype(BF16), pool_ref[...]), 0.0).astype(BF16)
    tokens = input_ref.shape[0]
    owned = (lanes((tokens, count), 0) == owner_ref[...]).astype(F32)
    counts = jnp.sum(owned, axis=1, keepdims=True)
    pooled = dot(owned.astype(BF16), lifted)
    single = input_ref[...].astype(F32) + pooled / counts
    single_ref[...] = single
    norm_ref[...] = layer_norm(single).astype(BF16)


def query_step(
    own_ref, after_ref, before_ref, far_ref, norm_ref, proj_hbm, q_ref, gate_ref, proj_ref, sems
):
    copies = [
        pltpu.make_async_copy(proj_hbm.at[3 * i], proj_ref.at[i], sems.at[i]) for i in range(2)
    ]
    for copy in copies:
        copy.start()
    tokens = norm_ref.shape[0]
    lane = 2 * SLOT
    rows = jnp.concatenate(
        [own_ref[...], after_ref[...], before_ref[...], far_ref[...]], axis=0
    )
    copies[0].wait()
    bands = spread(dot(rows, proj_ref[0]).astype(BF16))
    ring = lax.axis_size("col") // 2
    me = lax.axis_index("col")
    high, low = me // ring, me % ring
    for i, step in enumerate((0, ring - 1, 1, 2)):
        for j in range(2):
            source = lax.rem(high + j, 2) * ring + lax.rem(low + step, ring)
            at = pl.ds(pl.multiple_of(source * tokens, 16), tokens)
            first = (2 * i + j) * tokens
            for g, band in enumerate(bands):
                block = band[first : first + tokens].astype(BF16)
                q_ref[2 * g, at, :] = block[:, :lane]
                q_ref[2 * g + 1, at, :] = block[:, lane:]
    copies[1].wait()
    gates = jax.nn.sigmoid(dot(norm_ref[...], proj_ref[1]))
    top = gates.astype(BF16)
    rest = (gates - top.astype(F32)).astype(BF16)
    for g, (a, b) in enumerate(zip(spread(top), spread(rest))):
        gate_ref[:, g * BAND : (g + 1) * BAND] = a + b


def key_rows(blocks_ref, weight, k_ref):
    rows = jnp.concatenate([blocks_ref[i] for i in ORDER], axis=0)
    store_pairs(k_ref, spread(dot(rows, weight).astype(BF16)))


def value_rows(blocks_ref, weight, v_ref):
    rows = jnp.concatenate([blocks_ref[i] for i in ORDER], axis=0)
    mass = lanes((1, BAND), 1) % SLOT == HEAD_DIM
    bands = spread(dot(rows, weight).astype(BF16))
    store_pairs(v_ref, [jnp.where(mass, 1.0, band) for band in bands])


def near_step(blocks_ref, proj_hbm, k_ref, v_ref, proj_ref, sems):
    copies = [
        pltpu.make_async_copy(proj_hbm.at[1 + i], proj_ref.at[i], sems.at[i]) for i in range(2)
    ]
    for copy in copies:
        copy.start()
    copies[0].wait()
    key_rows(blocks_ref, proj_ref[0], k_ref)
    copies[1].wait()
    value_rows(blocks_ref, proj_ref[1], v_ref)


def token_step(
    q_ref, k_ref, v_ref, blocks_ref, proj_ref, bias_hbm, part_ref, bias_ref, other_k, other_v, sems
):
    lane = 2 * SLOT
    heads = (slice(0, 4), slice(4, HEADS))
    copies = [
        pltpu.make_async_copy(bias_hbm.at[span], bias_ref.at[span], sems.at[i])
        for i, span in enumerate(heads)
    ]
    for copy in copies:
        copy.start()
    key_rows(blocks_ref, proj_ref[0], other_k)
    value_rows(blocks_ref, proj_ref[1], other_v)
    core = lax.rem(lax.axis_index("row"), 2)
    count, half = q_ref.shape[1], k_ref.shape[1]
    mine_at = pl.ds(pl.multiple_of(core * half, lane), half)
    other_at = pl.ds(pl.multiple_of((1 - core) * half, lane), half)
    at = lanes((count, lane), 1)
    factor = 1.0 / math.sqrt(HEAD_DIM)
    for pair in range(PAIRS):
        if pair == 0:
            copies[0].wait()
        if pair == 2:
            copies[1].wait()
        query = q_ref[pair]
        key = jnp.concatenate([k_ref[pair], other_k[pair]], axis=0)
        value = jnp.concatenate([v_ref[pair], other_v[pair]], axis=0)
        result = jnp.zeros((count, lane), F32)
        for a in range(2):
            head = 2 * pair + a
            mine = jnp.where(at // SLOT == a, query, jnp.zeros_like(query))
            bias = jnp.concatenate(
                [bias_ref[head, :, mine_at], bias_ref[head, :, other_at]], axis=1
            )
            scores = dot(mine, key, ((1,), (1,))) * factor + bias.astype(F32)
            top = jnp.max(scores, axis=-1, keepdims=True)
            mixed = dot(jnp.exp(scores - top).astype(BF16), value)
            base = a * SLOT + HEAD_DIM
            mass = mixed[:, base : base + 1]
            level = top + jnp.log(mass)
            high = level.astype(BF16).astype(F32)
            middle = (level - high).astype(BF16).astype(F32)
            low = level - high - middle
            part = mixed / mass
            part = jnp.where(at == base, high, part)
            part = jnp.where(at == base + 1, middle, part)
            part = jnp.where(at == base + 2, low, part)
            result = jnp.where(at // SLOT == a, part, result)
        part_ref[:, pair * lane : (pair + 1) * lane] = result.astype(BF16)


def last_step(
    part_ref, gate_ref, single_ref, mid_ref, owner_ref, output_ref, back_ref, atom_ref,
    token_ref,
):
    lane = 2 * SLOT
    shares, tokens, _ = part_ref.shape
    here, there = lanes((lane, lane), 0), lanes((lane, lane), 1)
    level_of = (
        (here // SLOT == there // SLOT)
        & (here % SLOT >= HEAD_DIM)
        & (here % SLOT < HEAD_DIM + 3)
    ).astype(BF16)
    gated = []
    for p in range(PAIRS):
        span = slice(p * lane, (p + 1) * lane)
        parts = [part_ref[c, :, span] for c in range(shares)]
        levels = [dot(part, level_of) for part in parts]
        top = levels[0]
        for level in levels[1:]:
            top = jnp.maximum(top, level)
        mass = jnp.zeros((tokens, lane), F32)
        mix = jnp.zeros((tokens, lane), F32)
        for part, level in zip(parts, levels):
            weight = jnp.exp(level - top)
            mass = mass + weight
            mix = mix + weight * part.astype(F32)
        gated.append((mix / mass * gate_ref[:, span]).astype(BF16))
    gated = [jnp.concatenate(gated[g : g + 2], axis=1) for g in range(0, PAIRS, 2)]
    update = dot(gather_lanes(gated).astype(BF16), output_ref[...])
    token_state = (single_ref[...] + update).astype(BF16)
    token_ref[...] = token_state
    returned = dot(token_state, back_ref[...])
    high = returned.astype(BF16)
    low = (returned - high.astype(F32)).astype(BF16)
    count = mid_ref.shape[0]
    owned = (lanes((tokens, count), 0) == owner_ref[...]).astype(F32).T.astype(BF16)
    atom_ref[...] = (mid_ref[...] + dot(owned, high) + dot(owned, low)).astype(BF16)


def call(kernel, out, megabytes, cost, **more):
    flops, size = cost
    return pl.pallas_call(
        kernel,
        out_shape=out,
        compiler_params=pltpu.CompilerParams(vmem_limit_bytes=megabytes * 1024 * 1024),
        cost_estimate=pl.CostEstimate(flops=flops, bytes_accessed=size, transcendentals=0),
        **more,
    )


def shape(dims, kind):
    return jax.ShapeDtypeStruct(dims, kind)


def per_device(
    atom_state, token_input, atom_owner, atom_bias, pair_bias, atom_proj, atom_output,
    pool_weight, token_proj, token_output, back_weight,
):
    rows, cols = lax.axis_size("row"), lax.axis_size("col")
    devices = rows * cols
    count, width = atom_state.shape
    tokens, depth = token_input.shape
    wide = HEADS * SLOT
    ends = devices - 1
    left = lax.ppermute(
        atom_state[count - REACH :], BOTH, [(i, i + 1) for i in range(ends)]
    )
    right = lax.ppermute(atom_state[:REACH], BOTH, [(i + 1, i) for i in range(ends)])
    narrow = jnp.concatenate(
        [atom_state]
        + [array.reshape(-1, width) for array in (atom_bias, atom_proj, atom_output)],
        axis=0,
    )
    broad = jnp.concatenate([pool_weight, token_input], axis=0)
    mid, single, norm = call(
        atom_step,
        (
            shape((count, width), F32),
            shape((tokens, depth), F32),
            shape((tokens, depth), BF16),
        ),
        ATOM_MB,
        (400_000_000, 2_000_000),
    )(left, right, narrow, broad, atom_owner)
    ring = cols // 2
    turn = []
    for r in range(rows):
        for c in range(cols):
            to_row = (c // ring) * cols + 2 * ((c % ring + 2) % ring) + r % 2
            turn.append((r * cols + c, to_row * cols + r // 2))
    turned = lax.ppermute(norm, BOTH, turn)
    across = lax.ppermute(norm, "col", [(i, (i + ring) % cols) for i in range(cols)])
    own = jnp.concatenate([norm, across], axis=0)
    turned, own = lax.optimization_barrier((turned, own))
    same_core = [[i for i in range(rows) if i % 2 == e] for e in range(2)]
    near = lax.all_to_all(
        jnp.broadcast_to(turned[None], (rows // 2, tokens, depth)), "row", 0, 0,
        axis_index_groups=same_core,
    )
    along = [
        lax.ppermute(
            own, "col", [(i, i // ring * ring + (i + step) % ring) for i in range(cols)]
        )
        for step in (1, ring - 1, 2)
    ]
    near, *along = lax.optimization_barrier((near, *along))
    far = lax.ppermute(near, "row", [(i, i ^ 1) for i in range(rows)])
    q_count, half = cols * tokens, rows * tokens // 2
    lane = 2 * SLOT
    in_vmem, in_hbm = (pl.BlockSpec(memory_space=space) for space in (pltpu.VMEM, pltpu.HBM))
    queries, gates = call(
        query_step,
        (shape((PAIRS, q_count, lane), BF16), shape((tokens, wide), F32)),
        MOST,
        SMALL,
        in_specs=[in_vmem] * 5 + [in_hbm],
        scratch_shapes=[pltpu.VMEM((2, depth, depth), BF16), pltpu.SemaphoreType.DMA((2,))],
    )(own, *along, norm, token_proj)
    near_k, near_v, key_weights = call(
        near_step,
        (
            shape((PAIRS, half, lane), BF16),
            shape((PAIRS, half, lane), BF16),
            shape((2, depth, depth), BF16),
        ),
        MOST,
        SMALL,
        in_specs=[in_vmem, in_hbm],
        scratch_shapes=[pltpu.SemaphoreType.DMA((2,))],
    )(near, token_proj)
    parts = call(
        token_step,
        shape((q_count, wide), BF16),
        MOST,
        (6_000_000_000, 14_000_000),
        in_specs=[in_vmem] * 5 + [in_hbm],
        scratch_shapes=[
            pltpu.VMEM((HEADS, q_count, 2 * half), BF16),
            pltpu.VMEM((PAIRS, half, lane), BF16),
            pltpu.VMEM((PAIRS, half, lane), BF16),
            pltpu.SemaphoreType.DMA((2,)),
        ],
    )(queries, near_k, near_v, far, key_weights, pair_bias)
    parts = lax.all_to_all(parts.reshape(cols, tokens, wide), "col", 0, 0)
    return call(
        last_step,
        (shape((count, width), BF16), shape((tokens, depth), BF16)),
        12,
        (400_000_000, 5_000_000),
    )(parts, gates, single, mid, atom_owner, token_output, back_weight)


def solution(mesh):
    split = P(BOTH, None)
    placed = (
        split, split, split, P(None, BOTH, None), P(None, "row", "col"),
        P(), P(), P(), P(), P(), P(),
    )
    return jax.shard_map(
        per_device, mesh=mesh, in_specs=placed, out_specs=(split, split), check_vma=False
    )
```

```python
import math

import jax
import jax.numpy as jnp
from jax import lax
from jax.experimental import pallas as pl
from jax.experimental.pallas import tpu as pltpu
from jax.sharding import PartitionSpec as P

HEADS = 16
HEAD_DIM = 48
SLOT = 64
PAIRS = HEADS // 2
ATOM_HEADS = 4
WIN_Q = 32
WIN_K = 128
REACH = 48
EPSILON = 1e-05

BOTH = ("row", "col")
F32 = jnp.float32
BF16 = jnp.bfloat16
ATOM_MB = 20
SMALL = (1_000_000, 100_000)
ORDER = (2, 3, 0, 1, 6, 7, 4, 5)


def dot(a, b, contract=((1,), (0,))):
    return lax.dot_general(a, b, (contract, ((), ())), preferred_element_type=F32)


def layer_norm(values):
    centred = values - jnp.mean(values, axis=-1, keepdims=True)
    spread = jnp.mean(centred * centred, axis=-1, keepdims=True)
    return centred * lax.rsqrt(spread + EPSILON)


def lanes(shape, axis):
    return lax.broadcasted_iota(jnp.int32, shape, axis)


BAND = 2 * 2 * SLOT
STARTS = (0, 128, 384, 512)


def band_place(group, back=False):
    near = lanes((BAND, BAND), 1 if back else 0) + STARTS[group]
    far = lanes((BAND, BAND), 0 if back else 1) + group * BAND
    return ((near // HEAD_DIM == far // SLOT) & (near % HEAD_DIM == far % SLOT)).astype(BF16)


def spread(values):
    return [
        dot(values[:, STARTS[g] : STARTS[g] + BAND], band_place(g)) for g in range(HEADS // 4)
    ]


def gather_lanes(values):
    parts = [dot(values[g], band_place(g, True)) for g in range(HEADS // 4)]
    lane = 2 * SLOT
    return jnp.concatenate(
        [
            parts[0][:, :lane],
            parts[0][:, lane:] + parts[1][:, :lane],
            parts[1][:, lane:],
            parts[2][:, :lane],
            parts[2][:, lane:] + parts[3][:, :lane],
            parts[3][:, lane:],
        ],
        axis=1,
    )


def store_pairs(ref, bands):
    lane = 2 * SLOT
    for g, band in enumerate(bands):
        ref[2 * g] = band[:, :lane].astype(BF16)
        ref[2 * g + 1] = band[:, lane:].astype(BF16)


def atom_step(
    left_ref, right_ref, narrow_ref, broad_ref, owner_ref, mid_ref, single_ref, norm_ref,
):
    width = narrow_ref.shape[1]
    count = owner_ref.shape[1]
    state_ref = narrow_ref.at[:count]
    after = (1 + ATOM_HEADS) * count
    bias_ref = [narrow_ref.at[(1 + h) * count : (2 + h) * count] for h in range(ATOM_HEADS)]
    proj_ref = [narrow_ref.at[after + i * width : after + (i + 1) * width] for i in range(5)]
    output_ref = proj_ref[4]
    pool_ref, input_ref = broad_ref.at[:width], broad_ref.at[width:]
    windows = count // WIN_Q
    rows, cols = lax.axis_size("row"), lax.axis_size("col")
    first = (lax.axis_index("row") * cols + lax.axis_index("col")) * count
    total = count * rows * cols
    state = state_ref[...].astype(F32)
    extended = jnp.concatenate(
        [left_ref[...].astype(F32), state, right_ref[...].astype(F32)], axis=0
    )
    normed = layer_norm(extended).astype(BF16)
    keys = dot(normed, proj_ref[1][...]).astype(BF16)
    values = dot(normed, proj_ref[2][...]).astype(BF16)
    own = normed[REACH : REACH + count]
    queries = dot(own, proj_ref[0][...]).astype(BF16)
    gates = jax.nn.sigmoid(dot(own, proj_ref[3][...]))
    head_width = width // ATOM_HEADS
    head_of = lanes((WIN_Q, width), 1) // head_width
    factor = 1.0 / math.sqrt(head_width)
    gated = []
    for w in range(windows):
        start = w * WIN_Q
        query = queries[start : start + WIN_Q]
        stacked = jnp.concatenate(
            [jnp.where(head_of == h, query, jnp.zeros_like(query)) for h in range(ATOM_HEADS)],
            axis=0,
        )
        scores = dot(stacked, keys[start : start + WIN_K], ((1,), (1,))) * factor
        scores = scores + jnp.concatenate(
            [bias_ref[h][start : start + WIN_Q, :] for h in range(ATOM_HEADS)], axis=0
        ).astype(F32)
        if start < REACH or start + WIN_K > count + REACH:
            position = first + (start - REACH) + lanes(scores.shape, 1)
            scores = jnp.where((position >= 0) & (position < total), scores, -1e30)
        top = jnp.max(scores, axis=-1, keepdims=True)
        weights = jnp.exp(scores - top)
        weights = (weights / jnp.sum(weights, axis=-1, keepdims=True)).astype(BF16)
        mixed = dot(weights, values[start : start + WIN_K])
        mix = jnp.zeros((WIN_Q, width), F32)
        for h in range(ATOM_HEADS):
            mix = jnp.where(head_of == h, mixed[h * WIN_Q : (h + 1) * WIN_Q], mix)
        gated.append((mix * gates[start : start + WIN_Q]).astype(BF16))
    gated = jnp.concatenate(gated, axis=0)
    mid = state + dot(gated, output_ref[...])
    mid_ref[...] = mid
    lifted = jnp.maximum(dot(mid.astype(BF16), pool_ref[...]), 0.0).astype(BF16)
    tokens = input_ref.shape[0]
    owned = (lanes((tokens, count), 0) == owner_ref[...]).astype(F32)
    counts = jnp.sum(owned, axis=1, keepdims=True)
    pooled = dot(owned.astype(BF16), lifted)
    single = input_ref[...].astype(F32) + pooled / counts
    single_ref[...] = single
    norm_ref[...] = layer_norm(single).astype(BF16)


def query_step(own_ref, after_ref, before_ref, far_ref, norm_ref, proj_ref, q_ref, gate_ref):
    tokens = norm_ref.shape[0]
    lane = 2 * SLOT
    rows = jnp.concatenate(
        [own_ref[...], after_ref[...], before_ref[...], far_ref[...]], axis=0
    )
    bands = spread(dot(rows, proj_ref[0]).astype(BF16))
    ring = lax.axis_size("col") // 2
    me = lax.axis_index("col")
    high, low = me // ring, me % ring
    for i, step in enumerate((0, ring - 1, 1, 2)):
        for j in range(2):
            source = lax.rem(high + j, 2) * ring + lax.rem(low + step, ring)
            at = pl.ds(pl.multiple_of(source * tokens, 16), tokens)
            first = (2 * i + j) * tokens
            for g, band in enumerate(bands):
                block = band[first : first + tokens].astype(BF16)
                q_ref[2 * g, at, :] = block[:, :lane]
                q_ref[2 * g + 1, at, :] = block[:, lane:]
    gates = jax.nn.sigmoid(dot(norm_ref[...], proj_ref[3]))
    top = gates.astype(BF16)
    rest = (gates - top.astype(F32)).astype(BF16)
    for g, (a, b) in enumerate(zip(spread(top), spread(rest))):
        gate_ref[:, g * BAND : (g + 1) * BAND] = a + b


def project(blocks_ref, proj_ref, k_ref, v_ref):
    rows = jnp.concatenate([blocks_ref[i] for i in ORDER], axis=0)
    store_pairs(k_ref, spread(dot(rows, proj_ref[1]).astype(BF16)))
    mass = lanes((1, BAND), 1) % SLOT == HEAD_DIM
    bands = spread(dot(rows, proj_ref[2]).astype(BF16))
    store_pairs(v_ref, [jnp.where(mass, 1.0, band) for band in bands])


def token_step(q_ref, k_ref, v_ref, blocks_ref, proj_ref, bias_ref, part_ref, other_k, other_v):
    lane = 2 * SLOT
    project(blocks_ref, proj_ref, other_k, other_v)
    core = lax.rem(lax.axis_index("row"), 2)
    count, half = q_ref.shape[1], k_ref.shape[1]
    mine_at = pl.ds(pl.multiple_of(core * half, lane), half)
    other_at = pl.ds(pl.multiple_of((1 - core) * half, lane), half)
    at = lanes((count, lane), 1)
    factor = 1.0 / math.sqrt(HEAD_DIM)
    for pair in range(PAIRS):
        query = q_ref[pair]
        key = jnp.concatenate([k_ref[pair], other_k[pair]], axis=0)
        value = jnp.concatenate([v_ref[pair], other_v[pair]], axis=0)
        result = jnp.zeros((count, lane), F32)
        for a in range(2):
            head = 2 * pair + a
            mine = jnp.where(at // SLOT == a, query, jnp.zeros_like(query))
            bias = jnp.concatenate(
                [bias_ref[head, :, mine_at], bias_ref[head, :, other_at]], axis=1
            )
            scores = dot(mine, key, ((1,), (1,))) * factor + bias.astype(F32)
            top = jnp.max(scores, axis=-1, keepdims=True)
            mixed = dot(jnp.exp(scores - top).astype(BF16), value)
            base = a * SLOT + HEAD_DIM
            mass = mixed[:, base : base + 1]
            level = top + jnp.log(mass)
            high = level.astype(BF16).astype(F32)
            middle = (level - high).astype(BF16).astype(F32)
            low = level - high - middle
            part = mixed / mass
            part = jnp.where(at == base, high, part)
            part = jnp.where(at == base + 1, middle, part)
            part = jnp.where(at == base + 2, low, part)
            result = jnp.where(at // SLOT == a, part, result)
        part_ref[:, pair * lane : (pair + 1) * lane] = result.astype(BF16)


def last_step(
    part_ref, gate_ref, single_ref, mid_ref, owner_ref, output_ref, back_ref, atom_ref,
    token_ref,
):
    lane = 2 * SLOT
    shares, tokens, _ = part_ref.shape
    here, there = lanes((lane, lane), 0), lanes((lane, lane), 1)
    level_of = (
        (here // SLOT == there // SLOT)
        & (here % SLOT >= HEAD_DIM)
        & (here % SLOT < HEAD_DIM + 3)
    ).astype(BF16)
    gated = []
    for p in range(PAIRS):
        span = slice(p * lane, (p + 1) * lane)
        parts = [part_ref[c, :, span] for c in range(shares)]
        levels = [dot(part, level_of) for part in parts]
        top = levels[0]
        for level in levels[1:]:
            top = jnp.maximum(top, level)
        mass = jnp.zeros((tokens, lane), F32)
        mix = jnp.zeros((tokens, lane), F32)
        for part, level in zip(parts, levels):
            weight = jnp.exp(level - top)
            mass = mass + weight
            mix = mix + weight * part.astype(F32)
        gated.append((mix / mass * gate_ref[:, span]).astype(BF16))
    gated = [jnp.concatenate(gated[g : g + 2], axis=1) for g in range(0, PAIRS, 2)]
    update = dot(gather_lanes(gated).astype(BF16), output_ref[...])
    token_state = (single_ref[...] + update).astype(BF16)
    token_ref[...] = token_state
    returned = dot(token_state, back_ref[...])
    high = returned.astype(BF16)
    low = (returned - high.astype(F32)).astype(BF16)
    count = mid_ref.shape[0]
    owned = (lanes((tokens, count), 0) == owner_ref[...]).astype(F32).T.astype(BF16)
    atom_ref[...] = (mid_ref[...] + dot(owned, high) + dot(owned, low)).astype(BF16)


def call(kernel, out, megabytes, cost, **more):
    flops, size = cost
    return pl.pallas_call(
        kernel,
        out_shape=out,
        compiler_params=pltpu.CompilerParams(vmem_limit_bytes=megabytes * 1024 * 1024),
        cost_estimate=pl.CostEstimate(flops=flops, bytes_accessed=size, transcendentals=0),
        **more,
    )


def shape(dims, kind):
    return jax.ShapeDtypeStruct(dims, kind)


def per_device(
    atom_state, token_input, atom_owner, atom_bias, pair_bias, atom_proj, atom_output,
    pool_weight, token_proj, token_output, back_weight,
):
    rows, cols = lax.axis_size("row"), lax.axis_size("col")
    devices = rows * cols
    count, width = atom_state.shape
    tokens, depth = token_input.shape
    wide = HEADS * SLOT
    ends = devices - 1
    left = lax.ppermute(
        atom_state[count - REACH :], BOTH, [(i, i + 1) for i in range(ends)]
    )
    right = lax.ppermute(atom_state[:REACH], BOTH, [(i + 1, i) for i in range(ends)])
    narrow = jnp.concatenate(
        [atom_state]
        + [array.reshape(-1, width) for array in (atom_bias, atom_proj, atom_output)],
        axis=0,
    )
    broad = jnp.concatenate([pool_weight, token_input], axis=0)
    mid, single, norm = call(
        atom_step,
        (
            shape((count, width), F32),
            shape((tokens, depth), F32),
            shape((tokens, depth), BF16),
        ),
        ATOM_MB,
        (400_000_000, 2_000_000),
    )(left, right, narrow, broad, atom_owner)
    ring = cols // 2
    turn = []
    for r in range(rows):
        for c in range(cols):
            to_row = (c // ring) * cols + 2 * ((c % ring + 2) % ring) + r % 2
            turn.append((r * cols + c, to_row * cols + r // 2))
    turned = lax.ppermute(norm, BOTH, turn)
    across = lax.ppermute(norm, "col", [(i, (i + ring) % cols) for i in range(cols)])
    own = jnp.concatenate([norm, across], axis=0)
    along = [
        lax.ppermute(
            own, "col", [(i, i // ring * ring + (i + step) % ring) for i in range(cols)]
        )
        for step in (1, ring - 1, 2)
    ]
    turned, *along = lax.optimization_barrier((turned, *along))
    same_core = [[i for i in range(rows) if i % 2 == e] for e in range(2)]
    near = lax.all_to_all(
        jnp.broadcast_to(turned[None], (rows // 2, tokens, depth)), "row", 0, 0,
        axis_index_groups=same_core,
    )
    far = lax.ppermute(near, "row", [(i, i ^ 1) for i in range(rows)])
    q_count, half = cols * tokens, rows * tokens // 2
    lane = 2 * SLOT
    queries, gates = call(
        query_step,
        (shape((PAIRS, q_count, lane), BF16), shape((tokens, wide), F32)),
        14,
        SMALL,
    )(own, *along, norm, token_proj)
    near_k, near_v = call(
        project,
        (shape((PAIRS, half, lane), BF16), shape((PAIRS, half, lane), BF16)),
        14,
        SMALL,
    )(near, token_proj)
    parts = call(
        token_step,
        shape((q_count, wide), BF16),
        32,
        (6_000_000_000, 14_000_000),
        scratch_shapes=[
            pltpu.VMEM((PAIRS, half, lane), BF16),
            pltpu.VMEM((PAIRS, half, lane), BF16),
        ],
    )(queries, near_k, near_v, far, token_proj, pair_bias)
    parts = lax.all_to_all(parts.reshape(cols, tokens, wide), "col", 0, 0)
    return call(
        last_step,
        (shape((count, width), BF16), shape((tokens, depth), BF16)),
        12,
        (400_000_000, 5_000_000),
    )(parts, gates, single, mid, atom_owner, token_output, back_weight)


def solution(mesh):
    split = P(BOTH, None)
    placed = (
        split, split, split, P(None, BOTH, None), P(None, "row", "col"),
        P(), P(), P(), P(), P(), P(),
    )
    return jax.shard_map(
        per_device, mesh=mesh, in_specs=placed, out_specs=(split, split), check_vma=False
    )
```

```python
import math

import jax
import jax.numpy as jnp
from jax import lax
from jax.experimental import pallas as pl
from jax.experimental.pallas import tpu as pltpu
from jax.sharding import PartitionSpec as P

HEADS = 16
HEAD_DIM = 48
SLOT = 64
PAIRS = HEADS // 2
ATOM_HEADS = 4
WIN_Q = 32
WIN_K = 128
REACH = 48
EPSILON = 1e-05

BOTH = ("row", "col")
F32 = jnp.float32
BF16 = jnp.bfloat16
ATOM_MB = 20
MOST = 47
SMALL = (1_000_000, 100_000)
ORDER = (2, 3, 0, 1, 6, 7, 4, 5)


def dot(a, b, contract=((1,), (0,))):
    return lax.dot_general(a, b, (contract, ((), ())), preferred_element_type=F32)


def layer_norm(values):
    centred = values - jnp.mean(values, axis=-1, keepdims=True)
    spread = jnp.mean(centred * centred, axis=-1, keepdims=True)
    return centred * lax.rsqrt(spread + EPSILON)


def lanes(shape, axis):
    return lax.broadcasted_iota(jnp.int32, shape, axis)


BAND = 2 * 2 * SLOT
STARTS = (0, 128, 384, 512)


def band_place(group, back=False):
    near = lanes((BAND, BAND), 1 if back else 0) + STARTS[group]
    far = lanes((BAND, BAND), 0 if back else 1) + group * BAND
    return ((near // HEAD_DIM == far // SLOT) & (near % HEAD_DIM == far % SLOT)).astype(BF16)


def spread(values):
    return [
        dot(values[:, STARTS[g] : STARTS[g] + BAND], band_place(g)) for g in range(HEADS // 4)
    ]


def gather_lanes(values):
    parts = [dot(values[g], band_place(g, True)) for g in range(HEADS // 4)]
    lane = 2 * SLOT
    return jnp.concatenate(
        [
            parts[0][:, :lane],
            parts[0][:, lane:] + parts[1][:, :lane],
            parts[1][:, lane:],
            parts[2][:, :lane],
            parts[2][:, lane:] + parts[3][:, :lane],
            parts[3][:, lane:],
        ],
        axis=1,
    )


def store_pairs(ref, bands):
    lane = 2 * SLOT
    for g, band in enumerate(bands):
        ref[2 * g] = band[:, :lane].astype(BF16)
        ref[2 * g + 1] = band[:, lane:].astype(BF16)


def atom_step(
    left_ref, right_ref, narrow_ref, broad_ref, owner_ref, mid_ref, single_ref, norm_ref,
):
    width = narrow_ref.shape[1]
    count = owner_ref.shape[1]
    state_ref = narrow_ref.at[:count]
    after = (1 + ATOM_HEADS) * count
    bias_ref = [narrow_ref.at[(1 + h) * count : (2 + h) * count] for h in range(ATOM_HEADS)]
    proj_ref = [narrow_ref.at[after + i * width : after + (i + 1) * width] for i in range(5)]
    output_ref = proj_ref[4]
    pool_ref, input_ref = broad_ref.at[:width], broad_ref.at[width:]
    windows = count // WIN_Q
    rows, cols = lax.axis_size("row"), lax.axis_size("col")
    first = (lax.axis_index("row") * cols + lax.axis_index("col")) * count
    total = count * rows * cols
    state = state_ref[...].astype(F32)
    extended = jnp.concatenate(
        [left_ref[...].astype(F32), state, right_ref[...].astype(F32)], axis=0
    )
    normed = layer_norm(extended).astype(BF16)
    keys = dot(normed, proj_ref[1][...]).astype(BF16)
    values = dot(normed, proj_ref[2][...]).astype(BF16)
    own = normed[REACH : REACH + count]
    queries = dot(own, proj_ref[0][...]).astype(BF16)
    gates = jax.nn.sigmoid(dot(own, proj_ref[3][...]))
    head_width = width // ATOM_HEADS
    head_of = lanes((WIN_Q, width), 1) // head_width
    factor = 1.0 / math.sqrt(head_width)
    gated = []
    for w in range(windows):
        start = w * WIN_Q
        query = queries[start : start + WIN_Q]
        stacked = jnp.concatenate(
            [jnp.where(head_of == h, query, jnp.zeros_like(query)) for h in range(ATOM_HEADS)],
            axis=0,
        )
        scores = dot(stacked, keys[start : start + WIN_K], ((1,), (1,))) * factor
        scores = scores + jnp.concatenate(
            [bias_ref[h][start : start + WIN_Q, :] for h in range(ATOM_HEADS)], axis=0
        ).astype(F32)
        if start < REACH or start + WIN_K > count + REACH:
            position = first + (start - REACH) + lanes(scores.shape, 1)
            scores = jnp.where((position >= 0) & (position < total), scores, -1e30)
        top = jnp.max(scores, axis=-1, keepdims=True)
        weights = jnp.exp(scores - top)
        weights = (weights / jnp.sum(weights, axis=-1, keepdims=True)).astype(BF16)
        mixed = dot(weights, values[start : start + WIN_K])
        mix = jnp.zeros((WIN_Q, width), F32)
        for h in range(ATOM_HEADS):
            mix = jnp.where(head_of == h, mixed[h * WIN_Q : (h + 1) * WIN_Q], mix)
        gated.append((mix * gates[start : start + WIN_Q]).astype(BF16))
    gated = jnp.concatenate(gated, axis=0)
    mid = state + dot(gated, output_ref[...])
    mid_ref[...] = mid
    lifted = jnp.maximum(dot(mid.astype(BF16), pool_ref[...]), 0.0).astype(BF16)
    tokens = input_ref.shape[0]
    owned = (lanes((tokens, count), 0) == owner_ref[...]).astype(F32)
    counts = jnp.sum(owned, axis=1, keepdims=True)
    pooled = dot(owned.astype(BF16), lifted)
    single = input_ref[...].astype(F32) + pooled / counts
    single_ref[...] = single
    norm_ref[...] = layer_norm(single).astype(BF16)


def query_rows(parts, weight, q_ref):
    tokens = parts[0].shape[0] // 2
    lane = 2 * SLOT
    bands = spread(dot(jnp.concatenate(parts, axis=0), weight).astype(BF16))
    ring = lax.axis_size("col") // 2
    me = lax.axis_index("col")
    high, low = me // ring, me % ring
    for i, step in enumerate((0, ring - 1, 1, 2)):
        for j in range(2):
            source = lax.rem(high + j, 2) * ring + lax.rem(low + step, ring)
            at = pl.ds(pl.multiple_of(source * tokens, 16), tokens)
            first = (2 * i + j) * tokens
            for g, band in enumerate(bands):
                block = band[first : first + tokens].astype(BF16)
                q_ref[2 * g, at, :] = block[:, :lane]
                q_ref[2 * g + 1, at, :] = block[:, lane:]


def key_rows(blocks_ref, weight, k_ref):
    rows = jnp.concatenate([blocks_ref[i] for i in ORDER], axis=0)
    store_pairs(k_ref, spread(dot(rows, weight).astype(BF16)))


def value_rows(blocks_ref, weight, v_ref):
    rows = jnp.concatenate([blocks_ref[i] for i in ORDER], axis=0)
    mass = lanes((1, BAND), 1) % SLOT == HEAD_DIM
    bands = spread(dot(rows, weight).astype(BF16))
    store_pairs(v_ref, [jnp.where(mass, 1.0, band) for band in bands])


def project_step(
    own_ref, after_ref, before_ref, far_ref, norm_ref, blocks_ref, proj_hbm, q_ref, gate_ref,
    k_ref, v_ref, key_ref, edge_ref, sems,
):
    targets = (edge_ref.at[0], key_ref.at[0], key_ref.at[1], edge_ref.at[1])
    copies = [
        pltpu.make_async_copy(proj_hbm.at[i], target, sems.at[i])
        for i, target in enumerate(targets)
    ]
    for copy in copies:
        copy.start()
    copies[0].wait()
    query_rows(
        [own_ref[...], after_ref[...], before_ref[...], far_ref[...]], edge_ref[0], q_ref
    )
    copies[1].wait()
    key_rows(blocks_ref, key_ref[0], k_ref)
    copies[2].wait()
    value_rows(blocks_ref, key_ref[1], v_ref)
    copies[3].wait()
    gates = jax.nn.sigmoid(dot(norm_ref[...], edge_ref[1]))
    top = gates.astype(BF16)
    rest = (gates - top.astype(F32)).astype(BF16)
    for g, (a, b) in enumerate(zip(spread(top), spread(rest))):
        gate_ref[:, g * BAND : (g + 1) * BAND] = a + b


def token_step(
    q_ref, k_ref, v_ref, blocks_ref, proj_ref, bias_hbm, part_ref, bias_ref, other_k, other_v, sems
):
    lane = 2 * SLOT
    heads = (slice(0, 4), slice(4, HEADS))
    copies = [
        pltpu.make_async_copy(bias_hbm.at[span], bias_ref.at[span], sems.at[i])
        for i, span in enumerate(heads)
    ]
    for copy in copies:
        copy.start()
    key_rows(blocks_ref, proj_ref[0], other_k)
    value_rows(blocks_ref, proj_ref[1], other_v)
    core = lax.rem(lax.axis_index("row"), 2)
    count, half = q_ref.shape[1], k_ref.shape[1]
    mine_at = pl.ds(pl.multiple_of(core * half, lane), half)
    other_at = pl.ds(pl.multiple_of((1 - core) * half, lane), half)
    at = lanes((count, lane), 1)
    factor = 1.0 / math.sqrt(HEAD_DIM)
    for pair in range(PAIRS):
        if pair == 0:
            copies[0].wait()
        if pair == 2:
            copies[1].wait()
        query = q_ref[pair]
        key = jnp.concatenate([k_ref[pair], other_k[pair]], axis=0)
        value = jnp.concatenate([v_ref[pair], other_v[pair]], axis=0)
        both = []
        for a in range(2):
            head = 2 * pair + a
            mine = jnp.where(at // SLOT == a, query, jnp.zeros_like(query))
            bias = jnp.concatenate(
                [bias_ref[head, :, mine_at], bias_ref[head, :, other_at]], axis=1
            )
            scores = dot(mine, key, ((1,), (1,))) * factor + bias.astype(F32)
            top = jnp.max(scores, axis=-1, keepdims=True)
            both.append((dot(jnp.exp(scores - top).astype(BF16), value), top))
        result = jnp.where(at < SLOT, both[0][0], both[1][0])
        top = jnp.where(at < SLOT, both[0][1], both[1][1])
        place = at % SLOT - HEAD_DIM
        rest = result - result.astype(BF16).astype(F32)
        result = jnp.where(place == 1, pltpu.roll(rest, 1, 1), result)
        for piece in range(3):
            part = top.astype(BF16).astype(F32)
            result = jnp.where(place == 2 + piece, part, result)
            top = top - part
        part_ref[:, pair * lane : (pair + 1) * lane] = result.astype(BF16)


def last_step(
    part_ref, gate_ref, single_ref, mid_ref, owner_ref, output_ref, back_ref, atom_ref,
    token_ref,
):
    lane = 2 * SLOT
    shares, tokens, _ = part_ref.shape
    here, there = lanes((lane, lane), 0), lanes((lane, lane), 1)
    same, place = here // SLOT == there // SLOT, here % SLOT - HEAD_DIM
    mass_of = (same & (place >= 0) & (place < 2)).astype(BF16)
    top_of = (same & (place >= 2) & (place < 5)).astype(BF16)
    gated = []
    for p in range(PAIRS):
        span = slice(p * lane, (p + 1) * lane)
        parts = [part_ref[c, :, span] for c in range(shares)]
        tops = [dot(part, top_of) for part in parts]
        most = tops[0]
        for top in tops[1:]:
            most = jnp.maximum(most, top)
        mix = jnp.zeros((tokens, lane), F32)
        for part, top in zip(parts, tops):
            mix = mix + jnp.exp(top - most) * part.astype(F32)
        high = mix.astype(BF16)
        low = (mix - high.astype(F32)).astype(BF16)
        mass = dot(high, mass_of) + dot(low, mass_of)
        gated.append((mix / mass * gate_ref[:, span]).astype(BF16))
    gated = [jnp.concatenate(gated[g : g + 2], axis=1) for g in range(0, PAIRS, 2)]
    update = dot(gather_lanes(gated).astype(BF16), output_ref[...])
    token_state = (single_ref[...] + update).astype(BF16)
    token_ref[...] = token_state
    returned = dot(token_state, back_ref[...])
    high = returned.astype(BF16)
    low = (returned - high.astype(F32)).astype(BF16)
    count = mid_ref.shape[0]
    owned = (lanes((tokens, count), 0) == owner_ref[...]).astype(F32).T.astype(BF16)
    atom_ref[...] = (mid_ref[...] + dot(owned, high) + dot(owned, low)).astype(BF16)


def call(kernel, out, megabytes, cost, **more):
    flops, size = cost
    return pl.pallas_call(
        kernel,
        out_shape=out,
        compiler_params=pltpu.CompilerParams(vmem_limit_bytes=megabytes * 1024 * 1024),
        cost_estimate=pl.CostEstimate(flops=flops, bytes_accessed=size, transcendentals=0),
        **more,
    )


def shape(dims, kind):
    return jax.ShapeDtypeStruct(dims, kind)


def per_device(
    atom_state, token_input, atom_owner, atom_bias, pair_bias, atom_proj, atom_output,
    pool_weight, token_proj, token_output, back_weight,
):
    rows, cols = lax.axis_size("row"), lax.axis_size("col")
    devices = rows * cols
    count, width = atom_state.shape
    tokens, depth = token_input.shape
    wide = HEADS * SLOT
    ends = devices - 1
    left = lax.ppermute(
        atom_state[count - REACH :], BOTH, [(i, i + 1) for i in range(ends)]
    )
    right = lax.ppermute(atom_state[:REACH], BOTH, [(i + 1, i) for i in range(ends)])
    narrow = jnp.concatenate(
        [atom_state]
        + [array.reshape(-1, width) for array in (atom_bias, atom_proj, atom_output)],
        axis=0,
    )
    broad = jnp.concatenate([pool_weight, token_input], axis=0)
    mid, single, norm = call(
        atom_step,
        (
            shape((count, width), F32),
            shape((tokens, depth), F32),
            shape((tokens, depth), BF16),
        ),
        ATOM_MB,
        (400_000_000, 2_000_000),
    )(left, right, narrow, broad, atom_owner)
    ring = cols // 2
    turn = []
    for r in range(rows):
        for c in range(cols):
            to_row = (c // ring) * cols + 2 * ((c % ring + 2) % ring) + r % 2
            turn.append((r * cols + c, to_row * cols + r // 2))
    turned = lax.ppermute(norm, BOTH, turn)
    across = lax.ppermute(norm, "col", [(i, (i + ring) % cols) for i in range(cols)])
    own = jnp.concatenate([norm, across], axis=0)
    turned, own = lax.optimization_barrier((turned, own))
    same_core = [[i for i in range(rows) if i % 2 == e] for e in range(2)]
    near = lax.all_to_all(
        jnp.broadcast_to(turned[None], (rows // 2, tokens, depth)), "row", 0, 0,
        axis_index_groups=same_core,
    )
    along = [
        lax.ppermute(
            own, "col", [(i, i // ring * ring + (i + step) % ring) for i in range(cols)]
        )
        for step in (1, ring - 1, 2)
    ]
    near, *along = lax.optimization_barrier((near, *along))
    far = lax.ppermute(near, "row", [(i, i ^ 1) for i in range(rows)])
    q_count, half = cols * tokens, rows * tokens // 2
    lane = 2 * SLOT
    in_vmem, in_hbm = (pl.BlockSpec(memory_space=space) for space in (pltpu.VMEM, pltpu.HBM))
    queries, gates, near_k, near_v, key_weights = call(
        project_step,
        (
            shape((PAIRS, q_count, lane), BF16),
            shape((tokens, wide), F32),
            shape((PAIRS, half, lane), BF16),
            shape((PAIRS, half, lane), BF16),
            shape((2, depth, depth), BF16),
        ),
        MOST,
        SMALL,
        in_specs=[in_vmem] * 6 + [in_hbm],
        scratch_shapes=[pltpu.VMEM((2, depth, depth), BF16), pltpu.SemaphoreType.DMA((4,))],
    )(own, *along, norm, near, token_proj)
    parts = call(
        token_step,
        shape((q_count, wide), BF16),
        MOST,
        (6_000_000_000, 14_000_000),
        in_specs=[in_vmem] * 5 + [in_hbm],
        scratch_shapes=[
            pltpu.VMEM((HEADS, q_count, 2 * half), BF16),
            pltpu.VMEM((PAIRS, half, lane), BF16),
            pltpu.VMEM((PAIRS, half, lane), BF16),
            pltpu.SemaphoreType.DMA((2,)),
        ],
    )(queries, near_k, near_v, far, key_weights, pair_bias)
    parts = lax.all_to_all(parts.reshape(cols, tokens, wide), "col", 0, 0)
    return call(
        last_step,
        (shape((count, width), BF16), shape((tokens, depth), BF16)),
        12,
        (400_000_000, 5_000_000),
    )(parts, gates, single, mid, atom_owner, token_output, back_weight)


def solution(mesh):
    split = P(BOTH, None)
    placed = (
        split, split, split, P(None, BOTH, None), P(None, "row", "col"),
        P(), P(), P(), P(), P(), P(),
    )
    return jax.shard_map(
        per_device, mesh=mesh, in_specs=placed, out_specs=(split, split), check_vma=False
    )
```

```python
import math

import jax
import jax.numpy as jnp
from jax import lax
from jax.experimental import pallas as pl
from jax.experimental.pallas import tpu as pltpu
from jax.sharding import PartitionSpec as P

HEADS = 16
HEAD_DIM = 48
SLOT = 64
PAIRS = HEADS // 2
ATOM_HEADS = 4
WIN_Q = 32
WIN_K = 128
REACH = 48
EDGE = 2
EPSILON = 1e-05

BOTH = ("row", "col")
F32 = jnp.float32
BF16 = jnp.bfloat16
ATOM_MB = 20
MOST = 47
SMALL = (1_000_000, 100_000)
ORDER = (2, 3, 0, 1, 6, 7, 4, 5)


def dot(a, b, contract=((1,), (0,))):
    return lax.dot_general(a, b, (contract, ((), ())), preferred_element_type=F32)


def layer_norm(values):
    centred = values - jnp.mean(values, axis=-1, keepdims=True)
    spread = jnp.mean(centred * centred, axis=-1, keepdims=True)
    return centred * lax.rsqrt(spread + EPSILON)


def lanes(shape, axis):
    return lax.broadcasted_iota(jnp.int32, shape, axis)


BAND = 2 * 2 * SLOT
STARTS = (0, 128, 384, 512)


def band_place(group, back=False):
    near = lanes((BAND, BAND), 1 if back else 0) + STARTS[group]
    far = lanes((BAND, BAND), 0 if back else 1) + group * BAND
    return ((near // HEAD_DIM == far // SLOT) & (near % HEAD_DIM == far % SLOT)).astype(BF16)


def spread(values):
    return [
        dot(values[:, STARTS[g] : STARTS[g] + BAND], band_place(g)) for g in range(HEADS // 4)
    ]


def gather_lanes(values):
    parts = [dot(values[g], band_place(g, True)) for g in range(HEADS // 4)]
    lane = 2 * SLOT
    return jnp.concatenate(
        [
            parts[0][:, :lane],
            parts[0][:, lane:] + parts[1][:, :lane],
            parts[1][:, lane:],
            parts[2][:, :lane],
            parts[2][:, lane:] + parts[3][:, :lane],
            parts[3][:, lane:],
        ],
        axis=1,
    )


def store_pairs(ref, bands):
    lane = 2 * SLOT
    for g, band in enumerate(bands):
        ref[2 * g] = band[:, :lane].astype(BF16)
        ref[2 * g + 1] = band[:, lane:].astype(BF16)


def narrow_parts(narrow_ref, count):
    width = narrow_ref.shape[1]
    after = (1 + ATOM_HEADS) * count
    biases = [narrow_ref.at[(1 + h) * count : (2 + h) * count] for h in range(ATOM_HEADS)]
    weights = [narrow_ref.at[after + i * width : after + (i + 1) * width] for i in range(5)]
    return narrow_ref.at[:count], biases, weights


def window(start, query, keys, values, gates, biases, bounds=None):
    width = query.shape[1]
    head_width = width // ATOM_HEADS
    head_of = lanes((WIN_Q, width), 1) // head_width
    stacked = jnp.concatenate(
        [jnp.where(head_of == h, query, jnp.zeros_like(query)) for h in range(ATOM_HEADS)],
        axis=0,
    )
    scores = dot(stacked, keys, ((1,), (1,))) * (1.0 / math.sqrt(head_width))
    scores = scores + jnp.concatenate(
        [bias[start : start + WIN_Q, :] for bias in biases], axis=0
    ).astype(F32)
    if bounds is not None:
        first, total = bounds
        position = first + (start - REACH) + lanes(scores.shape, 1)
        scores = jnp.where((position >= 0) & (position < total), scores, -1e30)
    top = jnp.max(scores, axis=-1, keepdims=True)
    weights = jnp.exp(scores - top)
    weights = (weights / jnp.sum(weights, axis=-1, keepdims=True)).astype(BF16)
    mixed = dot(weights, values)
    mix = jnp.zeros((WIN_Q, width), F32)
    for h in range(ATOM_HEADS):
        mix = jnp.where(head_of == h, mixed[h * WIN_Q : (h + 1) * WIN_Q], mix)
    return (mix * gates).astype(BF16)


def inner_step(narrow_ref, q_ref, k_ref, v_ref, gate_ref, gated_ref):
    count = q_ref.shape[0]
    state_ref, biases, weights = narrow_parts(narrow_ref, count)
    normed = layer_norm(state_ref[...].astype(F32)).astype(BF16)
    queries = dot(normed, weights[0][...]).astype(BF16)
    keys = dot(normed, weights[1][...]).astype(BF16)
    values = dot(normed, weights[2][...]).astype(BF16)
    gates = jax.nn.sigmoid(dot(normed, weights[3][...]))
    q_ref[...], k_ref[...], v_ref[...], gate_ref[...] = queries, keys, values, gates
    for w in range(EDGE, count // WIN_Q - EDGE):
        start = w * WIN_Q
        seen = slice(start - REACH, start - REACH + WIN_K)
        mine = slice(start, start + WIN_Q)
        gated_ref[start - EDGE * WIN_Q : start - EDGE * WIN_Q + WIN_Q, :] = window(
            start, queries[mine], keys[seen], values[seen], gates[mine], biases
        )


def atom_step(
    left_ref, right_ref, narrow_ref, broad_ref, owner_ref, q_ref, k_ref, v_ref, gate_ref,
    gated_ref, mid_ref, single_ref, norm_ref,
):
    width = narrow_ref.shape[1]
    count = owner_ref.shape[1]
    state_ref, biases, weights = narrow_parts(narrow_ref, count)
    pool_ref, input_ref = broad_ref.at[:width], broad_ref.at[width:]
    rows, cols = lax.axis_size("row"), lax.axis_size("col")
    first = (lax.axis_index("row") * cols + lax.axis_index("col")) * count
    bounds = (first, count * rows * cols)
    beside = jnp.concatenate([left_ref[...], right_ref[...]], axis=0).astype(F32)
    normed = layer_norm(beside).astype(BF16)
    keys = dot(normed, weights[1][...]).astype(BF16)
    values = dot(normed, weights[2][...]).astype(BF16)
    reach = WIN_K + WIN_Q - REACH
    ends = (
        (jnp.concatenate([keys[:REACH], k_ref[:reach, :]], axis=0),
         jnp.concatenate([values[:REACH], v_ref[:reach, :]], axis=0)),
        (jnp.concatenate([k_ref[count - reach :, :], keys[REACH:]], axis=0),
         jnp.concatenate([v_ref[count - reach :, :], values[REACH:]], axis=0)),
    )
    outer = []
    for side in range(2):
        for w in range(EDGE):
            start = w * WIN_Q + side * (count - EDGE * WIN_Q)
            mine = slice(start, start + WIN_Q)
            seen = slice(w * WIN_Q, w * WIN_Q + WIN_K)
            outer.append(
                window(
                    start, q_ref[mine, :], ends[side][0][seen], ends[side][1][seen],
                    gate_ref[mine, :], biases, bounds,
                )
            )
    gated = jnp.concatenate(outer[:EDGE] + [gated_ref[...]] + outer[EDGE:], axis=0)
    mid = state_ref[...].astype(F32) + dot(gated, weights[4][...])
    mid_ref[...] = mid
    lifted = jnp.maximum(dot(mid.astype(BF16), pool_ref[...]), 0.0).astype(BF16)
    tokens = input_ref.shape[0]
    owned = (lanes((tokens, count), 0) == owner_ref[...]).astype(F32)
    counts = jnp.sum(owned, axis=1, keepdims=True)
    pooled = dot(owned.astype(BF16), lifted)
    single = input_ref[...].astype(F32) + pooled / counts
    single_ref[...] = single
    norm_ref[...] = layer_norm(single).astype(BF16)


def query_rows(parts, weight, q_ref):
    tokens = parts[0].shape[0] // 2
    lane = 2 * SLOT
    bands = spread(dot(jnp.concatenate(parts, axis=0), weight).astype(BF16))
    ring = lax.axis_size("col") // 2
    me = lax.axis_index("col")
    high, low = me // ring, me % ring
    for i, step in enumerate((0, ring - 1, 1, 2)):
        for j in range(2):
            source = lax.rem(high + j, 2) * ring + lax.rem(low + step, ring)
            at = pl.ds(pl.multiple_of(source * tokens, 16), tokens)
            first = (2 * i + j) * tokens
            for g, band in enumerate(bands):
                block = band[first : first + tokens].astype(BF16)
                q_ref[2 * g, at, :] = block[:, :lane]
                q_ref[2 * g + 1, at, :] = block[:, lane:]


def key_rows(blocks_ref, weight, k_ref):
    rows = jnp.concatenate([blocks_ref[i] for i in ORDER], axis=0)
    store_pairs(k_ref, spread(dot(rows, weight).astype(BF16)))


def value_rows(blocks_ref, weight, v_ref):
    rows = jnp.concatenate([blocks_ref[i] for i in ORDER], axis=0)
    mass = lanes((1, BAND), 1) % SLOT == HEAD_DIM
    bands = spread(dot(rows, weight).astype(BF16))
    store_pairs(v_ref, [jnp.where(mass, 1.0, band) for band in bands])


def project_step(
    own_ref, after_ref, before_ref, far_ref, norm_ref, blocks_ref, proj_hbm, q_ref, gate_ref,
    k_ref, v_ref, key_ref, edge_ref, sems,
):
    targets = (edge_ref.at[0], key_ref.at[0], key_ref.at[1], edge_ref.at[1])
    copies = [
        pltpu.make_async_copy(proj_hbm.at[i], target, sems.at[i])
        for i, target in enumerate(targets)
    ]
    for copy in copies:
        copy.start()
    copies[0].wait()
    query_rows(
        [own_ref[...], after_ref[...], before_ref[...], far_ref[...]], edge_ref[0], q_ref
    )
    copies[1].wait()
    key_rows(blocks_ref, key_ref[0], k_ref)
    copies[2].wait()
    value_rows(blocks_ref, key_ref[1], v_ref)
    copies[3].wait()
    gates = jax.nn.sigmoid(dot(norm_ref[...], edge_ref[1]))
    top = gates.astype(BF16)
    rest = (gates - top.astype(F32)).astype(BF16)
    for g, (a, b) in enumerate(zip(spread(top), spread(rest))):
        gate_ref[:, g * BAND : (g + 1) * BAND] = a + b


def token_step(
    q_ref, k_ref, v_ref, blocks_ref, proj_ref, bias_hbm, part_ref, bias_ref, other_k, other_v, sems
):
    lane = 2 * SLOT
    heads = (slice(0, 4), slice(4, HEADS))
    copies = [
        pltpu.make_async_copy(bias_hbm.at[span], bias_ref.at[span], sems.at[i])
        for i, span in enumerate(heads)
    ]
    for copy in copies:
        copy.start()
    key_rows(blocks_ref, proj_ref[0], other_k)
    value_rows(blocks_ref, proj_ref[1], other_v)
    core = lax.rem(lax.axis_index("row"), 2)
    count, half = q_ref.shape[1], k_ref.shape[1]
    mine_at = pl.ds(pl.multiple_of(core * half, lane), half)
    other_at = pl.ds(pl.multiple_of((1 - core) * half, lane), half)
    at = lanes((count, lane), 1)
    factor = 1.0 / math.sqrt(HEAD_DIM)
    for pair in range(PAIRS):
        if pair == 0:
            copies[0].wait()
        if pair == 2:
            copies[1].wait()
        query = q_ref[pair]
        key = jnp.concatenate([k_ref[pair], other_k[pair]], axis=0)
        value = jnp.concatenate([v_ref[pair], other_v[pair]], axis=0)
        both = []
        for a in range(2):
            head = 2 * pair + a
            mine = jnp.where(at // SLOT == a, query, jnp.zeros_like(query))
            bias = jnp.concatenate(
                [bias_ref[head, :, mine_at], bias_ref[head, :, other_at]], axis=1
            )
            scores = dot(mine, key, ((1,), (1,))) * factor + bias.astype(F32)
            top = jnp.max(scores, axis=-1, keepdims=True)
            both.append((dot(jnp.exp(scores - top).astype(BF16), value), top))
        result = jnp.where(at < SLOT, both[0][0], both[1][0])
        top = jnp.where(at < SLOT, both[0][1], both[1][1])
        place = at % SLOT - HEAD_DIM
        rest = result - result.astype(BF16).astype(F32)
        result = jnp.where(place == 1, pltpu.roll(rest, 1, 1), result)
        for piece in range(3):
            part = top.astype(BF16).astype(F32)
            result = jnp.where(place == 2 + piece, part, result)
            top = top - part
        part_ref[:, pair * lane : (pair + 1) * lane] = result.astype(BF16)


def last_step(
    part_ref, gate_ref, single_ref, mid_ref, owner_ref, output_ref, back_ref, atom_ref,
    token_ref,
):
    shares, tokens, _ = part_ref.shape
    here, there = lanes((BAND, BAND), 0), lanes((BAND, BAND), 1)
    same, place = here // SLOT == there // SLOT, here % SLOT - HEAD_DIM
    mass_of = (same & (place >= 0) & (place < 2)).astype(BF16)
    top_of = (same & (place >= 2) & (place < 5)).astype(BF16)
    gated = []
    for g in range(HEADS // 4):
        span = slice(g * BAND, (g + 1) * BAND)
        parts = jnp.concatenate([part_ref[c, :, span] for c in range(shares)], axis=0)
        tops = dot(parts, top_of).reshape(shares, tokens, BAND)
        weights = jnp.exp(tops - jnp.max(tops, axis=0))
        mix = jnp.sum(weights * parts.astype(F32).reshape(tops.shape), axis=0)
        high = mix.astype(BF16)
        low = (mix - high.astype(F32)).astype(BF16)
        mass = dot(high, mass_of) + dot(low, mass_of)
        gated.append((mix / mass * gate_ref[:, span]).astype(BF16))
    update = dot(gather_lanes(gated).astype(BF16), output_ref[...])
    token_state = (single_ref[...] + update).astype(BF16)
    token_ref[...] = token_state
    returned = dot(token_state, back_ref[...])
    high = returned.astype(BF16)
    low = (returned - high.astype(F32)).astype(BF16)
    count = mid_ref.shape[0]
    owned = (lanes((tokens, count), 0) == owner_ref[...]).astype(F32).T.astype(BF16)
    atom_ref[...] = (mid_ref[...] + dot(owned, high) + dot(owned, low)).astype(BF16)


def call(kernel, out, megabytes, cost, **more):
    flops, size = cost
    return pl.pallas_call(
        kernel,
        out_shape=out,
        compiler_params=pltpu.CompilerParams(vmem_limit_bytes=megabytes * 1024 * 1024),
        cost_estimate=pl.CostEstimate(flops=flops, bytes_accessed=size, transcendentals=0),
        **more,
    )


def shape(dims, kind):
    return jax.ShapeDtypeStruct(dims, kind)


def per_device(
    atom_state, token_input, atom_owner, atom_bias, pair_bias, atom_proj, atom_output,
    pool_weight, token_proj, token_output, back_weight,
):
    rows, cols = lax.axis_size("row"), lax.axis_size("col")
    devices = rows * cols
    count, width = atom_state.shape
    tokens, depth = token_input.shape
    wide = HEADS * SLOT
    ends = devices - 1
    left = lax.ppermute(
        atom_state[count - REACH :], BOTH, [(i, i + 1) for i in range(ends)]
    )
    right = lax.ppermute(atom_state[:REACH], BOTH, [(i + 1, i) for i in range(ends)])
    narrow = jnp.concatenate(
        [atom_state]
        + [array.reshape(-1, width) for array in (atom_bias, atom_proj, atom_output)],
        axis=0,
    )
    broad = jnp.concatenate([pool_weight, token_input], axis=0)
    inner = call(
        inner_step,
        tuple(shape((count, width), kind) for kind in (BF16, BF16, BF16, F32))
        + (shape((count - 2 * EDGE * WIN_Q, width), BF16),),
        ATOM_MB,
        (200_000_000, 1_000_000),
    )(narrow)
    mid, single, norm = call(
        atom_step,
        (
            shape((count, width), F32),
            shape((tokens, depth), F32),
            shape((tokens, depth), BF16),
        ),
        ATOM_MB,
        (200_000_000, 2_000_000),
    )(left, right, narrow, broad, atom_owner, *inner)
    ring = cols // 2
    turn = []
    for r in range(rows):
        for c in range(cols):
            to_row = (c // ring) * cols + 2 * ((c % ring + 2) % ring) + r % 2
            turn.append((r * cols + c, to_row * cols + r // 2))
    turned = lax.ppermute(norm, BOTH, turn)
    across = lax.ppermute(norm, "col", [(i, (i + ring) % cols) for i in range(cols)])
    own = jnp.concatenate([norm, across], axis=0)
    turned, own = lax.optimization_barrier((turned, own))
    same_core = [[i for i in range(rows) if i % 2 == e] for e in range(2)]
    near = lax.all_to_all(
        jnp.broadcast_to(turned[None], (rows // 2, tokens, depth)), "row", 0, 0,
        axis_index_groups=same_core,
    )
    along = [
        lax.ppermute(
            own, "col", [(i, i // ring * ring + (i + step) % ring) for i in range(cols)]
        )
        for step in (1, ring - 1, 2)
    ]
    near, *along = lax.optimization_barrier((near, *along))
    far = lax.ppermute(near, "row", [(i, i ^ 1) for i in range(rows)])
    q_count, half = cols * tokens, rows * tokens // 2
    lane = 2 * SLOT
    in_vmem, in_hbm = (pl.BlockSpec(memory_space=space) for space in (pltpu.VMEM, pltpu.HBM))
    queries, gates, near_k, near_v, key_weights = call(
        project_step,
        (
            shape((PAIRS, q_count, lane), BF16),
            shape((tokens, wide), F32),
            shape((PAIRS, half, lane), BF16),
            shape((PAIRS, half, lane), BF16),
            shape((2, depth, depth), BF16),
        ),
        MOST,
        SMALL,
        in_specs=[in_vmem] * 6 + [in_hbm],
        scratch_shapes=[pltpu.VMEM((2, depth, depth), BF16), pltpu.SemaphoreType.DMA((4,))],
    )(own, *along, norm, near, token_proj)
    parts = call(
        token_step,
        shape((q_count, wide), BF16),
        MOST,
        (6_000_000_000, 14_000_000),
        in_specs=[in_vmem] * 5 + [in_hbm],
        scratch_shapes=[
            pltpu.VMEM((HEADS, q_count, 2 * half), BF16),
            pltpu.VMEM((PAIRS, half, lane), BF16),
            pltpu.VMEM((PAIRS, half, lane), BF16),
            pltpu.SemaphoreType.DMA((2,)),
        ],
    )(queries, near_k, near_v, far, key_weights, pair_bias)
    parts = lax.all_to_all(parts.reshape(cols, tokens, wide), "col", 0, 0)
    return call(
        last_step,
        (shape((count, width), BF16), shape((tokens, depth), BF16)),
        12,
        (400_000_000, 5_000_000),
    )(parts, gates, single, mid, atom_owner, token_output, back_weight)


def solution(mesh):
    split = P(BOTH, None)
    placed = (
        split, split, split, P(None, BOTH, None), P(None, "row", "col"),
        P(), P(), P(), P(), P(), P(),
    )
    return jax.shard_map(
        per_device, mesh=mesh, in_specs=placed, out_specs=(split, split), check_vma=False
    )
```

```python
import math

import jax
import jax.numpy as jnp
from jax import lax
from jax.experimental import pallas as pl
from jax.experimental.pallas import tpu as pltpu
from jax.sharding import PartitionSpec as P

HEADS = 16
HEAD_DIM = 48
SLOT = 64
PAIRS = HEADS // 2
ATOM_HEADS = 4
WIN_Q = 32
WIN_K = 128
REACH = 48
EDGE = 2
EPSILON = 1e-05

BOTH = ("row", "col")
F32 = jnp.float32
BF16 = jnp.bfloat16
ATOM_MB = 20
MOST = 47
SMALL = (1_000_000, 100_000)
ORDER = (2, 3, 0, 1, 6, 7, 4, 5)


def dot(a, b, contract=((1,), (0,))):
    return lax.dot_general(a, b, (contract, ((), ())), preferred_element_type=F32)


def layer_norm(values):
    centred = values - jnp.mean(values, axis=-1, keepdims=True)
    spread = jnp.mean(centred * centred, axis=-1, keepdims=True)
    return centred * lax.rsqrt(spread + EPSILON)


def lanes(shape, axis):
    return lax.broadcasted_iota(jnp.int32, shape, axis)


BAND = 2 * 2 * SLOT
STARTS = (0, 128, 384, 512)


def band_place(group, back=False):
    far = lanes((BAND, 1) if back else (1, BAND), 0 if back else 1) + group * BAND
    within = far & (SLOT - 1)
    source = (far >> 6) * HEAD_DIM + within - STARTS[group]
    source = jnp.where(within < HEAD_DIM, source, -1)
    return (lanes((BAND, BAND), 1 if back else 0) == source).astype(BF16)


def level_place(first, amount):
    here, there = lanes((BAND, 1), 0), lanes((1, BAND), 1)
    within = (here & (SLOT - 1)) - HEAD_DIM - first
    head = jnp.where((within >= 0) & (within < amount), here >> 6, -1)
    return (head == there >> 6).astype(BF16)


def places(back=False):
    return [band_place(g, back) for g in range(HEADS // 4)]


def spread(values, into):
    return [
        dot(values[:, STARTS[g] : STARTS[g] + BAND], into[g]) for g in range(HEADS // 4)
    ]


def gather_lanes(values):
    parts = [dot(values[g], place) for g, place in enumerate(places(True))]
    lane = 2 * SLOT
    return jnp.concatenate(
        [
            parts[0][:, :lane],
            parts[0][:, lane:] + parts[1][:, :lane],
            parts[1][:, lane:],
            parts[2][:, :lane],
            parts[2][:, lane:] + parts[3][:, :lane],
            parts[3][:, lane:],
        ],
        axis=1,
    )


def store_pairs(ref, bands):
    lane = 2 * SLOT
    for g, band in enumerate(bands):
        ref[2 * g] = band[:, :lane].astype(BF16)
        ref[2 * g + 1] = band[:, lane:].astype(BF16)


def narrow_parts(narrow_ref, count):
    width = narrow_ref.shape[1]
    after = (1 + ATOM_HEADS) * count
    biases = [narrow_ref.at[(1 + h) * count : (2 + h) * count] for h in range(ATOM_HEADS)]
    weights = [narrow_ref.at[after + i * width : after + (i + 1) * width] for i in range(5)]
    return narrow_ref.at[:count], biases, weights


def window(start, query, keys, values, gates, biases, bounds=None):
    width = query.shape[1]
    head_width = width // ATOM_HEADS
    head_of = lanes((1, width), 1) >> 5
    masks = [(head_of == h).astype(F32) for h in range(ATOM_HEADS)]
    stacked = jnp.concatenate([query * mask.astype(BF16) for mask in masks], axis=0)
    scores = dot(stacked, keys, ((1,), (1,))) * (1.0 / math.sqrt(head_width))
    scores = scores + jnp.concatenate(
        [bias[start : start + WIN_Q, :] for bias in biases], axis=0
    ).astype(F32)
    if bounds is not None:
        first, total = bounds
        position = first + (start - REACH) + lanes(scores.shape, 1)
        scores = jnp.where((position >= 0) & (position < total), scores, -1e30)
    top = jnp.max(scores, axis=-1, keepdims=True)
    weights = jnp.exp(scores - top)
    weights = (weights / jnp.sum(weights, axis=-1, keepdims=True)).astype(BF16)
    mixed = dot(weights, values)
    mix = jnp.zeros((WIN_Q, width), F32)
    for h in range(ATOM_HEADS):
        mix = mix + mixed[h * WIN_Q : (h + 1) * WIN_Q] * masks[h]
    return (mix * gates).astype(BF16)


def inner_step(narrow_ref, q_ref, k_ref, v_ref, gate_ref, gated_ref):
    count = q_ref.shape[0]
    state_ref, biases, weights = narrow_parts(narrow_ref, count)
    normed = layer_norm(state_ref[...].astype(F32)).astype(BF16)
    queries = dot(normed, weights[0][...]).astype(BF16)
    keys = dot(normed, weights[1][...]).astype(BF16)
    values = dot(normed, weights[2][...]).astype(BF16)
    gates = jax.nn.sigmoid(dot(normed, weights[3][...]))
    q_ref[...], k_ref[...], v_ref[...], gate_ref[...] = queries, keys, values, gates
    for w in range(EDGE, count // WIN_Q - EDGE):
        start = w * WIN_Q
        seen = slice(start - REACH, start - REACH + WIN_K)
        mine = slice(start, start + WIN_Q)
        gated_ref[start - EDGE * WIN_Q : start - EDGE * WIN_Q + WIN_Q, :] = window(
            start, queries[mine], keys[seen], values[seen], gates[mine], biases
        )


def atom_step(
    left_ref, right_ref, narrow_ref, pool_ref, input_ref, owner_ref, q_ref, k_ref, v_ref,
    gate_ref, gated_ref, mid_ref, single_ref, norm_ref,
):
    count = owner_ref.shape[1]
    state_ref, biases, weights = narrow_parts(narrow_ref, count)
    rows, cols = lax.axis_size("row"), lax.axis_size("col")
    first = (lax.axis_index("row") * cols + lax.axis_index("col")) * count
    bounds = (first, count * rows * cols)
    beside = jnp.concatenate([left_ref[...], right_ref[...]], axis=0).astype(F32)
    normed = layer_norm(beside).astype(BF16)
    keys = dot(normed, weights[1][...]).astype(BF16)
    values = dot(normed, weights[2][...]).astype(BF16)
    reach = WIN_K + WIN_Q - REACH
    ends = (
        (jnp.concatenate([keys[:REACH], k_ref[:reach, :]], axis=0),
         jnp.concatenate([values[:REACH], v_ref[:reach, :]], axis=0)),
        (jnp.concatenate([k_ref[count - reach :, :], keys[REACH:]], axis=0),
         jnp.concatenate([v_ref[count - reach :, :], values[REACH:]], axis=0)),
    )
    outer = []
    for side in range(2):
        for w in range(EDGE):
            start = w * WIN_Q + side * (count - EDGE * WIN_Q)
            mine = slice(start, start + WIN_Q)
            seen = slice(w * WIN_Q, w * WIN_Q + WIN_K)
            outer.append(
                window(
                    start, q_ref[mine, :], ends[side][0][seen], ends[side][1][seen],
                    gate_ref[mine, :], biases, bounds,
                )
            )
    gated = jnp.concatenate(outer[:EDGE] + [gated_ref[...]] + outer[EDGE:], axis=0)
    mid = state_ref[...].astype(F32) + dot(gated, weights[4][...])
    mid_ref[...] = mid
    lifted = jnp.maximum(dot(mid.astype(BF16), pool_ref[...]), 0.0).astype(BF16)
    tokens = input_ref.shape[0]
    owned = (lanes((tokens, count), 0) == owner_ref[...]).astype(F32)
    counts = jnp.sum(owned, axis=1, keepdims=True)
    pooled = dot(owned.astype(BF16), lifted)
    single = input_ref[...].astype(F32) + pooled / counts
    single_ref[...] = single
    norm_ref[...] = layer_norm(single).astype(BF16)


def query_rows(parts, weight, into, q_ref):
    tokens = parts[0].shape[0] // 2
    lane = 2 * SLOT
    bands = spread(dot(jnp.concatenate(parts, axis=0), weight).astype(BF16), into)
    ring = lax.axis_size("col") // 2
    me = lax.axis_index("col")
    high, low = me // ring, me % ring
    for i, step in enumerate((0, ring - 1, 1, 2)):
        for j in range(2):
            source = lax.rem(high + j, 2) * ring + lax.rem(low + step, ring)
            at = pl.ds(pl.multiple_of(source * tokens, 16), tokens)
            first = (2 * i + j) * tokens
            for g, band in enumerate(bands):
                block = band[first : first + tokens].astype(BF16)
                q_ref[2 * g, at, :] = block[:, :lane]
                q_ref[2 * g + 1, at, :] = block[:, lane:]


def key_rows(blocks_ref, weight, into, k_ref):
    rows = jnp.concatenate([blocks_ref[i] for i in ORDER], axis=0)
    store_pairs(k_ref, spread(dot(rows, weight).astype(BF16), into))


def value_rows(blocks_ref, weight, into, v_ref):
    rows = jnp.concatenate([blocks_ref[i] for i in ORDER], axis=0)
    mass = (lanes((1, BAND), 1) & (SLOT - 1)) == HEAD_DIM
    bands = spread(dot(rows, weight).astype(BF16), into)
    store_pairs(v_ref, [jnp.where(mass, 1.0, band) for band in bands])


def project_step(
    own_ref, after_ref, before_ref, far_ref, norm_ref, blocks_ref, proj_hbm, q_ref, gate_ref,
    k_ref, v_ref, key_ref, edge_ref, sems,
):
    targets = (edge_ref.at[0], key_ref.at[0], key_ref.at[1], edge_ref.at[1])
    copies = [
        pltpu.make_async_copy(proj_hbm.at[i], target, sems.at[i])
        for i, target in enumerate(targets)
    ]
    for copy in copies:
        copy.start()
    into = places()
    copies[0].wait()
    query_rows(
        [own_ref[...], after_ref[...], before_ref[...], far_ref[...]], edge_ref[0], into, q_ref
    )
    copies[1].wait()
    key_rows(blocks_ref, key_ref[0], into, k_ref)
    copies[2].wait()
    value_rows(blocks_ref, key_ref[1], into, v_ref)
    copies[3].wait()
    gates = jax.nn.sigmoid(dot(norm_ref[...], edge_ref[1]))
    top = gates.astype(BF16)
    rest = (gates - top.astype(F32)).astype(BF16)
    for g, (a, b) in enumerate(zip(spread(top, into), spread(rest, into))):
        gate_ref[:, g * BAND : (g + 1) * BAND] = a + b


def token_step(
    q_ref, k_ref, v_ref, blocks_ref, proj_ref, bias_hbm, part_ref, bias_ref, other_k, other_v, sems
):
    lane = 2 * SLOT
    heads = (slice(0, 4), slice(4, HEADS))
    copies = [
        pltpu.make_async_copy(bias_hbm.at[span], bias_ref.at[span], sems.at[i])
        for i, span in enumerate(heads)
    ]
    for copy in copies:
        copy.start()
    into = places()
    key_rows(blocks_ref, proj_ref[0], into, other_k)
    value_rows(blocks_ref, proj_ref[1], into, other_v)
    core = lax.rem(lax.axis_index("row"), 2)
    count, half = q_ref.shape[1], k_ref.shape[1]
    mine_at = pl.ds(pl.multiple_of(core * half, lane), half)
    other_at = pl.ds(pl.multiple_of((1 - core) * half, lane), half)
    at = lanes((count, lane), 1)
    first_head = at < SLOT
    spare = (at & (SLOT - 1)) - HEAD_DIM
    spares = [spare == i for i in range(5)]
    row = lanes((1, lane), 1)
    masks = [(row < SLOT).astype(BF16), (row >= SLOT).astype(BF16)]
    factor = 1.0 / math.sqrt(HEAD_DIM)
    for pair in range(PAIRS):
        if pair == 0:
            copies[0].wait()
        if pair == 2:
            copies[1].wait()
        query = q_ref[pair]
        key = jnp.concatenate([k_ref[pair], other_k[pair]], axis=0)
        value = jnp.concatenate([v_ref[pair], other_v[pair]], axis=0)
        both = []
        for a in range(2):
            head = 2 * pair + a
            mine = query * masks[a]
            bias = jnp.concatenate(
                [bias_ref[head, :, mine_at], bias_ref[head, :, other_at]], axis=1
            )
            scores = dot(mine, key, ((1,), (1,))) * factor + bias.astype(F32)
            top = jnp.max(scores, axis=-1, keepdims=True)
            both.append((dot(jnp.exp(scores - top).astype(BF16), value), top))
        result = jnp.where(first_head, both[0][0], both[1][0])
        top = jnp.where(first_head, both[0][1], both[1][1])
        rest = result - result.astype(BF16).astype(F32)
        result = jnp.where(spares[1], pltpu.roll(rest, 1, 1), result)
        for piece in range(3):
            part = top.astype(BF16).astype(F32)
            result = jnp.where(spares[2 + piece], part, result)
            top = top - part
        part_ref[:, pair * lane : (pair + 1) * lane] = result.astype(BF16)


def last_step(
    part_ref, gate_ref, single_ref, mid_ref, owner_ref, output_ref, back_ref, atom_ref,
    token_ref,
):
    shares, tokens, _ = part_ref.shape
    mass_of, top_of = level_place(0, 2), level_place(2, 3)
    gated = []
    for g in range(HEADS // 4):
        span = slice(g * BAND, (g + 1) * BAND)
        parts = jnp.concatenate([part_ref[c, :, span] for c in range(shares)], axis=0)
        tops = dot(parts, top_of).reshape(shares, tokens, BAND)
        weights = jnp.exp(tops - jnp.max(tops, axis=0))
        mix = jnp.sum(weights * parts.astype(F32).reshape(tops.shape), axis=0)
        high = mix.astype(BF16)
        low = (mix - high.astype(F32)).astype(BF16)
        mass = dot(high, mass_of) + dot(low, mass_of)
        gated.append((mix / mass * gate_ref[:, span]).astype(BF16))
    update = dot(gather_lanes(gated).astype(BF16), output_ref[...])
    token_state = (single_ref[...] + update).astype(BF16)
    token_ref[...] = token_state
    returned = dot(token_state, back_ref[...])
    high = returned.astype(BF16)
    low = (returned - high.astype(F32)).astype(BF16)
    count = mid_ref.shape[0]
    owned = (lanes((tokens, count), 0) == owner_ref[...]).astype(F32).T.astype(BF16)
    atom_ref[...] = (mid_ref[...] + dot(owned, high) + dot(owned, low)).astype(BF16)


def call(kernel, out, megabytes, cost, **more):
    flops, size = cost
    return pl.pallas_call(
        kernel,
        out_shape=out,
        compiler_params=pltpu.CompilerParams(vmem_limit_bytes=megabytes * 1024 * 1024),
        cost_estimate=pl.CostEstimate(flops=flops, bytes_accessed=size, transcendentals=0),
        **more,
    )


def shape(dims, kind):
    return jax.ShapeDtypeStruct(dims, kind)


def per_device(
    atom_state, token_input, atom_owner, atom_bias, pair_bias, atom_proj, atom_output,
    pool_weight, token_proj, token_output, back_weight,
):
    rows, cols = lax.axis_size("row"), lax.axis_size("col")
    devices = rows * cols
    count, width = atom_state.shape
    tokens, depth = token_input.shape
    wide = HEADS * SLOT
    ends = devices - 1
    left = lax.ppermute(
        atom_state[count - REACH :], BOTH, [(i, i + 1) for i in range(ends)]
    )
    right = lax.ppermute(atom_state[:REACH], BOTH, [(i + 1, i) for i in range(ends)])
    narrow = jnp.concatenate(
        [atom_state]
        + [array.reshape(-1, width) for array in (atom_bias, atom_proj, atom_output)],
        axis=0,
    )
    inner = call(
        inner_step,
        tuple(shape((count, width), kind) for kind in (BF16, BF16, BF16, F32))
        + (shape((count - 2 * EDGE * WIN_Q, width), BF16),),
        ATOM_MB,
        (200_000_000, 1_000_000),
    )(narrow)
    mid, single, norm = call(
        atom_step,
        (
            shape((count, width), F32),
            shape((tokens, depth), F32),
            shape((tokens, depth), BF16),
        ),
        ATOM_MB,
        (200_000_000, 2_000_000),
    )(left, right, narrow, pool_weight, token_input, atom_owner, *inner)
    ring = cols // 2
    turn = []
    for r in range(rows):
        for c in range(cols):
            to_row = (c // ring) * cols + 2 * ((c % ring + 2) % ring) + r % 2
            turn.append((r * cols + c, to_row * cols + r // 2))
    turned = lax.ppermute(norm, BOTH, turn)
    across = lax.ppermute(norm, "col", [(i, (i + ring) % cols) for i in range(cols)])
    own = jnp.concatenate([norm, across], axis=0)
    turned, own = lax.optimization_barrier((turned, own))
    same_core = [[i for i in range(rows) if i % 2 == e] for e in range(2)]
    near = lax.all_to_all(
        jnp.broadcast_to(turned[None], (rows // 2, tokens, depth)), "row", 0, 0,
        axis_index_groups=same_core,
    )
    along = [
        lax.ppermute(
            own, "col", [(i, i // ring * ring + (i + step) % ring) for i in range(cols)]
        )
        for step in (1, ring - 1, 2)
    ]
    near, *along = lax.optimization_barrier((near, *along))
    far = lax.ppermute(near, "row", [(i, i ^ 1) for i in range(rows)])
    q_count, half = cols * tokens, rows * tokens // 2
    lane = 2 * SLOT
    in_vmem, in_hbm = (pl.BlockSpec(memory_space=space) for space in (pltpu.VMEM, pltpu.HBM))
    queries, gates, near_k, near_v, key_weights = call(
        project_step,
        (
            shape((PAIRS, q_count, lane), BF16),
            shape((tokens, wide), F32),
            shape((PAIRS, half, lane), BF16),
            shape((PAIRS, half, lane), BF16),
            shape((2, depth, depth), BF16),
        ),
        MOST,
        SMALL,
        in_specs=[in_vmem] * 6 + [in_hbm],
        scratch_shapes=[pltpu.VMEM((2, depth, depth), BF16), pltpu.SemaphoreType.DMA((4,))],
    )(own, *along, norm, near, token_proj)
    parts = call(
        token_step,
        shape((q_count, wide), BF16),
        MOST,
        (6_000_000_000, 14_000_000),
        in_specs=[in_vmem] * 5 + [in_hbm],
        scratch_shapes=[
            pltpu.VMEM((HEADS, q_count, 2 * half), BF16),
            pltpu.VMEM((PAIRS, half, lane), BF16),
            pltpu.VMEM((PAIRS, half, lane), BF16),
            pltpu.SemaphoreType.DMA((2,)),
        ],
    )(queries, near_k, near_v, far, key_weights, pair_bias)
    parts = lax.all_to_all(parts.reshape(cols, tokens, wide), "col", 0, 0)
    return call(
        last_step,
        (shape((count, width), BF16), shape((tokens, depth), BF16)),
        12,
        (400_000_000, 5_000_000),
    )(parts, gates, single, mid, atom_owner, token_output, back_weight)


def solution(mesh):
    split = P(BOTH, None)
    placed = (
        split, split, split, P(None, BOTH, None), P(None, "row", "col"),
        P(), P(), P(), P(), P(), P(),
    )
    return jax.shard_map(
        per_device, mesh=mesh, in_specs=placed, out_specs=(split, split), check_vma=False
    )
```

```python
import math

import jax
import jax.numpy as jnp
from jax import lax
from jax.experimental import pallas as pl
from jax.experimental.pallas import tpu as pltpu
from jax.sharding import PartitionSpec as P

HEADS = 16
HEAD_DIM = 48
SLOT = 64
PAIRS = HEADS // 2
ATOM_HEADS = 4
WIN_Q = 32
WIN_K = 128
REACH = 48
EDGE = 2
EPSILON = 1e-05

BOTH = ("row", "col")
F32 = jnp.float32
BF16 = jnp.bfloat16
ATOM_MB = 20
MOST = 47
SMALL = (1_000_000, 100_000)
ORDER = (2, 3, 0, 1, 6, 7, 4, 5)


def dot(a, b, contract=((1,), (0,))):
    return lax.dot_general(a, b, (contract, ((), ())), preferred_element_type=F32)


def layer_norm(values):
    centred = values - jnp.mean(values, axis=-1, keepdims=True)
    spread = jnp.mean(centred * centred, axis=-1, keepdims=True)
    return centred * lax.rsqrt(spread + EPSILON)


def lanes(shape, axis):
    return lax.broadcasted_iota(jnp.int32, shape, axis)


META = 8
BAND = 2 * 2 * SLOT
STARTS = (0, 128, 384, 512)


def band_place(group, back=False):
    far = lanes((BAND, 1) if back else (1, BAND), 0 if back else 1) + group * BAND
    within = far & (SLOT - 1)
    source = (far >> 6) * HEAD_DIM + within - STARTS[group]
    source = jnp.where(within < HEAD_DIM, source, -1)
    return (lanes((BAND, BAND), 1 if back else 0) == source).astype(BF16)


def meta_place(group):
    far = lanes((BAND, 1), 0) + group * BAND
    within = (far & (SLOT - 1)) - HEAD_DIM
    target = jnp.where((within >= 0) & (within < 5), (far >> 6) * META + within, -1)
    return (lanes((BAND, 2 * SLOT), 1) == target).astype(BF16)


def level_place(block, first, amount):
    here, there = lanes((2 * SLOT, 1), 0), lanes((1, BAND), 1) + block * BAND
    within = (here & (META - 1)) - first
    head = jnp.where((within >= 0) & (within < amount), here >> 3, -1)
    return (head == there // HEAD_DIM).astype(BF16)


def places(back=False):
    return [band_place(g, back) for g in range(HEADS // 4)]


def spread(values, into):
    return [
        dot(values[:, STARTS[g] : STARTS[g] + BAND], into[g]) for g in range(HEADS // 4)
    ]


def gather_lanes(values):
    parts = [dot(values[g], place) for g, place in enumerate(places(True))]
    lane = 2 * SLOT
    return jnp.concatenate(
        [
            parts[0][:, :lane],
            parts[0][:, lane:] + parts[1][:, :lane],
            parts[1][:, lane:],
            parts[2][:, :lane],
            parts[2][:, lane:] + parts[3][:, :lane],
            parts[3][:, lane:],
        ],
        axis=1,
    )


def store_pairs(ref, bands):
    lane = 2 * SLOT
    for g, band in enumerate(bands):
        ref[2 * g] = band[:, :lane].astype(BF16)
        ref[2 * g + 1] = band[:, lane:].astype(BF16)


def narrow_parts(narrow_ref, count):
    width = narrow_ref.shape[1]
    after = (1 + ATOM_HEADS) * count
    biases = [narrow_ref.at[(1 + h) * count : (2 + h) * count] for h in range(ATOM_HEADS)]
    weights = [narrow_ref.at[after + i * width : after + (i + 1) * width] for i in range(5)]
    return narrow_ref.at[:count], biases, weights


def window(start, query, keys, values, gates, biases, bounds=None):
    width = query.shape[1]
    head_width = width // ATOM_HEADS
    head_of = lanes((1, width), 1) >> 5
    masks = [(head_of == h).astype(F32) for h in range(ATOM_HEADS)]
    stacked = jnp.concatenate([query * mask.astype(BF16) for mask in masks], axis=0)
    scores = dot(stacked, keys, ((1,), (1,))) * (1.0 / math.sqrt(head_width))
    scores = scores + jnp.concatenate(
        [bias[start : start + WIN_Q, :] for bias in biases], axis=0
    ).astype(F32)
    if bounds is not None:
        first, total = bounds
        position = first + (start - REACH) + lanes(scores.shape, 1)
        scores = jnp.where((position >= 0) & (position < total), scores, -1e30)
    top = jnp.max(scores, axis=-1, keepdims=True)
    weights = jnp.exp(scores - top)
    weights = (weights / jnp.sum(weights, axis=-1, keepdims=True)).astype(BF16)
    mixed = dot(weights, values)
    mix = jnp.zeros((WIN_Q, width), F32)
    for h in range(ATOM_HEADS):
        mix = mix + mixed[h * WIN_Q : (h + 1) * WIN_Q] * masks[h]
    return (mix * gates).astype(BF16)


def inner_step(narrow_ref, q_ref, k_ref, v_ref, gate_ref, gated_ref):
    count = q_ref.shape[0]
    state_ref, biases, weights = narrow_parts(narrow_ref, count)
    normed = layer_norm(state_ref[...].astype(F32)).astype(BF16)
    queries = dot(normed, weights[0][...]).astype(BF16)
    keys = dot(normed, weights[1][...]).astype(BF16)
    values = dot(normed, weights[2][...]).astype(BF16)
    gates = jax.nn.sigmoid(dot(normed, weights[3][...]))
    q_ref[...], k_ref[...], v_ref[...], gate_ref[...] = queries, keys, values, gates
    for w in range(EDGE, count // WIN_Q - EDGE):
        start = w * WIN_Q
        seen = slice(start - REACH, start - REACH + WIN_K)
        mine = slice(start, start + WIN_Q)
        gated_ref[start - EDGE * WIN_Q : start - EDGE * WIN_Q + WIN_Q, :] = window(
            start, queries[mine], keys[seen], values[seen], gates[mine], biases
        )


def atom_step(
    left_ref, right_ref, narrow_ref, pool_ref, input_ref, owner_ref, q_ref, k_ref, v_ref,
    gate_ref, gated_ref, mid_ref, single_ref, norm_ref,
):
    count = owner_ref.shape[1]
    state_ref, biases, weights = narrow_parts(narrow_ref, count)
    rows, cols = lax.axis_size("row"), lax.axis_size("col")
    first = (lax.axis_index("row") * cols + lax.axis_index("col")) * count
    bounds = (first, count * rows * cols)
    beside = jnp.concatenate([left_ref[...], right_ref[...]], axis=0).astype(F32)
    normed = layer_norm(beside).astype(BF16)
    keys = dot(normed, weights[1][...]).astype(BF16)
    values = dot(normed, weights[2][...]).astype(BF16)
    reach = WIN_K + WIN_Q - REACH
    ends = (
        (jnp.concatenate([keys[:REACH], k_ref[:reach, :]], axis=0),
         jnp.concatenate([values[:REACH], v_ref[:reach, :]], axis=0)),
        (jnp.concatenate([k_ref[count - reach :, :], keys[REACH:]], axis=0),
         jnp.concatenate([v_ref[count - reach :, :], values[REACH:]], axis=0)),
    )
    outer = []
    for side in range(2):
        for w in range(EDGE):
            start = w * WIN_Q + side * (count - EDGE * WIN_Q)
            mine = slice(start, start + WIN_Q)
            seen = slice(w * WIN_Q, w * WIN_Q + WIN_K)
            outer.append(
                window(
                    start, q_ref[mine, :], ends[side][0][seen], ends[side][1][seen],
                    gate_ref[mine, :], biases, bounds,
                )
            )
    gated = jnp.concatenate(outer[:EDGE] + [gated_ref[...]] + outer[EDGE:], axis=0)
    mid = state_ref[...].astype(F32) + dot(gated, weights[4][...])
    mid_ref[...] = mid
    lifted = jnp.maximum(dot(mid.astype(BF16), pool_ref[...]), 0.0).astype(BF16)
    tokens = input_ref.shape[0]
    owned = (lanes((tokens, count), 0) == owner_ref[...]).astype(F32)
    counts = jnp.sum(owned, axis=1, keepdims=True)
    pooled = dot(owned.astype(BF16), lifted)
    single = input_ref[...].astype(F32) + pooled / counts
    single_ref[...] = single
    norm_ref[...] = layer_norm(single).astype(BF16)


def query_rows(parts, weight, into, q_ref):
    tokens = parts[0].shape[0] // 2
    lane = 2 * SLOT
    bands = spread(dot(jnp.concatenate(parts, axis=0), weight).astype(BF16), into)
    ring = lax.axis_size("col") // 2
    me = lax.axis_index("col")
    high, low = me // ring, me % ring
    for i, step in enumerate((0, ring - 1, 1, 2)):
        for j in range(2):
            source = lax.rem(high + j, 2) * ring + lax.rem(low + step, ring)
            at = pl.ds(pl.multiple_of(source * tokens, 16), tokens)
            first = (2 * i + j) * tokens
            for g, band in enumerate(bands):
                block = band[first : first + tokens].astype(BF16)
                q_ref[2 * g, at, :] = block[:, :lane]
                q_ref[2 * g + 1, at, :] = block[:, lane:]


def key_rows(blocks_ref, weight, into, k_ref):
    rows = jnp.concatenate([blocks_ref[i] for i in ORDER], axis=0)
    store_pairs(k_ref, spread(dot(rows, weight).astype(BF16), into))


def value_rows(blocks_ref, weight, into, v_ref):
    rows = jnp.concatenate([blocks_ref[i] for i in ORDER], axis=0)
    mass = (lanes((1, BAND), 1) & (SLOT - 1)) == HEAD_DIM
    bands = spread(dot(rows, weight).astype(BF16), into)
    store_pairs(v_ref, [jnp.where(mass, 1.0, band) for band in bands])


def project_step(
    own_ref, after_ref, before_ref, far_ref, norm_ref, blocks_ref, proj_hbm, q_ref, gate_ref,
    k_ref, v_ref, key_ref, edge_ref, sems,
):
    targets = (edge_ref.at[0], key_ref.at[0], key_ref.at[1], edge_ref.at[1])
    copies = [
        pltpu.make_async_copy(proj_hbm.at[i], target, sems.at[i])
        for i, target in enumerate(targets)
    ]
    for copy in copies:
        copy.start()
    into = places()
    copies[0].wait()
    query_rows(
        [own_ref[...], after_ref[...], before_ref[...], far_ref[...]], edge_ref[0], into, q_ref
    )
    copies[1].wait()
    key_rows(blocks_ref, key_ref[0], into, k_ref)
    copies[2].wait()
    value_rows(blocks_ref, key_ref[1], into, v_ref)
    copies[3].wait()
    gate_ref[...] = jax.nn.sigmoid(dot(norm_ref[...], edge_ref[1]))


def token_step(
    q_ref, k_ref, v_ref, blocks_ref, proj_ref, bias_hbm, part_ref, bias_ref, other_k, other_v, sems
):
    lane = 2 * SLOT
    heads = (slice(0, 4), slice(4, HEADS))
    copies = [
        pltpu.make_async_copy(bias_hbm.at[span], bias_ref.at[span], sems.at[i])
        for i, span in enumerate(heads)
    ]
    for copy in copies:
        copy.start()
    into = places()
    key_rows(blocks_ref, proj_ref[0], into, other_k)
    value_rows(blocks_ref, proj_ref[1], into, other_v)
    core = lax.rem(lax.axis_index("row"), 2)
    count, half = q_ref.shape[1], k_ref.shape[1]
    mine_at = pl.ds(pl.multiple_of(core * half, lane), half)
    other_at = pl.ds(pl.multiple_of((1 - core) * half, lane), half)
    at = lanes((count, lane), 1)
    first_head = at < SLOT
    spare = (at & (SLOT - 1)) - HEAD_DIM
    spares = [spare == i for i in range(5)]
    factor = 1.0 / math.sqrt(HEAD_DIM)
    results = []
    for pair in range(PAIRS):
        if pair == 0:
            copies[0].wait()
        if pair == 2:
            copies[1].wait()
        query = q_ref[pair]
        key = jnp.concatenate([k_ref[pair], other_k[pair]], axis=0)
        value = jnp.concatenate([v_ref[pair], other_v[pair]], axis=0)
        both = []
        for a in range(2):
            head = 2 * pair + a
            mine = jnp.where((at < SLOT) if a == 0 else (at >= SLOT), query, jnp.zeros_like(query))
            bias = jnp.concatenate(
                [bias_ref[head, :, mine_at], bias_ref[head, :, other_at]], axis=1
            )
            scores = dot(mine, key, ((1,), (1,))) * factor + bias.astype(F32)
            top = jnp.max(scores, axis=-1, keepdims=True)
            both.append((dot(jnp.exp(scores - top).astype(BF16), value), top))
        result = jnp.where(first_head, both[0][0], both[1][0])
        top = jnp.where(first_head, both[0][1], both[1][1])
        rest = result - result.astype(BF16).astype(F32)
        result = jnp.where(spares[1], pltpu.roll(rest, 1, 1), result)
        for piece in range(3):
            part = top.astype(BF16).astype(F32)
            result = jnp.where(spares[2 + piece], part, result)
            top = top - part
        results.append(result.astype(BF16))
    bands = [jnp.concatenate(results[i : i + 2], axis=1) for i in range(0, PAIRS, 2)]
    width = HEADS * HEAD_DIM
    part_ref[:, :width] = gather_lanes(bands).astype(BF16)
    part_ref[:, width:] = sum(dot(band, meta_place(g)) for g, band in enumerate(bands)).astype(BF16)


def last_step(
    part_ref, gate_ref, single_ref, mid_ref, owner_ref, output_ref, back_ref, atom_ref,
    token_ref,
):
    shares, tokens, _ = part_ref.shape
    width = HEADS * HEAD_DIM
    meta = jnp.concatenate([part_ref[c, :, width:] for c in range(shares)], axis=0)
    gated = []
    for block in range(width // BAND):
        span = slice(block * BAND, (block + 1) * BAND)
        tops = dot(meta, level_place(block, 2, 3)).reshape(shares, tokens, BAND)
        masses = dot(meta, level_place(block, 0, 2)).reshape(shares, tokens, BAND)
        weights = jnp.exp(tops - jnp.max(tops, axis=0))
        mix = sum(weights[c] * part_ref[c, :, span].astype(F32) for c in range(shares))
        mass = jnp.sum(weights * masses, axis=0)
        gated.append((mix / mass * gate_ref[:, span]).astype(BF16))
    update = dot(jnp.concatenate(gated, axis=1), output_ref[...])
    token_state = (single_ref[...] + update).astype(BF16)
    token_ref[...] = token_state
    returned = dot(token_state, back_ref[...])
    high = returned.astype(BF16)
    low = (returned - high.astype(F32)).astype(BF16)
    count = mid_ref.shape[0]
    owned = (lanes((tokens, count), 0) == owner_ref[...]).astype(F32).T.astype(BF16)
    atom_ref[...] = (mid_ref[...] + dot(owned, high) + dot(owned, low)).astype(BF16)


def call(kernel, out, megabytes, cost, **more):
    flops, size = cost
    return pl.pallas_call(
        kernel,
        out_shape=out,
        compiler_params=pltpu.CompilerParams(vmem_limit_bytes=megabytes * 1024 * 1024),
        cost_estimate=pl.CostEstimate(flops=flops, bytes_accessed=size, transcendentals=0),
        **more,
    )


def shape(dims, kind):
    return jax.ShapeDtypeStruct(dims, kind)


def per_device(
    atom_state, token_input, atom_owner, atom_bias, pair_bias, atom_proj, atom_output,
    pool_weight, token_proj, token_output, back_weight,
):
    rows, cols = lax.axis_size("row"), lax.axis_size("col")
    devices = rows * cols
    count, width = atom_state.shape
    tokens, depth = token_input.shape
    wide = depth + HEADS * META
    ends = devices - 1
    left = lax.ppermute(
        atom_state[count - REACH :], BOTH, [(i, i + 1) for i in range(ends)]
    )
    right = lax.ppermute(atom_state[:REACH], BOTH, [(i + 1, i) for i in range(ends)])
    narrow = jnp.concatenate(
        [atom_state]
        + [array.reshape(-1, width) for array in (atom_bias, atom_proj, atom_output)],
        axis=0,
    )
    inner = call(
        inner_step,
        tuple(shape((count, width), kind) for kind in (BF16, BF16, BF16, F32))
        + (shape((count - 2 * EDGE * WIN_Q, width), BF16),),
        ATOM_MB,
        (200_000_000, 1_000_000),
    )(narrow)
    mid, single, norm = call(
        atom_step,
        (
            shape((count, width), F32),
            shape((tokens, depth), F32),
            shape((tokens, depth), BF16),
        ),
        ATOM_MB,
        (200_000_000, 2_000_000),
    )(left, right, narrow, pool_weight, token_input, atom_owner, *inner)
    ring = cols // 2
    turn = []
    for r in range(rows):
        for c in range(cols):
            to_row = (c // ring) * cols + 2 * ((c % ring + 2) % ring) + r % 2
            turn.append((r * cols + c, to_row * cols + r // 2))
    turned = lax.ppermute(norm, BOTH, turn)
    across = lax.ppermute(norm, "col", [(i, (i + ring) % cols) for i in range(cols)])
    own = jnp.concatenate([norm, across], axis=0)
    turned, own = lax.optimization_barrier((turned, own))
    same_core = [[i for i in range(rows) if i % 2 == e] for e in range(2)]
    near = lax.all_to_all(
        jnp.broadcast_to(turned[None], (rows // 2, tokens, depth)), "row", 0, 0,
        axis_index_groups=same_core,
    )
    along = [
        lax.ppermute(
            own, "col", [(i, i // ring * ring + (i + step) % ring) for i in range(cols)]
        )
        for step in (1, ring - 1, 2)
    ]
    near, *along = lax.optimization_barrier((near, *along))
    far = lax.ppermute(near, "row", [(i, i ^ 1) for i in range(rows)])
    q_count, half = cols * tokens, rows * tokens // 2
    lane = 2 * SLOT
    in_vmem, in_hbm = (pl.BlockSpec(memory_space=space) for space in (pltpu.VMEM, pltpu.HBM))
    queries, gates, near_k, near_v, key_weights = call(
        project_step,
        (
            shape((PAIRS, q_count, lane), BF16),
            shape((tokens, depth), F32),
            shape((PAIRS, half, lane), BF16),
            shape((PAIRS, half, lane), BF16),
            shape((2, depth, depth), BF16),
        ),
        MOST,
        SMALL,
        in_specs=[in_vmem] * 6 + [in_hbm],
        scratch_shapes=[pltpu.VMEM((2, depth, depth), BF16), pltpu.SemaphoreType.DMA((4,))],
    )(own, *along, norm, near, token_proj)
    parts = call(
        token_step,
        shape((q_count, wide), BF16),
        MOST,
        (6_000_000_000, 14_000_000),
        in_specs=[in_vmem] * 5 + [in_hbm],
        scratch_shapes=[
            pltpu.VMEM((HEADS, q_count, 2 * half), BF16),
            pltpu.VMEM((PAIRS, half, lane), BF16),
            pltpu.VMEM((PAIRS, half, lane), BF16),
            pltpu.SemaphoreType.DMA((2,)),
        ],
    )(queries, near_k, near_v, far, key_weights, pair_bias)
    parts = lax.all_to_all(parts.reshape(cols, tokens, wide), "col", 0, 0)
    return call(
        last_step,
        (shape((count, width), BF16), shape((tokens, depth), BF16)),
        12,
        (400_000_000, 5_000_000),
    )(parts, gates, single, mid, atom_owner, token_output, back_weight)


def solution(mesh):
    split = P(BOTH, None)
    placed = (
        split, split, split, P(None, BOTH, None), P(None, "row", "col"),
        P(), P(), P(), P(), P(), P(),
    )
    return jax.shard_map(
        per_device, mesh=mesh, in_specs=placed, out_specs=(split, split), check_vma=False
    )
```

```python
import math

import jax
import jax.numpy as jnp
from jax import lax
from jax.experimental import pallas as pl
from jax.experimental.pallas import tpu as pltpu
from jax.sharding import PartitionSpec as P

HEADS = 16
HEAD_DIM = 48
SLOT = 64
PAIRS = HEADS // 2
ATOM_HEADS = 4
WIN_Q = 32
WIN_K = 128
REACH = 48
EDGE = 2
EPSILON = 1e-05

BOTH = ("row", "col")
F32 = jnp.float32
BF16 = jnp.bfloat16
ATOM_MB = 20
MOST = 47
SMALL = (1_000_000, 100_000)
ORDER = (2, 3, 0, 1, 6, 7, 4, 5)


def dot(a, b, contract=((1,), (0,))):
    return lax.dot_general(a, b, (contract, ((), ())), preferred_element_type=F32)


def layer_norm(values):
    centred = values - jnp.mean(values, axis=-1, keepdims=True)
    spread = jnp.mean(centred * centred, axis=-1, keepdims=True)
    return centred * lax.rsqrt(spread + EPSILON)


def lanes(shape, axis):
    return lax.broadcasted_iota(jnp.int32, shape, axis)


META = 8
BAND = 2 * 2 * SLOT
STARTS = (0, 128, 384, 512)


def band_place(group, back=False):
    far = lanes((BAND, 1) if back else (1, BAND), 0 if back else 1) + group * BAND
    within = far & (SLOT - 1)
    source = (far >> 6) * HEAD_DIM + within - STARTS[group]
    source = jnp.where(within < HEAD_DIM, source, -1)
    return (lanes((BAND, BAND), 1 if back else 0) == source).astype(BF16)


def meta_place(group):
    far = lanes((BAND, 1), 0) + group * BAND
    within = (far & (SLOT - 1)) - HEAD_DIM
    target = jnp.where((within >= 0) & (within < 5), (far >> 6) * META + within, -1)
    return (lanes((BAND, 2 * SLOT), 1) == target).astype(BF16)


def level_place(block, first, amount):
    here, there = lanes((2 * SLOT, 1), 0), lanes((1, BAND), 1) + block * BAND
    within = (here & (META - 1)) - first
    head = jnp.where((within >= 0) & (within < amount), here >> 3, -1)
    return (head == there // HEAD_DIM).astype(BF16)


def places(back=False):
    return [band_place(g, back) for g in range(HEADS // 4)]


def spread(values, into):
    return [
        dot(values[:, STARTS[g] : STARTS[g] + BAND], into[g]) for g in range(HEADS // 4)
    ]


def gather_lanes(values):
    parts = [dot(values[g], place) for g, place in enumerate(places(True))]
    lane = 2 * SLOT
    return jnp.concatenate(
        [
            parts[0][:, :lane],
            parts[0][:, lane:] + parts[1][:, :lane],
            parts[1][:, lane:],
            parts[2][:, :lane],
            parts[2][:, lane:] + parts[3][:, :lane],
            parts[3][:, lane:],
        ],
        axis=1,
    )


def store_pairs(ref, bands):
    lane = 2 * SLOT
    for g, band in enumerate(bands):
        ref[2 * g] = band[:, :lane].astype(BF16)
        ref[2 * g + 1] = band[:, lane:].astype(BF16)


def narrow_parts(narrow_ref, count):
    width = narrow_ref.shape[1]
    after = (1 + ATOM_HEADS) * count
    biases = [narrow_ref.at[(1 + h) * count : (2 + h) * count] for h in range(ATOM_HEADS)]
    weights = [narrow_ref.at[after + i * width : after + (i + 1) * width] for i in range(5)]
    return narrow_ref.at[:count], biases, weights


def window(start, query, keys, values, gates, biases, bounds=None):
    width = query.shape[1]
    head_width = width // ATOM_HEADS
    head_of = lanes((1, width), 1) >> 5
    masks = [(head_of == h).astype(F32) for h in range(ATOM_HEADS)]
    stacked = jnp.concatenate([query * mask.astype(BF16) for mask in masks], axis=0)
    scores = dot(stacked, keys, ((1,), (1,))) * (1.0 / math.sqrt(head_width))
    scores = scores + jnp.concatenate(
        [bias[start : start + WIN_Q, :] for bias in biases], axis=0
    ).astype(F32)
    if bounds is not None:
        first, total = bounds
        position = first + (start - REACH) + lanes(scores.shape, 1)
        scores = jnp.where((position >= 0) & (position < total), scores, -1e30)
    top = jnp.max(scores, axis=-1, keepdims=True)
    weights = jnp.exp(scores - top)
    weights = (weights / jnp.sum(weights, axis=-1, keepdims=True)).astype(BF16)
    mixed = dot(weights, values)
    mix = jnp.zeros((WIN_Q, width), F32)
    for h in range(ATOM_HEADS):
        mix = mix + mixed[h * WIN_Q : (h + 1) * WIN_Q] * masks[h]
    return (mix * gates).astype(BF16)


def inner_step(narrow_ref, q_ref, k_ref, v_ref, gate_ref, gated_ref):
    count = q_ref.shape[0]
    state_ref, biases, weights = narrow_parts(narrow_ref, count)
    normed = layer_norm(state_ref[...].astype(F32)).astype(BF16)
    queries = dot(normed, weights[0][...]).astype(BF16)
    keys = dot(normed, weights[1][...]).astype(BF16)
    values = dot(normed, weights[2][...]).astype(BF16)
    gates = jax.nn.sigmoid(dot(normed, weights[3][...]))
    q_ref[...], k_ref[...], v_ref[...], gate_ref[...] = queries, keys, values, gates
    for w in range(EDGE, count // WIN_Q - EDGE):
        start = w * WIN_Q
        seen = slice(start - REACH, start - REACH + WIN_K)
        mine = slice(start, start + WIN_Q)
        gated_ref[start - EDGE * WIN_Q : start - EDGE * WIN_Q + WIN_Q, :] = window(
            start, queries[mine], keys[seen], values[seen], gates[mine], biases
        )


def atom_step(
    left_ref, right_ref, narrow_ref, pool_ref, input_ref, owner_ref, q_ref, k_ref, v_ref,
    gate_ref, gated_ref, mid_ref, single_ref, norm_ref,
):
    count = owner_ref.shape[1]
    state_ref, biases, weights = narrow_parts(narrow_ref, count)
    rows, cols = lax.axis_size("row"), lax.axis_size("col")
    first = (lax.axis_index("row") * cols + lax.axis_index("col")) * count
    bounds = (first, count * rows * cols)
    beside = jnp.concatenate([left_ref[...], right_ref[...]], axis=0).astype(F32)
    normed = layer_norm(beside).astype(BF16)
    keys = dot(normed, weights[1][...]).astype(BF16)
    values = dot(normed, weights[2][...]).astype(BF16)
    reach = WIN_K + WIN_Q - REACH
    ends = (
        (jnp.concatenate([keys[:REACH], k_ref[:reach, :]], axis=0),
         jnp.concatenate([values[:REACH], v_ref[:reach, :]], axis=0)),
        (jnp.concatenate([k_ref[count - reach :, :], keys[REACH:]], axis=0),
         jnp.concatenate([v_ref[count - reach :, :], values[REACH:]], axis=0)),
    )
    outer = []
    for side in range(2):
        for w in range(EDGE):
            start = w * WIN_Q + side * (count - EDGE * WIN_Q)
            mine = slice(start, start + WIN_Q)
            seen = slice(w * WIN_Q, w * WIN_Q + WIN_K)
            outer.append(
                window(
                    start, q_ref[mine, :], ends[side][0][seen], ends[side][1][seen],
                    gate_ref[mine, :], biases, bounds,
                )
            )
    gated = jnp.concatenate(outer[:EDGE] + [gated_ref[...]] + outer[EDGE:], axis=0)
    mid = state_ref[...].astype(F32) + dot(gated, weights[4][...])
    mid_ref[...] = mid
    lifted = jnp.maximum(dot(mid.astype(BF16), pool_ref[...]), 0.0).astype(BF16)
    tokens = input_ref.shape[0]
    owned = (lanes((tokens, count), 0) == owner_ref[...]).astype(F32)
    counts = jnp.sum(owned, axis=1, keepdims=True)
    pooled = dot(owned.astype(BF16), lifted)
    single = input_ref[...].astype(F32) + pooled / counts
    single_ref[...] = single
    norm_ref[...] = layer_norm(single).astype(BF16)


def query_rows(parts, weight, into, q_ref):
    tokens = parts[0].shape[0] // 2
    lane = 2 * SLOT
    bands = spread(dot(jnp.concatenate(parts, axis=0), weight).astype(BF16), into)
    ring = lax.axis_size("col") // 2
    me = lax.axis_index("col")
    high, low = me // ring, me % ring
    for i, step in enumerate((0, ring - 1, 1, 2)):
        for j in range(2):
            source = lax.rem(high + j, 2) * ring + lax.rem(low + step, ring)
            at = pl.ds(pl.multiple_of(source * tokens, 16), tokens)
            first = (2 * i + j) * tokens
            for g, band in enumerate(bands):
                block = band[first : first + tokens].astype(BF16)
                q_ref[2 * g, at, :] = block[:, :lane]
                q_ref[2 * g + 1, at, :] = block[:, lane:]


def key_rows(blocks_ref, weight, into, k_ref):
    rows = jnp.concatenate([blocks_ref[i] for i in ORDER], axis=0)
    store_pairs(k_ref, spread(dot(rows, weight).astype(BF16), into))


def value_rows(blocks_ref, weight, into, v_ref):
    rows = jnp.concatenate([blocks_ref[i] for i in ORDER], axis=0)
    mass = (lanes((1, BAND), 1) & (SLOT - 1)) == HEAD_DIM
    bands = spread(dot(rows, weight).astype(BF16), into)
    store_pairs(v_ref, [jnp.where(mass, 1.0, band) for band in bands])


def near_step(blocks_ref, proj_hbm, k_ref, v_ref, key_ref, sems):
    copies = [
        pltpu.make_async_copy(proj_hbm.at[1 + i], key_ref.at[i], sems.at[i]) for i in range(2)
    ]
    for copy in copies:
        copy.start()
    into = places()
    copies[0].wait()
    key_rows(blocks_ref, key_ref[0], into, k_ref)
    copies[1].wait()
    value_rows(blocks_ref, key_ref[1], into, v_ref)


def query_step(
    own_ref, after_ref, before_ref, far_ref, norm_ref, proj_hbm, q_ref, gate_ref, edge_ref, sems
):
    copies = [
        pltpu.make_async_copy(proj_hbm.at[3 * i], edge_ref.at[i], sems.at[i]) for i in range(2)
    ]
    for copy in copies:
        copy.start()
    into = places()
    copies[0].wait()
    query_rows(
        [own_ref[...], after_ref[...], before_ref[...], far_ref[...]], edge_ref[0], into, q_ref
    )
    copies[1].wait()
    gate_ref[...] = jax.nn.sigmoid(dot(norm_ref[...], edge_ref[1]))


def token_step(
    q_ref, k_ref, v_ref, blocks_ref, proj_ref, bias_hbm, part_ref, bias_ref, other_k, other_v, sems
):
    lane = 2 * SLOT
    heads = (slice(0, 4), slice(4, HEADS))
    copies = [
        pltpu.make_async_copy(bias_hbm.at[span], bias_ref.at[span], sems.at[i])
        for i, span in enumerate(heads)
    ]
    for copy in copies:
        copy.start()
    into = places()
    key_rows(blocks_ref, proj_ref[0], into, other_k)
    value_rows(blocks_ref, proj_ref[1], into, other_v)
    core = lax.rem(lax.axis_index("row"), 2)
    count, half = q_ref.shape[1], k_ref.shape[1]
    mine_at = pl.ds(pl.multiple_of(core * half, lane), half)
    other_at = pl.ds(pl.multiple_of((1 - core) * half, lane), half)
    at = lanes((count, lane), 1)
    first_head = at < SLOT
    spare = (at & (SLOT - 1)) - HEAD_DIM
    spares = [spare == i for i in range(5)]
    factor = 1.0 / math.sqrt(HEAD_DIM)
    results = []
    for pair in range(PAIRS):
        if pair == 0:
            copies[0].wait()
        if pair == 2:
            copies[1].wait()
        query = q_ref[pair]
        key = jnp.concatenate([k_ref[pair], other_k[pair]], axis=0)
        value = jnp.concatenate([v_ref[pair], other_v[pair]], axis=0)
        both = []
        for a in range(2):
            head = 2 * pair + a
            mine = jnp.where((at < SLOT) if a == 0 else (at >= SLOT), query, jnp.zeros_like(query))
            bias = jnp.concatenate(
                [bias_ref[head, :, mine_at], bias_ref[head, :, other_at]], axis=1
            )
            scores = dot(mine, key, ((1,), (1,))) * factor + bias.astype(F32)
            top = jnp.max(scores, axis=-1, keepdims=True)
            both.append((dot(jnp.exp(scores - top).astype(BF16), value), top))
        result = jnp.where(first_head, both[0][0], both[1][0])
        top = jnp.where(first_head, both[0][1], both[1][1])
        rest = result - result.astype(BF16).astype(F32)
        result = jnp.where(spares[1], pltpu.roll(rest, 1, 1), result)
        for piece in range(3):
            part = top.astype(BF16).astype(F32)
            result = jnp.where(spares[2 + piece], part, result)
            top = top - part
        results.append(result.astype(BF16))
    bands = [jnp.concatenate(results[i : i + 2], axis=1) for i in range(0, PAIRS, 2)]
    width = HEADS * HEAD_DIM
    part_ref[:, :width] = gather_lanes(bands).astype(BF16)
    part_ref[:, width:] = sum(dot(band, meta_place(g)) for g, band in enumerate(bands)).astype(BF16)


def last_step(
    part_ref, gate_ref, single_ref, mid_ref, owner_ref, output_ref, back_ref, atom_ref,
    token_ref,
):
    shares, tokens, _ = part_ref.shape
    width = HEADS * HEAD_DIM
    meta = jnp.concatenate([part_ref[c, :, width:] for c in range(shares)], axis=0)
    gated = []
    for block in range(width // BAND):
        span = slice(block * BAND, (block + 1) * BAND)
        tops = dot(meta, level_place(block, 2, 3)).reshape(shares, tokens, BAND)
        masses = dot(meta, level_place(block, 0, 2)).reshape(shares, tokens, BAND)
        weights = jnp.exp(tops - jnp.max(tops, axis=0))
        mix = sum(weights[c] * part_ref[c, :, span].astype(F32) for c in range(shares))
        mass = jnp.sum(weights * masses, axis=0)
        gated.append((mix / mass * gate_ref[:, span]).astype(BF16))
    update = dot(jnp.concatenate(gated, axis=1), output_ref[...])
    token_state = (single_ref[...] + update).astype(BF16)
    token_ref[...] = token_state
    returned = dot(token_state, back_ref[...])
    high = returned.astype(BF16)
    low = (returned - high.astype(F32)).astype(BF16)
    count = mid_ref.shape[0]
    owned = (lanes((tokens, count), 0) == owner_ref[...]).astype(F32).T.astype(BF16)
    atom_ref[...] = (mid_ref[...] + dot(owned, high) + dot(owned, low)).astype(BF16)


def call(kernel, out, megabytes, cost, **more):
    flops, size = cost
    return pl.pallas_call(
        kernel,
        out_shape=out,
        compiler_params=pltpu.CompilerParams(vmem_limit_bytes=megabytes * 1024 * 1024),
        cost_estimate=pl.CostEstimate(flops=flops, bytes_accessed=size, transcendentals=0),
        **more,
    )


def shape(dims, kind):
    return jax.ShapeDtypeStruct(dims, kind)


def per_device(
    atom_state, token_input, atom_owner, atom_bias, pair_bias, atom_proj, atom_output,
    pool_weight, token_proj, token_output, back_weight,
):
    rows, cols = lax.axis_size("row"), lax.axis_size("col")
    devices = rows * cols
    count, width = atom_state.shape
    tokens, depth = token_input.shape
    wide = depth + HEADS * META
    ends = devices - 1
    left = lax.ppermute(
        atom_state[count - REACH :], BOTH, [(i, i + 1) for i in range(ends)]
    )
    right = lax.ppermute(atom_state[:REACH], BOTH, [(i + 1, i) for i in range(ends)])
    narrow = jnp.concatenate(
        [atom_state]
        + [array.reshape(-1, width) for array in (atom_bias, atom_proj, atom_output)],
        axis=0,
    )
    inner = call(
        inner_step,
        tuple(shape((count, width), kind) for kind in (BF16, BF16, BF16, F32))
        + (shape((count - 2 * EDGE * WIN_Q, width), BF16),),
        ATOM_MB,
        (200_000_000, 1_000_000),
    )(narrow)
    mid, single, norm = call(
        atom_step,
        (
            shape((count, width), F32),
            shape((tokens, depth), F32),
            shape((tokens, depth), BF16),
        ),
        ATOM_MB,
        (200_000_000, 2_000_000),
    )(left, right, narrow, pool_weight, token_input, atom_owner, *inner)
    ring = cols // 2
    turn = []
    for r in range(rows):
        for c in range(cols):
            to_row = (c // ring) * cols + 2 * ((c % ring + 2) % ring) + r % 2
            turn.append((r * cols + c, to_row * cols + r // 2))
    turned = lax.ppermute(norm, BOTH, turn)
    across = lax.ppermute(norm, "col", [(i, (i + ring) % cols) for i in range(cols)])
    own = jnp.concatenate([norm, across], axis=0)
    turned, own = lax.optimization_barrier((turned, own))
    same_core = [[i for i in range(rows) if i % 2 == e] for e in range(2)]
    near = lax.all_to_all(
        jnp.broadcast_to(turned[None], (rows // 2, tokens, depth)), "row", 0, 0,
        axis_index_groups=same_core,
    )
    along = [
        lax.ppermute(
            own, "col", [(i, i // ring * ring + (i + step) % ring) for i in range(cols)]
        )
        for step in (1, ring - 1, 2)
    ]
    in_vmem, in_hbm = (pl.BlockSpec(memory_space=space) for space in (pltpu.VMEM, pltpu.HBM))
    q_count, half = cols * tokens, rows * tokens // 2
    lane = 2 * SLOT
    near_k, near_v, key_weights = call(
        near_step,
        (
            shape((PAIRS, half, lane), BF16),
            shape((PAIRS, half, lane), BF16),
            shape((2, depth, depth), BF16),
        ),
        MOST,
        SMALL,
        in_specs=[in_vmem, in_hbm],
        scratch_shapes=[pltpu.SemaphoreType.DMA((2,))],
    )(near, token_proj)
    near, near_k, near_v, *along = lax.optimization_barrier((near, near_k, near_v, *along))
    far = lax.ppermute(near, "row", [(i, i ^ 1) for i in range(rows)])
    queries, gates = call(
        query_step,
        (shape((PAIRS, q_count, lane), BF16), shape((tokens, depth), F32)),
        MOST,
        SMALL,
        in_specs=[in_vmem] * 5 + [in_hbm],
        scratch_shapes=[pltpu.VMEM((2, depth, depth), BF16), pltpu.SemaphoreType.DMA((2,))],
    )(own, *along, norm, token_proj)
    parts = call(
        token_step,
        shape((q_count, wide), BF16),
        MOST,
        (6_000_000_000, 14_000_000),
        in_specs=[in_vmem] * 5 + [in_hbm],
        scratch_shapes=[
            pltpu.VMEM((HEADS, q_count, 2 * half), BF16),
            pltpu.VMEM((PAIRS, half, lane), BF16),
            pltpu.VMEM((PAIRS, half, lane), BF16),
            pltpu.SemaphoreType.DMA((2,)),
        ],
    )(queries, near_k, near_v, far, key_weights, pair_bias)
    parts = lax.all_to_all(parts.reshape(cols, tokens, wide), "col", 0, 0)
    return call(
        last_step,
        (shape((count, width), BF16), shape((tokens, depth), BF16)),
        12,
        (400_000_000, 5_000_000),
    )(parts, gates, single, mid, atom_owner, token_output, back_weight)


def solution(mesh):
    split = P(BOTH, None)
    placed = (
        split, split, split, P(None, BOTH, None), P(None, "row", "col"),
        P(), P(), P(), P(), P(), P(),
    )
    return jax.shard_map(
        per_device, mesh=mesh, in_specs=placed, out_specs=(split, split), check_vma=False
    )
```

```python
import math

import jax
import jax.numpy as jnp
from jax import lax
from jax.experimental import pallas as pl
from jax.experimental.pallas import tpu as pltpu
from jax.sharding import PartitionSpec as P

HEADS = 16
HEAD_DIM = 48
SLOT = 64
PAIRS = HEADS // 2
ATOM_HEADS = 4
WIN_Q = 32
WIN_K = 128
REACH = 48
EDGE = 2
EPSILON = 1e-05

BOTH = ("row", "col")
F32 = jnp.float32
BF16 = jnp.bfloat16
ATOM_MB = 20
MOST = 47
SMALL = (1_000_000, 100_000)
ORDER = (2, 3, 0, 1, 6, 7, 4, 5)


def dot(a, b, contract=((1,), (0,))):
    return lax.dot_general(a, b, (contract, ((), ())), preferred_element_type=F32)


def layer_norm(values):
    centred = values - jnp.mean(values, axis=-1, keepdims=True)
    spread = jnp.mean(centred * centred, axis=-1, keepdims=True)
    return centred * lax.rsqrt(spread + EPSILON)


def lanes(shape, axis):
    return lax.broadcasted_iota(jnp.int32, shape, axis)


META = 8
BAND = 2 * 2 * SLOT
STARTS = (0, 128, 384, 512)


def band_place(group, back=False):
    far = lanes((BAND, 1) if back else (1, BAND), 0 if back else 1) + group * BAND
    within = far & (SLOT - 1)
    source = (far >> 6) * HEAD_DIM + within - STARTS[group]
    source = jnp.where(within < HEAD_DIM, source, -1)
    return (lanes((BAND, BAND), 1 if back else 0) == source).astype(BF16)


def meta_place(group):
    far = lanes((BAND, 1), 0) + group * BAND
    within = (far & (SLOT - 1)) - HEAD_DIM
    target = jnp.where((within >= 0) & (within < 5), (far >> 6) * META + within, -1)
    return (lanes((BAND, 2 * SLOT), 1) == target).astype(BF16)


def level_place(block, first, amount):
    here, there = lanes((2 * SLOT, 1), 0), lanes((1, BAND), 1) + block * BAND
    within = (here & (META - 1)) - first
    head = jnp.where((within >= 0) & (within < amount), here >> 3, -1)
    return (head == there // HEAD_DIM).astype(BF16)


def places(back=False):
    return [band_place(g, back) for g in range(HEADS // 4)]


def spread(values, into):
    return [
        dot(values[:, STARTS[g] : STARTS[g] + BAND], into[g]) for g in range(HEADS // 4)
    ]


def gather_lanes(values):
    parts = [dot(values[g], place) for g, place in enumerate(places(True))]
    lane = 2 * SLOT
    return jnp.concatenate(
        [
            parts[0][:, :lane],
            parts[0][:, lane:] + parts[1][:, :lane],
            parts[1][:, lane:],
            parts[2][:, :lane],
            parts[2][:, lane:] + parts[3][:, :lane],
            parts[3][:, lane:],
        ],
        axis=1,
    )


def store_pairs(ref, bands):
    lane = 2 * SLOT
    for g, band in enumerate(bands):
        ref[2 * g] = band[:, :lane].astype(BF16)
        ref[2 * g + 1] = band[:, lane:].astype(BF16)


def narrow_parts(narrow_ref, count):
    width = narrow_ref.shape[1]
    after = (1 + ATOM_HEADS) * count
    biases = [narrow_ref.at[(1 + h) * count : (2 + h) * count] for h in range(ATOM_HEADS)]
    weights = [narrow_ref.at[after + i * width : after + (i + 1) * width] for i in range(5)]
    return narrow_ref.at[:count], biases, weights


def window(start, query, keys, values, gates, biases, bounds=None):
    width = query.shape[1]
    head_width = width // ATOM_HEADS
    head_of = lanes((1, width), 1) >> 5
    masks = [(head_of == h).astype(F32) for h in range(ATOM_HEADS)]
    stacked = jnp.concatenate([query * mask.astype(BF16) for mask in masks], axis=0)
    scores = dot(stacked, keys, ((1,), (1,))) * (1.0 / math.sqrt(head_width))
    scores = scores + jnp.concatenate(
        [bias[start : start + WIN_Q, :] for bias in biases], axis=0
    ).astype(F32)
    if bounds is not None:
        first, total = bounds
        position = first + (start - REACH) + lanes(scores.shape, 1)
        scores = jnp.where((position >= 0) & (position < total), scores, -1e30)
    top = jnp.max(scores, axis=-1, keepdims=True)
    weights = jnp.exp(scores - top)
    weights = (weights / jnp.sum(weights, axis=-1, keepdims=True)).astype(BF16)
    mixed = dot(weights, values)
    mix = jnp.zeros((WIN_Q, width), F32)
    for h in range(ATOM_HEADS):
        mix = mix + mixed[h * WIN_Q : (h + 1) * WIN_Q] * masks[h]
    return (mix * gates).astype(BF16)


def inner_step(narrow_ref, q_ref, k_ref, v_ref, gate_ref, gated_ref):
    count = q_ref.shape[0]
    state_ref, biases, weights = narrow_parts(narrow_ref, count)
    normed = layer_norm(state_ref[...].astype(F32)).astype(BF16)
    queries = dot(normed, weights[0][...]).astype(BF16)
    keys = dot(normed, weights[1][...]).astype(BF16)
    values = dot(normed, weights[2][...]).astype(BF16)
    gates = jax.nn.sigmoid(dot(normed, weights[3][...]))
    q_ref[...], k_ref[...], v_ref[...], gate_ref[...] = queries, keys, values, gates
    for w in range(EDGE, count // WIN_Q - EDGE):
        start = w * WIN_Q
        seen = slice(start - REACH, start - REACH + WIN_K)
        mine = slice(start, start + WIN_Q)
        gated_ref[start - EDGE * WIN_Q : start - EDGE * WIN_Q + WIN_Q, :] = window(
            start, queries[mine], keys[seen], values[seen], gates[mine], biases
        )


def atom_step(
    right_ref, left_ref, narrow_ref, pool_ref, input_ref, owner_ref, q_ref, k_ref, v_ref,
    gate_ref, gated_ref, mid_ref, single_ref, norm_ref,
):
    count = owner_ref.shape[1]
    state_ref, biases, weights = narrow_parts(narrow_ref, count)
    rows, cols = lax.axis_size("row"), lax.axis_size("col")
    first = (lax.axis_index("row") * cols + lax.axis_index("col")) * count
    bounds = (first, count * rows * cols)
    beside = jnp.concatenate([left_ref[...], right_ref[...]], axis=0).astype(F32)
    normed = layer_norm(beside).astype(BF16)
    keys = dot(normed, weights[1][...]).astype(BF16)
    values = dot(normed, weights[2][...]).astype(BF16)
    reach = WIN_K + WIN_Q - REACH
    ends = (
        (jnp.concatenate([keys[:REACH], k_ref[:reach, :]], axis=0),
         jnp.concatenate([values[:REACH], v_ref[:reach, :]], axis=0)),
        (jnp.concatenate([k_ref[count - reach :, :], keys[REACH:]], axis=0),
         jnp.concatenate([v_ref[count - reach :, :], values[REACH:]], axis=0)),
    )
    outer = []
    for side in range(2):
        for w in range(EDGE):
            start = w * WIN_Q + side * (count - EDGE * WIN_Q)
            mine = slice(start, start + WIN_Q)
            seen = slice(w * WIN_Q, w * WIN_Q + WIN_K)
            outer.append(
                window(
                    start, q_ref[mine, :], ends[side][0][seen], ends[side][1][seen],
                    gate_ref[mine, :], biases, bounds,
                )
            )
    gated = jnp.concatenate(outer[:EDGE] + [gated_ref[...]] + outer[EDGE:], axis=0)
    mid = state_ref[...].astype(F32) + dot(gated, weights[4][...])
    mid_ref[...] = mid
    lifted = jnp.maximum(dot(mid.astype(BF16), pool_ref[...]), 0.0).astype(BF16)
    tokens = input_ref.shape[0]
    owned = (lanes((tokens, count), 0) == owner_ref[...]).astype(F32)
    counts = jnp.sum(owned, axis=1, keepdims=True)
    pooled = dot(owned.astype(BF16), lifted)
    single = input_ref[...].astype(F32) + pooled / counts
    single_ref[...] = single
    norm_ref[...] = layer_norm(single).astype(BF16)


def query_rows(parts, weight, into, q_ref):
    tokens = parts[0].shape[0] // 2
    lane = 2 * SLOT
    bands = spread(dot(jnp.concatenate(parts, axis=0), weight).astype(BF16), into)
    ring = lax.axis_size("col") // 2
    me = lax.axis_index("col")
    high, low = me // ring, me % ring
    for i, step in enumerate((0, ring - 1, 1, 2)):
        for j in range(2):
            source = lax.rem(high + j, 2) * ring + lax.rem(low + step, ring)
            at = pl.ds(pl.multiple_of(source * tokens, 16), tokens)
            first = (2 * i + j) * tokens
            for g, band in enumerate(bands):
                block = band[first : first + tokens].astype(BF16)
                q_ref[2 * g, at, :] = block[:, :lane]
                q_ref[2 * g + 1, at, :] = block[:, lane:]


def key_rows(blocks_ref, weight, into, k_ref):
    rows = jnp.concatenate([blocks_ref[i] for i in ORDER], axis=0)
    store_pairs(k_ref, spread(dot(rows, weight).astype(BF16), into))


def value_rows(blocks_ref, weight, into, v_ref):
    rows = jnp.concatenate([blocks_ref[i] for i in ORDER], axis=0)
    mass = (lanes((1, BAND), 1) & (SLOT - 1)) == HEAD_DIM
    bands = spread(dot(rows, weight).astype(BF16), into)
    store_pairs(v_ref, [jnp.where(mass, 1.0, band) for band in bands])


def near_step(blocks_ref, proj_hbm, k_ref, v_ref, key_ref, sems):
    copies = [
        pltpu.make_async_copy(proj_hbm.at[1 + i], key_ref.at[i], sems.at[i]) for i in range(2)
    ]
    for copy in copies:
        copy.start()
    into = places()
    copies[0].wait()
    key_rows(blocks_ref, key_ref[0], into, k_ref)
    copies[1].wait()
    value_rows(blocks_ref, key_ref[1], into, v_ref)


def query_step(
    own_ref, far_ref, before_ref, after_ref, norm_ref, proj_hbm, q_ref, gate_ref, edge_ref, sems
):
    copies = [
        pltpu.make_async_copy(proj_hbm.at[3 * i], edge_ref.at[i], sems.at[i]) for i in range(2)
    ]
    for copy in copies:
        copy.start()
    into = places()
    copies[0].wait()
    query_rows(
        [own_ref[...], after_ref[...], before_ref[...], far_ref[...]], edge_ref[0], into, q_ref
    )
    copies[1].wait()
    gate_ref[...] = jax.nn.sigmoid(dot(norm_ref[...], edge_ref[1]))


def token_step(
    q_ref, k_ref, v_ref, blocks_ref, proj_ref, bias_hbm, part_ref, bias_ref, other_k, other_v, sems
):
    lane = 2 * SLOT
    heads = (slice(0, 4), slice(4, HEADS))
    copies = [
        pltpu.make_async_copy(bias_hbm.at[span], bias_ref.at[span], sems.at[i])
        for i, span in enumerate(heads)
    ]
    for copy in copies:
        copy.start()
    into = places()
    key_rows(blocks_ref, proj_ref[0], into, other_k)
    value_rows(blocks_ref, proj_ref[1], into, other_v)
    core = lax.rem(lax.axis_index("row"), 2)
    count, half = q_ref.shape[1], k_ref.shape[1]
    mine_at = pl.ds(pl.multiple_of(core * half, lane), half)
    other_at = pl.ds(pl.multiple_of((1 - core) * half, lane), half)
    at = lanes((count, lane), 1)
    first_head = at < SLOT
    spare = (at & (SLOT - 1)) - HEAD_DIM
    spares = [spare == i for i in range(5)]
    factor = 1.0 / math.sqrt(HEAD_DIM)
    results = []
    for pair in range(PAIRS):
        if pair == 0:
            copies[0].wait()
        if pair == 2:
            copies[1].wait()
        query = q_ref[pair]
        key = jnp.concatenate([k_ref[pair], other_k[pair]], axis=0)
        value = jnp.concatenate([v_ref[pair], other_v[pair]], axis=0)
        both = []
        for a in range(2):
            head = 2 * pair + a
            mine = jnp.where((at < SLOT) if a == 0 else (at >= SLOT), query, jnp.zeros_like(query))
            bias = jnp.concatenate(
                [bias_ref[head, :, mine_at], bias_ref[head, :, other_at]], axis=1
            )
            scores = dot(mine, key, ((1,), (1,))) * factor + bias.astype(F32)
            top = jnp.max(scores, axis=-1, keepdims=True)
            both.append((dot(jnp.exp(scores - top).astype(BF16), value), top))
        result = jnp.where(first_head, both[0][0], both[1][0])
        top = jnp.where(first_head, both[0][1], both[1][1])
        rest = result - result.astype(BF16).astype(F32)
        result = jnp.where(spares[1], pltpu.roll(rest, 1, 1), result)
        for piece in range(3):
            part = top.astype(BF16).astype(F32)
            result = jnp.where(spares[2 + piece], part, result)
            top = top - part
        results.append(result.astype(BF16))
    bands = [jnp.concatenate(results[i : i + 2], axis=1) for i in range(0, PAIRS, 2)]
    width = HEADS * HEAD_DIM
    part_ref[:, :width] = gather_lanes(bands).astype(BF16)
    part_ref[:, width:] = sum(dot(band, meta_place(g)) for g, band in enumerate(bands)).astype(BF16)


def last_step(
    part_ref, gate_ref, single_ref, mid_ref, owner_ref, output_ref, back_ref, atom_ref,
    token_ref,
):
    shares, tokens, _ = part_ref.shape
    width = HEADS * HEAD_DIM
    meta = jnp.concatenate([part_ref[c, :, width:] for c in range(shares)], axis=0)
    gated = []
    for block in range(width // BAND):
        span = slice(block * BAND, (block + 1) * BAND)
        tops = dot(meta, level_place(block, 2, 3)).reshape(shares, tokens, BAND)
        masses = dot(meta, level_place(block, 0, 2)).reshape(shares, tokens, BAND)
        weights = jnp.exp(tops - jnp.max(tops, axis=0))
        mix = sum(weights[c] * part_ref[c, :, span].astype(F32) for c in range(shares))
        mass = jnp.sum(weights * masses, axis=0)
        gated.append((mix / mass * gate_ref[:, span]).astype(BF16))
    update = dot(jnp.concatenate(gated, axis=1), output_ref[...])
    token_state = (single_ref[...] + update).astype(BF16)
    token_ref[...] = token_state
    returned = dot(token_state, back_ref[...])
    high = returned.astype(BF16)
    low = (returned - high.astype(F32)).astype(BF16)
    count = mid_ref.shape[0]
    owned = (lanes((tokens, count), 0) == owner_ref[...]).astype(F32).T.astype(BF16)
    atom_ref[...] = (mid_ref[...] + dot(owned, high) + dot(owned, low)).astype(BF16)


def call(kernel, out, megabytes, cost, **more):
    flops, size = cost
    return pl.pallas_call(
        kernel,
        out_shape=out,
        compiler_params=pltpu.CompilerParams(vmem_limit_bytes=megabytes * 1024 * 1024),
        cost_estimate=pl.CostEstimate(flops=flops, bytes_accessed=size, transcendentals=0),
        **more,
    )


def shape(dims, kind):
    return jax.ShapeDtypeStruct(dims, kind)


def per_device(
    atom_state, token_input, atom_owner, atom_bias, pair_bias, atom_proj, atom_output,
    pool_weight, token_proj, token_output, back_weight,
):
    rows, cols = lax.axis_size("row"), lax.axis_size("col")
    devices = rows * cols
    count, width = atom_state.shape
    tokens, depth = token_input.shape
    wide = depth + HEADS * META
    ends = devices - 1
    left = lax.ppermute(
        atom_state[count - REACH :], BOTH, [(i, i + 1) for i in range(ends)]
    )
    right = lax.ppermute(atom_state[:REACH], BOTH, [(i + 1, i) for i in range(ends)])
    narrow = jnp.concatenate(
        [atom_state]
        + [array.reshape(-1, width) for array in (atom_bias, atom_proj, atom_output)],
        axis=0,
    )
    inner = call(
        inner_step,
        tuple(shape((count, width), kind) for kind in (BF16, BF16, BF16, F32))
        + (shape((count - 2 * EDGE * WIN_Q, width), BF16),),
        ATOM_MB,
        (200_000_000, 1_000_000),
    )(narrow)
    mid, single, norm = call(
        atom_step,
        (
            shape((count, width), F32),
            shape((tokens, depth), F32),
            shape((tokens, depth), BF16),
        ),
        ATOM_MB,
        (200_000_000, 2_000_000),
    )(right, left, narrow, pool_weight, token_input, atom_owner, *inner)
    ring = cols // 2
    turn = []
    for r in range(rows):
        for c in range(cols):
            to_row = (c // ring) * cols + 2 * ((c % ring + 2) % ring) + r % 2
            turn.append((r * cols + c, to_row * cols + r // 2))
    turned = lax.ppermute(norm, BOTH, turn)
    across = lax.ppermute(norm, "col", [(i, (i + ring) % cols) for i in range(cols)])
    own = jnp.concatenate([norm, across], axis=0)
    turned, own = lax.optimization_barrier((turned, own))
    same_core = [[i for i in range(rows) if i % 2 == e] for e in range(2)]
    near = lax.all_to_all(
        jnp.broadcast_to(turned[None], (rows // 2, tokens, depth)), "row", 0, 0,
        axis_index_groups=same_core,
    )
    along = [
        lax.ppermute(
            own, "col", [(i, i // ring * ring + (i + step) % ring) for i in range(cols)]
        )
        for step in (1, ring - 1, 2)
    ]
    in_vmem, in_hbm = (pl.BlockSpec(memory_space=space) for space in (pltpu.VMEM, pltpu.HBM))
    q_count, half = cols * tokens, rows * tokens // 2
    lane = 2 * SLOT
    near_k, near_v, key_weights = call(
        near_step,
        (
            shape((PAIRS, half, lane), BF16),
            shape((PAIRS, half, lane), BF16),
            shape((2, depth, depth), BF16),
        ),
        MOST,
        SMALL,
        in_specs=[in_vmem, in_hbm],
        scratch_shapes=[pltpu.SemaphoreType.DMA((2,))],
    )(near, token_proj)
    near, near_k, near_v, *along = lax.optimization_barrier((near, near_k, near_v, *along[::-1]))
    far = lax.ppermute(near, "row", [(i, i ^ 1) for i in range(rows)])
    queries, gates = call(
        query_step,
        (shape((PAIRS, q_count, lane), BF16), shape((tokens, depth), F32)),
        MOST,
        SMALL,
        in_specs=[in_vmem] * 5 + [in_hbm],
        scratch_shapes=[pltpu.VMEM((2, depth, depth), BF16), pltpu.SemaphoreType.DMA((2,))],
    )(own, *along, norm, token_proj)
    parts = call(
        token_step,
        shape((q_count, wide), BF16),
        MOST,
        (6_000_000_000, 14_000_000),
        in_specs=[in_vmem] * 5 + [in_hbm],
        scratch_shapes=[
            pltpu.VMEM((HEADS, q_count, 2 * half), BF16),
            pltpu.VMEM((PAIRS, half, lane), BF16),
            pltpu.VMEM((PAIRS, half, lane), BF16),
            pltpu.SemaphoreType.DMA((2,)),
        ],
    )(queries, near_k, near_v, far, key_weights, pair_bias)
    parts = lax.all_to_all(parts.reshape(cols, tokens, wide), "col", 0, 0)
    return call(
        last_step,
        (shape((count, width), BF16), shape((tokens, depth), BF16)),
        12,
        (400_000_000, 5_000_000),
    )(parts, gates, single, mid, atom_owner, token_output, back_weight)


def solution(mesh):
    split = P(BOTH, None)
    placed = (
        split, split, split, P(None, BOTH, None), P(None, "row", "col"),
        P(), P(), P(), P(), P(), P(),
    )
    return jax.shard_map(
        per_device, mesh=mesh, in_specs=placed, out_specs=(split, split), check_vma=False
    )
```

```python
import math

import jax
import jax.numpy as jnp
from jax import lax
from jax.experimental import pallas as pl
from jax.experimental.pallas import tpu as pltpu
from jax.sharding import PartitionSpec as P

HEADS = 16
HEAD_DIM = 48
SLOT = 64
PAIRS = HEADS // 2
ATOM_HEADS = 4
WIN_Q = 32
WIN_K = 128
REACH = 48
EDGE = 2
EPSILON = 1e-05

BOTH = ("row", "col")
F32 = jnp.float32
BF16 = jnp.bfloat16
ATOM_MB = 20
MOST = 47
SMALL = (1_000_000, 100_000)
ORDER = (2, 3, 0, 1, 6, 7, 4, 5)


def dot(a, b, contract=((1,), (0,))):
    return lax.dot_general(a, b, (contract, ((), ())), preferred_element_type=F32)


def layer_norm(values):
    centred = values - jnp.mean(values, axis=-1, keepdims=True)
    spread = jnp.mean(centred * centred, axis=-1, keepdims=True)
    return centred * lax.rsqrt(spread + EPSILON)


def lanes(shape, axis):
    return lax.broadcasted_iota(jnp.int32, shape, axis)


META = 8
BAND = 2 * 2 * SLOT
STARTS = (0, 128, 384, 512)


def band_place(group, back=False):
    far = lanes((BAND, 1) if back else (1, BAND), 0 if back else 1) + group * BAND
    within = far & (SLOT - 1)
    source = (far >> 6) * HEAD_DIM + within - STARTS[group]
    source = jnp.where(within < HEAD_DIM, source, -1)
    return (lanes((BAND, BAND), 1 if back else 0) == source).astype(BF16)


def meta_place(group):
    far = lanes((BAND, 1), 0) + group * BAND
    within = (far & (SLOT - 1)) - HEAD_DIM
    target = jnp.where((within >= 0) & (within < 5), (far >> 6) * META + within, -1)
    return (lanes((BAND, 2 * SLOT), 1) == target).astype(BF16)


def level_place(block, first, amount):
    here, there = lanes((2 * SLOT, 1), 0), lanes((1, BAND), 1) + block * BAND
    within = (here & (META - 1)) - first
    head = jnp.where((within >= 0) & (within < amount), here >> 3, -1)
    return (head == there // HEAD_DIM).astype(BF16)


def places(back=False):
    return [band_place(g, back) for g in range(HEADS // 4)]


def spread(values, into):
    return [
        dot(values[:, STARTS[g] : STARTS[g] + BAND], into[g]) for g in range(HEADS // 4)
    ]


def gather_lanes(values):
    parts = [dot(values[g], place) for g, place in enumerate(places(True))]
    lane = 2 * SLOT
    return jnp.concatenate(
        [
            parts[0][:, :lane],
            parts[0][:, lane:] + parts[1][:, :lane],
            parts[1][:, lane:],
            parts[2][:, :lane],
            parts[2][:, lane:] + parts[3][:, :lane],
            parts[3][:, lane:],
        ],
        axis=1,
    )


def store_pairs(ref, bands):
    lane = 2 * SLOT
    for g, band in enumerate(bands):
        ref[2 * g] = band[:, :lane].astype(BF16)
        ref[2 * g + 1] = band[:, lane:].astype(BF16)


def narrow_parts(narrow_ref, count):
    width = narrow_ref.shape[1]
    after = (1 + ATOM_HEADS) * count
    biases = [narrow_ref.at[(1 + h) * count : (2 + h) * count] for h in range(ATOM_HEADS)]
    weights = [narrow_ref.at[after + i * width : after + (i + 1) * width] for i in range(5)]
    return narrow_ref.at[:count], biases, weights


def window(start, query, keys, values, gates, biases, bounds=None):
    width = query.shape[1]
    head_width = width // ATOM_HEADS
    head_of = lanes((1, width), 1) >> 5
    masks = [(head_of == h).astype(F32) for h in range(ATOM_HEADS)]
    stacked = jnp.concatenate([query * mask.astype(BF16) for mask in masks], axis=0)
    scores = dot(stacked, keys, ((1,), (1,))) * (1.0 / math.sqrt(head_width))
    scores = scores + jnp.concatenate(
        [bias[start : start + WIN_Q, :] for bias in biases], axis=0
    ).astype(F32)
    if bounds is not None:
        first, total = bounds
        position = first + (start - REACH) + lanes(scores.shape, 1)
        scores = jnp.where((position >= 0) & (position < total), scores, -1e30)
    top = jnp.max(scores, axis=-1, keepdims=True)
    weights = jnp.exp(scores - top)
    weights = (weights / jnp.sum(weights, axis=-1, keepdims=True)).astype(BF16)
    mixed = dot(weights, values)
    mix = jnp.zeros((WIN_Q, width), F32)
    for h in range(ATOM_HEADS):
        mix = mix + mixed[h * WIN_Q : (h + 1) * WIN_Q] * masks[h]
    return (mix * gates).astype(BF16)


def inner_step(narrow_ref, q_ref, k_ref, v_ref, gate_ref, gated_ref):
    count = q_ref.shape[0]
    state_ref, biases, weights = narrow_parts(narrow_ref, count)
    normed = layer_norm(state_ref[...].astype(F32)).astype(BF16)
    queries = dot(normed, weights[0][...]).astype(BF16)
    keys = dot(normed, weights[1][...]).astype(BF16)
    values = dot(normed, weights[2][...]).astype(BF16)
    gates = jax.nn.sigmoid(dot(normed, weights[3][...]))
    q_ref[...], k_ref[...], v_ref[...], gate_ref[...] = queries, keys, values, gates
    for w in range(EDGE, count // WIN_Q - EDGE):
        start = w * WIN_Q
        seen = slice(start - REACH, start - REACH + WIN_K)
        mine = slice(start, start + WIN_Q)
        gated_ref[start - EDGE * WIN_Q : start - EDGE * WIN_Q + WIN_Q, :] = window(
            start, queries[mine], keys[seen], values[seen], gates[mine], biases
        )


def atom_step(
    right_ref, left_ref, narrow_ref, pool_ref, input_ref, owner_ref, q_ref, k_ref, v_ref,
    gate_ref, gated_ref, mid_ref, single_ref, norm_ref,
):
    count = owner_ref.shape[1]
    state_ref, biases, weights = narrow_parts(narrow_ref, count)
    rows, cols = lax.axis_size("row"), lax.axis_size("col")
    first = (lax.axis_index("row") * cols + lax.axis_index("col")) * count
    bounds = (first, count * rows * cols)
    beside = jnp.concatenate([left_ref[...], right_ref[...]], axis=0).astype(F32)
    normed = layer_norm(beside).astype(BF16)
    keys = dot(normed, weights[1][...]).astype(BF16)
    values = dot(normed, weights[2][...]).astype(BF16)
    reach = WIN_K + WIN_Q - REACH
    ends = (
        (jnp.concatenate([keys[:REACH], k_ref[:reach, :]], axis=0),
         jnp.concatenate([values[:REACH], v_ref[:reach, :]], axis=0)),
        (jnp.concatenate([k_ref[count - reach :, :], keys[REACH:]], axis=0),
         jnp.concatenate([v_ref[count - reach :, :], values[REACH:]], axis=0)),
    )
    outer = []
    for side in range(2):
        for w in range(EDGE):
            start = w * WIN_Q + side * (count - EDGE * WIN_Q)
            mine = slice(start, start + WIN_Q)
            seen = slice(w * WIN_Q, w * WIN_Q + WIN_K)
            outer.append(
                window(
                    start, q_ref[mine, :], ends[side][0][seen], ends[side][1][seen],
                    gate_ref[mine, :], biases, bounds,
                )
            )
    gated = jnp.concatenate(outer[:EDGE] + [gated_ref[...]] + outer[EDGE:], axis=0)
    mid = state_ref[...].astype(F32) + dot(gated, weights[4][...])
    mid_ref[...] = mid
    lifted = jnp.maximum(dot(mid.astype(BF16), pool_ref[...]), 0.0).astype(BF16)
    tokens = input_ref.shape[0]
    owned = (lanes((tokens, count), 0) == owner_ref[...]).astype(F32)
    counts = jnp.sum(owned, axis=1, keepdims=True)
    pooled = dot(owned.astype(BF16), lifted)
    single = input_ref[...].astype(F32) + pooled / counts
    single_ref[...] = single
    norm_ref[...] = layer_norm(single).astype(BF16)


def query_rows(parts, weight, into, q_ref):
    tokens = parts[0].shape[0] // 2
    lane = 2 * SLOT
    bands = spread(dot(jnp.concatenate(parts, axis=0), weight).astype(BF16), into)
    ring = lax.axis_size("col") // 2
    me = lax.axis_index("col")
    high, low = me // ring, me % ring
    for i, step in enumerate((0, ring - 1, 1, 2)):
        for j in range(2):
            source = lax.rem(high + j, 2) * ring + lax.rem(low + step, ring)
            at = pl.ds(pl.multiple_of(source * tokens, 16), tokens)
            first = (2 * i + j) * tokens
            for g, band in enumerate(bands):
                block = band[first : first + tokens].astype(BF16)
                q_ref[2 * g, at, :] = block[:, :lane]
                q_ref[2 * g + 1, at, :] = block[:, lane:]


def key_rows(blocks_ref, weight, into, k_ref):
    rows = jnp.concatenate([blocks_ref[i] for i in ORDER], axis=0)
    store_pairs(k_ref, spread(dot(rows, weight).astype(BF16), into))


def value_rows(blocks_ref, weight, into, v_ref):
    rows = jnp.concatenate([blocks_ref[i] for i in ORDER], axis=0)
    mass = (lanes((1, BAND), 1) & (SLOT - 1)) == HEAD_DIM
    bands = spread(dot(rows, weight).astype(BF16), into)
    store_pairs(v_ref, [jnp.where(mass, 1.0, band) for band in bands])


def near_step(blocks_ref, proj_hbm, k_ref, v_ref, key_ref, sems):
    copies = [
        pltpu.make_async_copy(proj_hbm.at[1 + i], key_ref.at[i], sems.at[i]) for i in range(2)
    ]
    copies[0].start()
    into = places()
    copies[0].wait()
    copies[1].start()
    key_rows(blocks_ref, key_ref[0], into, k_ref)
    copies[1].wait()
    value_rows(blocks_ref, key_ref[1], into, v_ref)


def query_step(
    own_ref, far_ref, before_ref, after_ref, norm_ref, proj_hbm, q_ref, gate_ref, edge_ref, sems
):
    copies = [
        pltpu.make_async_copy(proj_hbm.at[3 * i], edge_ref.at[i], sems.at[i]) for i in range(2)
    ]
    copies[0].start()
    into = places()
    copies[0].wait()
    copies[1].start()
    query_rows(
        [own_ref[...], after_ref[...], before_ref[...], far_ref[...]], edge_ref[0], into, q_ref
    )
    copies[1].wait()
    gate_ref[...] = jax.nn.sigmoid(dot(norm_ref[...], edge_ref[1]))


def token_step(
    q_ref, k_ref, v_ref, blocks_ref, proj_ref, bias_hbm, part_ref, bias_ref, other_k, other_v, sems
):
    lane = 2 * SLOT
    heads = (slice(0, 4), slice(4, HEADS))
    copies = [
        pltpu.make_async_copy(bias_hbm.at[span], bias_ref.at[span], sems.at[i])
        for i, span in enumerate(heads)
    ]
    for copy in copies:
        copy.start()
    into = places()
    key_rows(blocks_ref, proj_ref[0], into, other_k)
    value_rows(blocks_ref, proj_ref[1], into, other_v)
    core = lax.rem(lax.axis_index("row"), 2)
    count, half = q_ref.shape[1], k_ref.shape[1]
    mine_at = pl.ds(pl.multiple_of(core * half, lane), half)
    other_at = pl.ds(pl.multiple_of((1 - core) * half, lane), half)
    at = lanes((count, lane), 1)
    first_head = at < SLOT
    spare = (at & (SLOT - 1)) - HEAD_DIM
    spares = [spare == i for i in range(5)]
    factor = 1.0 / math.sqrt(HEAD_DIM)
    results = []
    for pair in range(PAIRS):
        if pair == 0:
            copies[0].wait()
        if pair == 2:
            copies[1].wait()
        query = q_ref[pair]
        key = jnp.concatenate([k_ref[pair], other_k[pair]], axis=0)
        value = jnp.concatenate([v_ref[pair], other_v[pair]], axis=0)
        both = []
        for a in range(2):
            head = 2 * pair + a
            mine = jnp.where((at < SLOT) if a == 0 else (at >= SLOT), query, jnp.zeros_like(query))
            bias = jnp.concatenate(
                [bias_ref[head, :, mine_at], bias_ref[head, :, other_at]], axis=1
            )
            scores = dot(mine, key, ((1,), (1,))) * factor + bias.astype(F32)
            top = jnp.max(scores, axis=-1, keepdims=True)
            both.append((dot(jnp.exp(scores - top).astype(BF16), value), top))
        result = jnp.where(first_head, both[0][0], both[1][0])
        top = jnp.where(first_head, both[0][1], both[1][1])
        rest = result - result.astype(BF16).astype(F32)
        result = jnp.where(spares[1], pltpu.roll(rest, 1, 1), result)
        for piece in range(3):
            part = top.astype(BF16).astype(F32)
            result = jnp.where(spares[2 + piece], part, result)
            top = top - part
        results.append(result.astype(BF16))
    bands = [jnp.concatenate(results[i : i + 2], axis=1) for i in range(0, PAIRS, 2)]
    width = HEADS * HEAD_DIM
    part_ref[:, :width] = gather_lanes(bands).astype(BF16)
    part_ref[:, width:] = sum(dot(band, meta_place(g)) for g, band in enumerate(bands)).astype(BF16)


def last_step(
    part_ref, gate_ref, single_ref, mid_ref, owner_ref, output_ref, back_ref, atom_ref,
    token_ref,
):
    shares, tokens, _ = part_ref.shape
    width = HEADS * HEAD_DIM
    meta = jnp.concatenate([part_ref[c, :, width:] for c in range(shares)], axis=0)
    gated = []
    for block in range(width // BAND):
        span = slice(block * BAND, (block + 1) * BAND)
        tops = dot(meta, level_place(block, 2, 3)).reshape(shares, tokens, BAND)
        masses = dot(meta, level_place(block, 0, 2)).reshape(shares, tokens, BAND)
        weights = jnp.exp(tops - jnp.max(tops, axis=0))
        mix = sum(weights[c] * part_ref[c, :, span].astype(F32) for c in range(shares))
        mass = jnp.sum(weights * masses, axis=0)
        gated.append((mix / mass * gate_ref[:, span]).astype(BF16))
    update = dot(jnp.concatenate(gated, axis=1), output_ref[...])
    token_state = (single_ref[...] + update).astype(BF16)
    token_ref[...] = token_state
    returned = dot(token_state, back_ref[...])
    high = returned.astype(BF16)
    low = (returned - high.astype(F32)).astype(BF16)
    count = mid_ref.shape[0]
    owned = (lanes((tokens, count), 0) == owner_ref[...]).astype(F32).T.astype(BF16)
    atom_ref[...] = (mid_ref[...] + dot(owned, high) + dot(owned, low)).astype(BF16)


def call(kernel, out, megabytes, cost, **more):
    flops, size = cost
    return pl.pallas_call(
        kernel,
        out_shape=out,
        compiler_params=pltpu.CompilerParams(vmem_limit_bytes=megabytes * 1024 * 1024),
        cost_estimate=pl.CostEstimate(flops=flops, bytes_accessed=size, transcendentals=0),
        **more,
    )


def shape(dims, kind):
    return jax.ShapeDtypeStruct(dims, kind)


def per_device(
    atom_state, token_input, atom_owner, atom_bias, pair_bias, atom_proj, atom_output,
    pool_weight, token_proj, token_output, back_weight,
):
    rows, cols = lax.axis_size("row"), lax.axis_size("col")
    devices = rows * cols
    count, width = atom_state.shape
    tokens, depth = token_input.shape
    wide = depth + HEADS * META
    ends = devices - 1
    left = lax.ppermute(
        atom_state[count - REACH :], BOTH, [(i, i + 1) for i in range(ends)]
    )
    right = lax.ppermute(atom_state[:REACH], BOTH, [(i + 1, i) for i in range(ends)])
    narrow = jnp.concatenate(
        [atom_state]
        + [array.reshape(-1, width) for array in (atom_bias, atom_proj, atom_output)],
        axis=0,
    )
    inner = call(
        inner_step,
        tuple(shape((count, width), kind) for kind in (BF16, BF16, BF16, F32))
        + (shape((count - 2 * EDGE * WIN_Q, width), BF16),),
        ATOM_MB,
        (200_000_000, 1_000_000),
    )(narrow)
    mid, single, norm = call(
        atom_step,
        (
            shape((count, width), F32),
            shape((tokens, depth), F32),
            shape((tokens, depth), BF16),
        ),
        ATOM_MB,
        (200_000_000, 2_000_000),
    )(right, left, narrow, pool_weight, token_input, atom_owner, *inner)
    ring = cols // 2
    turn = []
    for r in range(rows):
        for c in range(cols):
            to_row = (c // ring) * cols + 2 * ((c % ring + 2) % ring) + r % 2
            turn.append((r * cols + c, to_row * cols + r // 2))
    turned = lax.ppermute(norm, BOTH, turn)
    across = lax.ppermute(norm, "col", [(i, (i + ring) % cols) for i in range(cols)])
    own = jnp.concatenate([norm, across], axis=0)
    turned, own = lax.optimization_barrier((turned, own))
    same_core = [[i for i in range(rows) if i % 2 == e] for e in range(2)]
    near = lax.all_to_all(
        jnp.broadcast_to(turned[None], (rows // 2, tokens, depth)), "row", 0, 0,
        axis_index_groups=same_core,
    )
    along = [
        lax.ppermute(
            own, "col", [(i, i // ring * ring + (i + step) % ring) for i in range(cols)]
        )
        for step in (1, ring - 1, 2)
    ]
    in_vmem, in_hbm = (pl.BlockSpec(memory_space=space) for space in (pltpu.VMEM, pltpu.HBM))
    q_count, half = cols * tokens, rows * tokens // 2
    lane = 2 * SLOT
    near_k, near_v, key_weights = call(
        near_step,
        (
            shape((PAIRS, half, lane), BF16),
            shape((PAIRS, half, lane), BF16),
            shape((2, depth, depth), BF16),
        ),
        MOST,
        SMALL,
        in_specs=[in_vmem, in_hbm],
        scratch_shapes=[pltpu.SemaphoreType.DMA((2,))],
    )(near, token_proj)
    near, near_k, near_v, *along = lax.optimization_barrier((near, near_k, near_v, *along[::-1]))
    far = lax.ppermute(near, "row", [(i, i ^ 1) for i in range(rows)])
    queries, gates = call(
        query_step,
        (shape((PAIRS, q_count, lane), BF16), shape((tokens, depth), F32)),
        MOST,
        SMALL,
        in_specs=[in_vmem] * 5 + [in_hbm],
        scratch_shapes=[pltpu.VMEM((2, depth, depth), BF16), pltpu.SemaphoreType.DMA((2,))],
    )(own, *along, norm, token_proj)
    parts = call(
        token_step,
        shape((q_count, wide), BF16),
        MOST,
        (6_000_000_000, 14_000_000),
        in_specs=[in_vmem] * 5 + [in_hbm],
        scratch_shapes=[
            pltpu.VMEM((HEADS, q_count, 2 * half), BF16),
            pltpu.VMEM((PAIRS, half, lane), BF16),
            pltpu.VMEM((PAIRS, half, lane), BF16),
            pltpu.SemaphoreType.DMA((2,)),
        ],
    )(queries, near_k, near_v, far, key_weights, pair_bias)
    parts = lax.all_to_all(parts.reshape(cols, tokens, wide), "col", 0, 0)
    return call(
        last_step,
        (shape((count, width), BF16), shape((tokens, depth), BF16)),
        12,
        (400_000_000, 5_000_000),
    )(parts, gates, single, mid, atom_owner, token_output, back_weight)


def solution(mesh):
    split = P(BOTH, None)
    placed = (
        split, split, split, P(None, BOTH, None), P(None, "row", "col"),
        P(), P(), P(), P(), P(), P(),
    )
    return jax.shard_map(
        per_device, mesh=mesh, in_specs=placed, out_specs=(split, split), check_vma=False
    )
```
